32 devices in a mesh: batch: 16 (over z, x, core), tensor: 2 (over y).
Axes of the slice: x: 2, y: 2, z: 4, core: 2. Of those that a mesh axis runs over, the one named last changes fastest.
Arguments:
- inputs: bfloat16 [32, 1024, 1024], P(('batch', 'tensor')), may hold values from -6 to 6
- counts: int32 [16], P('batch'), may hold values from 1 to 2, as said below
- ln1_gain: bfloat16 [1024], replicated, may hold values from 0.099609375 to 1.8984375
- ln1_bias: bfloat16 [1024], replicated, may hold values from -1.1953125 to 1.1953125
- log_dt: float32 [1024], P('tensor'), may hold values from -6.9 to -2.3
- log_a: float32 [1024, 32], P('tensor'), may hold values from -1 to 1
- freq: float32 [1024, 32], P('tensor'), may hold values from 0 to 100
- c_real: float32 [1024, 32], P('tensor'), may hold values from -3 to 3
- c_imag: float32 [1024, 32], P('tensor'), may hold values from -3 to 3
- skip_gain: float32 [1024], P('tensor'), may hold values from -4 to 4
- w_value: bfloat16 [1024, 1024], P(None, 'tensor'), may hold values from -0.375 to 0.375
- w_gate: bfloat16 [1024, 1024], P(None, 'tensor'), may hold values from -0.1875 to 0.1875
- ln2_gain: bfloat16 [1024], replicated, may hold values from 0.099609375 to 1.8984375
- ln2_bias: bfloat16 [1024], replicated, may hold values from -1.1953125 to 1.1953125
- w_in: bfloat16 [1024, 4096], P(None, 'tensor'), may hold values from -0.1875 to 0.1875
- w_out: bfloat16 [4096, 1024], P('tensor'), may hold values from -0.125 to 0.125
- cotangent: bfloat16 [32, 1024, 1024], P(('batch', 'tensor')), may hold values from -6 to 6
Outputs:
- output: bfloat16 [32, 1024, 1024], P(('batch', 'tensor'))
- input_grad: bfloat16 [32, 1024, 1024], P(('batch', 'tensor'))
- ln1_gain_grad: float32 [1024], P('tensor')
- ln1_bias_grad: float32 [1024], P('tensor')
- log_dt_grad: float32 [1024], P('tensor')
- log_a_grad: float32 [1024, 32], P('tensor')
- freq_grad: float32 [1024, 32], P('tensor')
- c_real_grad: float32 [1024, 32], P('tensor')
- c_imag_grad: float32 [1024, 32], P('tensor')
- skip_grad: float32 [1024], P('tensor')
- w_value_grad: float32 [1024, 1024], P(None, 'tensor')
- w_gate_grad: float32 [1024, 1024], P(None, 'tensor')
- ln2_gain_grad: float32 [1024], P('tensor')
- ln2_bias_grad: float32 [1024], P('tensor')
- w_in_grad: float32 [1024, 4096], P(None, 'tensor')
- w_out_grad: float32 [4096, 1024], P('tensor')
The draws below stay inside these ranges and needn't reach their ends.
Inputs may be any that keep to these rules, and one draw needn't show every extreme that they name: Slot t of batch shard b (sequence b * 2 + t) is used when t < counts[b]; some shard uses all 2 slots and some only one.
All inputs are finite; a program needn't handle non-finite values.
Results may differ from the reference program's by a relative error of at most 0.013.
Values may be sent and summed in bfloat16 or wider, within the bound.
A program may use at most 256 MiB of HBM per device.

```python
import jax
import jax.numpy as jnp
from jax import lax

D = 1024
MODES = 32
FF = 4096
SEQ = 1024
GROUP = 2
SHARDS = 16
SEQS = 32


def draw_counts(key, part):
    key = jax.random.fold_in(key, 7)
    counts = jax.random.randint(jax.random.fold_in(key, 1), (SHARDS,), 1, GROUP + 1)
    full_at = jax.random.randint(jax.random.fold_in(key, 2), (), 0, SHARDS)
    single_at = (full_at + jax.random.randint(jax.random.fold_in(key, 3), (), 1, SHARDS)) % SHARDS
    counts = counts.at[full_at].set(GROUP).at[single_at].set(1)
    return counts.astype(jnp.int32)


def steps_of(rng, dims, split, least, high):
    gain = 1.0
    for position, blocks in split:
        steps = jax.random.uniform(jax.random.fold_in(jax.random.fold_in(rng, 6), position), (blocks,), jnp.float32, least / len(split), high / len(split))
        gain = gain * jnp.repeat(jnp.exp(steps), dims[position] // blocks).reshape((-1,) + (1,) * (len(dims) - 1 - position))
    return gain


def centred(stream_key, shape, deviation, bound, shards=(), held_as=jnp.bfloat16):
    loudness = steps_of(stream_key, shape, shards, -0.22, 0.18) if shards else 1.0
    array = jax.random.normal(stream_key, shape, jnp.float32) * deviation * loudness
    return jnp.minimum(jnp.maximum(array, -bound), bound).astype(held_as)


def setup_inputs(seed: int = 0) -> dict:
    splits = jax.random.split(jax.random.key(seed), 18)
    return {
        "inputs": centred(splits[0], (SEQS, SEQ, D), 1.0, 6.0, ((0, 32),)),
        "counts": draw_counts(jax.random.fold_in(splits[17], 71), 0),
        "ln1_gain": jnp.clip(1.0 + 0.18 * jax.random.normal(splits[2], (D,), jnp.float32), 0.099609375, 1.8984375).astype(jnp.bfloat16),
        "ln1_bias": centred(splits[3], (D,), 0.3, 1.1953125),
        "log_dt": jnp.clip(-6.9 + 4.6000001430511475 * jax.random.uniform(splits[4], (D,), jnp.float32) ** steps_of(splits[4], (D,), ((0, 2),), -0.2, 0.2), -6.9, -2.3),
        "log_a": jnp.clip(jax.random.uniform(splits[5], (D, MODES), jnp.float32, -1.0, 1.0) * steps_of(splits[5], (D, MODES), ((0, 2),), -0.4, 0.0), -1.0, 1.0),
        "freq": jnp.clip(100.0 * jax.random.uniform(splits[6], (D, MODES), jnp.float32) ** steps_of(splits[6], (D, MODES), ((0, 2),), -0.2, 0.2), 0.0, 100.0),
        "c_real": centred(splits[7], (D, MODES), 0.5, 3.0, ((0, 2),), jnp.float32),
        "c_imag": centred(splits[8], (D, MODES), 0.5, 3.0, ((0, 2),), jnp.float32),
        "skip_gain": centred(splits[9], (D,), 1.0, 4.0, ((0, 2),), jnp.float32),
        "w_value": centred(splits[10], (D, D), (D // 4) ** -0.5, 0.375, ((1, 2),)),
        "w_gate": centred(splits[11], (D, D), D ** -0.5, 0.1875, ((1, 2),)),
        "ln2_gain": jnp.clip(1.0 + 0.18 * jax.random.normal(splits[12], (D,), jnp.float32), 0.099609375, 1.8984375).astype(jnp.bfloat16),
        "ln2_bias": centred(splits[13], (D,), 0.3, 1.1953125),
        "w_in": centred(splits[14], (D, FF), D ** -0.5, 0.1875, ((1, 2),)),
        "w_out": centred(splits[15], (FF, D), (FF // 2) ** -0.5, 0.125, ((0, 2),)),
        "cotangent": centred(splits[16], (SEQS, SEQ, D), 1.0, 6.0, ((0, 32),)),
    }


@jax.custom_vjp
def low(v):
    return lax.optimization_barrier(v.astype(jnp.bfloat16)).astype(jnp.float32)

@jax.custom_vjp
def low_back(v):
    return v

def low_keep(v):
    return (low(v), None)

def low_pass(kept, grad):
    return (grad,)

def back_keep(v):
    return (v, None)

def back_low(kept, grad):
    return (low(grad),)
low.defvjp(low_keep, low_pass)
low_back.defvjp(back_keep, back_low)
highest = lax.Precision.HIGHEST
norm_eps = 1e-05

def layer_norm(values, norm_gain, norm_bias):
    center = values - lax.optimization_barrier(jnp.mean(values, axis=-1, keepdims=True))
    inv_std = lax.rsqrt(lax.optimization_barrier(jnp.mean(center * center, axis=-1, keepdims=True)) + norm_eps)
    return center * inv_std * norm_gain + norm_bias

def kernel_of(log_dt, log_a, freq, c_real, c_imag):
    time_step = jnp.exp(log_dt)[:, None, None]
    positions = jnp.arange(SEQ).astype(jnp.float32)[None, None, :]
    decay_rate = time_step * jnp.exp(log_a)[:, :, None]
    decayed = jnp.exp(-decay_rate * positions)
    angles = time_step * freq[:, :, None] * positions
    summands = decayed * (c_real[:, :, None] * jnp.cos(angles) - c_imag[:, :, None] * jnp.sin(angles))
    return 2.0 * time_step[:, :, 0] * lax.optimization_barrier(jnp.sum(summands, axis=1))

def causal_conv(signal, kernel):
    length = signal.shape[1]
    spectrum = jnp.fft.rfft(signal, n=2 * length, axis=1) * jnp.fft.rfft(kernel.T, n=2 * length, axis=0)[None]
    return jnp.fft.irfft(spectrum, n=2 * length, axis=1)[:, :length]

def project(left, right):
    return jnp.einsum('nld,de->nle', left, right, precision=highest)

def reference(inputs, counts, ln1_gain, ln1_bias, log_dt, log_a, freq, c_real, c_imag, skip_gain, w_value, w_gate, ln2_gain, ln2_bias, w_in, w_out, cotangent):
    used_rows = (jnp.arange(SEQS) % GROUP < jnp.repeat(counts, GROUP)).astype(jnp.float32)

    def forward(source, gain1, bias1, step_log, rate_log, turn_rate, real_part, imag_part, direct, value_w, gate_w, gain2, bias2, in_w, out_w):
        kernel = low(kernel_of(step_log, rate_log, turn_rate, real_part, imag_part))

        def one_group(pair):
            block, flags = pair
            normed1 = low(layer_norm(block, gain1, bias1))
            mixed = low_back(causal_conv(normed1, kernel)) + direct * normed1
            act_low = low(jax.nn.gelu(mixed))
            value_proj = low_back(project(act_low, value_w))
            gate_proj = low_back(project(act_low, gate_w))
            glu_out = low_back(low(value_proj * jax.nn.sigmoid(gate_proj)))
            residual = block + glu_out
            normed2 = low(layer_norm(residual, gain2, bias2))
            pre_act = low_back(project(normed2, in_w))
            hidden = low(jax.nn.gelu(pre_act))
            ffn_out = low_back(project(hidden, out_w))
            return flags[:, None, None] * (residual + ffn_out)
        blocks = source.reshape(SHARDS, GROUP, SEQ, D)
        result = lax.map(jax.checkpoint(one_group), (blocks, used_rows.reshape(SHARDS, GROUP)))
        return result.reshape(SEQS, SEQ, D)
    floats = (inputs.astype(jnp.float32), ln1_gain.astype(jnp.float32), ln1_bias.astype(jnp.float32), log_dt.astype(jnp.float32), log_a.astype(jnp.float32), freq.astype(jnp.float32), c_real.astype(jnp.float32), c_imag.astype(jnp.float32), skip_gain.astype(jnp.float32), w_value.astype(jnp.float32), w_gate.astype(jnp.float32), ln2_gain.astype(jnp.float32), ln2_bias.astype(jnp.float32), w_in.astype(jnp.float32), w_out.astype(jnp.float32))
    output, backward = jax.vjp(forward, *floats)
    grads = backward(cotangent.astype(jnp.float32))
    return (output.astype(jnp.bfloat16), grads[0].astype(jnp.bfloat16), grads[1], grads[2], grads[3], grads[4], grads[5], grads[6], grads[7], grads[8], grads[9], grads[10], grads[11], grads[12], grads[13], grads[14])
```

```python
import numpy as np, ml_dtypes, jax, jax.numpy as jnp
from jax import lax
from jax.experimental import pallas as pl
from jax.experimental.pallas import tpu as pltpu
from jax.sharding import PartitionSpec as P

VMEM_LIMIT = 56 * 1024 * 1024
F32, BF16 = jnp.float32, jnp.bfloat16
LANES = 128
Q = 32


def transform_table(length):
    f = np.arange(length, dtype=np.int64)[:, None]
    t = np.arange(length, dtype=np.int64)[None, :]
    turn = ((4 * f + 1) * t) % (4 * length)
    angle = turn * (2.0 * np.pi / (4 * length))
    return np.concatenate([np.cos(angle), -np.sin(angle)], axis=0)


def cmul(a, b):
    return a[0] * b[0] - a[1] * b[1], a[0] * b[1] + a[1] * b[0]


def fill_powers(base_r, base_i, out_r, out_i, tmp, scale=None):
    modes = base_r.shape[0]
    p1 = (base_r, base_i)
    p2 = cmul(p1, p1)
    p4 = cmul(p2, p2)
    p8 = cmul(p4, p4)
    p16 = cmul(p8, p8)
    for i, p in enumerate((p1, p2, p4, p8, p16)):
        tmp[2 * i] = p[0]
        tmp[2 * i + 1] = p[1]
    if scale is not None:
        tmp[10] = scale[0]
        tmp[11] = scale[1]
    row = lax.broadcasted_iota(jnp.int32, (8, LANES), 0)
    one = jnp.ones((8, LANES), F32)
    zero = jnp.zeros((8, LANES), F32)

    def mode(n, carry):
        def at(i):
            return (
                jnp.broadcast_to(tmp[2 * i, pl.ds(n, 1), :], (8, LANES)),
                jnp.broadcast_to(tmp[2 * i + 1, pl.ds(n, 1), :], (8, LANES)),
            )

        p = (one, zero) if scale is None else at(5)
        for bit in range(3):
            q = cmul(p, at(bit))
            on = (row & (1 << bit)) != 0
            p = (jnp.where(on, q[0], p[0]), jnp.where(on, q[1], p[1]))
        parts = [p, cmul(p, at(3))]
        p16_here = at(4)
        parts += [cmul(parts[0], p16_here), cmul(parts[1], p16_here)]
        for j, part in enumerate(parts):
            out_r[n, 8 * j : 8 * j + 8, :] = part[0]
            out_i[n, 8 * j : 8 * j + 8, :] = part[1]
        return carry

    lax.fori_loop(0, modes, mode, 0)


def kernel_body(z_ref, k_ref, zr, zi, wr, wi, tmp):
    fill_powers(z_ref[0], z_ref[1], zr, zi, tmp)
    fill_powers(z_ref[2], z_ref[3], wr, wi, tmp, (z_ref[4], z_ref[5]))
    modes = z_ref.shape[1]
    step = 4
    blocks = k_ref.shape[0] // Q

    def rows(i, carry):
        d = i * step
        acc = [jnp.zeros((Q, LANES), F32) for _ in range(step)]
        for n in range(modes):
            a, b = zr[n], zi[n]
            for u in range(step):
                acc[u] = acc[u] + (
                    wr[n, pl.ds(d + u, 1), :] * a - wi[n, pl.ds(d + u, 1), :] * b
                )
        for u in range(step):
            k_ref[pl.ds(pl.multiple_of((d + u) * Q, Q), Q), :] = acc[u].astype(BF16)
        return carry

    lax.fori_loop(0, blocks // step, rows, 0)


def make_kernel(z, length):
    modes, channels = z.shape[1:]
    return pl.pallas_call(
        kernel_body,
        grid=(channels // LANES,),
        in_specs=[pl.BlockSpec((6, modes, LANES), lambda i: (0, 0, i))],
        out_specs=pl.BlockSpec((length, LANES), lambda i: (0, i)),
        out_shape=jax.ShapeDtypeStruct((length, channels), BF16),
        scratch_shapes=[pltpu.VMEM((modes, Q, LANES), F32)] * 4
        + [pltpu.VMEM((12, modes, LANES), F32)],
        compiler_params=pltpu.CompilerParams(vmem_limit_bytes=VMEM_LIMIT),
        name="make_kernel",
    )(z)


def moments_body(z_ref, g_ref, out_ref, zr, zi, wr, wi, tmp, gl):
    fill_powers(z_ref[0], z_ref[1], zr, zi, tmp)
    fill_powers(z_ref[2], z_ref[3], wr, wi, tmp)
    modes = z_ref.shape[1]
    blocks = g_ref.shape[0] // Q

    def weigh(i, carry):
        at = pl.ds(pl.multiple_of(i * Q, Q), Q)
        pos = (lax.broadcasted_iota(jnp.int32, (Q, LANES), 0) + i * Q).astype(F32)
        gl[at, :] = g_ref[at, :] * pos
        return carry

    lax.fori_loop(0, blocks, weigh, 0)
    pair = 2

    def mode(i, carry):
        n = i * pair
        sums = [[jnp.zeros((Q, LANES), F32) for _ in range(4)] for _ in range(pair)]
        for d in range(blocks):
            g = g_ref[d * Q : (d + 1) * Q, :]
            h = gl[d * Q : (d + 1) * Q, :]
            for u in range(pair):
                a = wr[n + u, d : d + 1, :]
                b = wi[n + u, d : d + 1, :]
                s = sums[u]
                s[0] = s[0] + g * a
                s[1] = s[1] + g * b
                s[2] = s[2] + h * a
                s[3] = s[3] + h * b
        for u in range(pair):
            s = sums[u]
            z = (zr[n + u], zi[n + u])
            first = cmul(z, (s[0], s[1]))
            second = cmul(z, (s[2], s[3]))
            for j, v in enumerate(first + second):
                out_ref[j, pl.ds(n + u, 1), :] = jnp.sum(v, axis=0, keepdims=True)
        return carry

    lax.fori_loop(0, modes // pair, mode, 0)


def make_moments(z, g):
    modes, channels = z.shape[1:]
    length = g.shape[0]
    return pl.pallas_call(
        moments_body,
        grid=(channels // LANES,),
        in_specs=[
            pl.BlockSpec((4, modes, LANES), lambda i: (0, 0, i)),
            pl.BlockSpec((length, LANES), lambda i: (0, i)),
        ],
        out_specs=pl.BlockSpec((4, modes, LANES), lambda i: (0, 0, i)),
        out_shape=jax.ShapeDtypeStruct((4, modes, channels), F32),
        scratch_shapes=[pltpu.VMEM((modes, Q, LANES), F32)] * 4
        + [pltpu.VMEM((12, modes, LANES), F32), pltpu.VMEM((length, LANES), F32)],
        compiler_params=pltpu.CompilerParams(vmem_limit_bytes=VMEM_LIMIT),
        name="make_moments",
    )(z, g)


GELU_A = 0.7978845608028654
GELU_B = 0.044715


def gelu(v):
    return 0.5 * v * (1.0 + jnp.tanh(GELU_A * (v + GELU_B * (v * v * v))))


def gelu_slope(v):
    sq = v * v
    th = jnp.tanh(GELU_A * (v + GELU_B * (sq * v)))
    return 0.5 * (1.0 + th) + 0.5 * v * (1.0 - th * th) * (GELU_A + (3.0 * GELU_A * GELU_B) * sq)


def dot(a, b):
    return jnp.dot(a, b, preferred_element_type=F32)


FT = 512
TT = 256


def conv_body(x_ref, k_ref, skip_ref, fwd_ref, inv_ref, mixed_ref, act_ref, xs_ref, ks_ref, ys):
    n = x_ref.shape[0]
    x = x_ref[...]
    k = k_ref[...]
    for i in range(n // FT):
        re = pl.ds(i * FT, FT)
        im = pl.ds(n + i * FT, FT)
        xr, xi = dot(fwd_ref[re, :], x), dot(fwd_ref[im, :], x)
        kr, ki = dot(fwd_ref[re, :], k), dot(fwd_ref[im, :], k)
        xs_ref[re, :] = xr.astype(BF16)
        xs_ref[im, :] = xi.astype(BF16)
        ks_ref[re, :] = kr.astype(BF16)
        ks_ref[im, :] = ki.astype(BF16)
        ys[re, :] = (xr * kr - xi * ki).astype(BF16)
        ys[im, :] = (xr * ki + xi * kr).astype(BF16)
    y = ys[...]
    for i in range(n // TT):
        at = pl.ds(i * TT, TT)
        mixed = dot(inv_ref[at, :], y) + skip_ref[...] * x_ref[at, :].astype(F32)
        mixed_ref[at, :] = mixed
        act_ref[at, :] = gelu(mixed).astype(BF16)


CB = 256


def conv_forward(x, k, skip, fwd, inv):
    n, channels = x.shape
    col = lambda rows: pl.BlockSpec((rows, CB), lambda i: (0, i))
    whole = lambda a: pl.BlockSpec(a.shape, lambda i: (0, 0), pipeline_mode=pl.Buffered(1))
    return pl.pallas_call(
        conv_body,
        grid=(channels // CB,),
        in_specs=[col(n), col(n), col(1), whole(fwd), whole(inv)],
        out_specs=[col(n), col(n), col(2 * n), col(2 * n)],
        out_shape=[
            jax.ShapeDtypeStruct((n, channels), F32),
            jax.ShapeDtypeStruct((n, channels), BF16),
            jax.ShapeDtypeStruct((2 * n, channels), BF16),
            jax.ShapeDtypeStruct((2 * n, channels), BF16),
        ],
        scratch_shapes=[pltpu.VMEM((2 * n, CB), BF16)],
        compiler_params=pltpu.CompilerParams(vmem_limit_bytes=VMEM_LIMIT),
        name="conv_forward",
    )(x, k, skip, fwd, inv)


def back_body(
    ga_ref, mixed_ref, x_ref, xs_ref, ks_ref, skip_ref, fwd_ref, inv_ref,
    gn_ref, gk_ref, sg_ref, gm, gy, ax, ak,
):
    n = x_ref.shape[0]
    total = jnp.zeros((1, CB), F32)
    for i in range(n // TT):
        at = pl.ds(i * TT, TT)
        v = ga_ref[at, :] * gelu_slope(mixed_ref[at, :])
        gm[at, :] = v
        gy[at, :] = v.astype(BF16)
        total += jnp.sum(v * x_ref[at, :].astype(F32), axis=0, keepdims=True)
    sg_ref[...] = total
    g = gy[...]
    for i in range(n // FT):
        re = pl.ds(i * FT, FT)
        im = pl.ds(n + i * FT, FT)
        gr, gi = dot(fwd_ref[re, :], g), dot(fwd_ref[im, :], g)
        for src, dst in ((ks_ref, ax), (xs_ref, ak)):
            a, b = src[re, :].astype(F32), src[im, :].astype(F32)
            dst[re, :] = (a * gr + b * gi).astype(BF16)
            dst[im, :] = (a * gi - b * gr).astype(BF16)
    yx = ax[...]
    yk = ak[...]
    for i in range(n // TT):
        at = pl.ds(i * TT, TT)
        gk_ref[at, :] = dot(inv_ref[at, :], yk)
        gn_ref[at, :] = dot(inv_ref[at, :], yx) + skip_ref[...] * gm[at, :]


def conv_backward(ga, mixed, x, xs, ks, skip, fwd, inv):
    n, channels = x.shape
    col = lambda rows: pl.BlockSpec((rows, CB), lambda i: (0, i))
    whole = lambda a: pl.BlockSpec(a.shape, lambda i: (0, 0), pipeline_mode=pl.Buffered(1))
    return pl.pallas_call(
        back_body,
        grid=(channels // CB,),
        in_specs=[col(n), col(n), col(n), col(2 * n), col(2 * n), col(1), whole(fwd), whole(inv)],
        out_specs=[col(n), col(n), col(1)],
        out_shape=[
            jax.ShapeDtypeStruct((n, channels), F32),
            jax.ShapeDtypeStruct((n, channels), F32),
            jax.ShapeDtypeStruct((1, channels), F32),
        ],
        scratch_shapes=[pltpu.VMEM((n, CB), F32), pltpu.VMEM((n, CB), BF16)]
        + [pltpu.VMEM((2 * n, CB), BF16)] * 2,
        compiler_params=pltpu.CompilerParams(vmem_limit_bytes=VMEM_LIMIT),
        name="conv_backward",
    )(ga, mixed, x, xs, ks, skip, fwd, inv)


def modes_of(log_dt, log_a, freq, c_real, c_imag):
    dt = jnp.exp(log_dt)[None, :]
    rate = dt * jnp.exp(log_a)
    turn = dt * freq
    rho, rho_q = jnp.exp(-rate), jnp.exp(-float(Q) * rate)
    return jnp.stack(
        [
            rho * jnp.cos(turn), rho * jnp.sin(turn),
            rho_q * jnp.cos(Q * turn), rho_q * jnp.sin(Q * turn),
            2.0 * dt * c_real, 2.0 * dt * c_imag,
        ]
    )
norm_eps = 1e-05


def norm_forward(values, norm_gain, norm_bias):
    center = values - jnp.mean(values, axis=-1, keepdims=True)
    inv_std = lax.rsqrt(jnp.mean(center * center, axis=-1, keepdims=True) + norm_eps)
    standard = center * inv_std
    return (standard * norm_gain + norm_bias, standard, inv_std)


def norm_backward(incoming, standard, inv_std, norm_gain):
    scaled = incoming * norm_gain
    value_grad = inv_std * (
        scaled
        - jnp.mean(scaled, axis=-1, keepdims=True)
        - standard * jnp.mean(scaled * standard, axis=-1, keepdims=True)
    )
    return (value_grad, jnp.sum(incoming * standard, axis=0), jnp.sum(incoming, axis=0))


def contract_rows(left, right):
    return lax.dot_general(left, right, (((0,), (0,)), ((), ())), preferred_element_type=F32)


def contract_cols(left, right):
    return lax.dot_general(left, right, (((1,), (1,)), ((), ())), preferred_element_type=F32)


SWAP = ((0, 1), (1, 0))


def over_core(values):
    return lax.ppermute(values, "core", SWAP)


def over_tensor(values):
    return lax.ppermute(values, "tensor", SWAP)


def ordered(index, mine, other, axis):
    first = jnp.where(index == 0, mine, other)
    second = jnp.where(index == 0, other, mine)
    return jnp.concatenate([first, second], axis=axis)


def part(values, index, axis):
    half = values.shape[axis] // 2
    return lax.dynamic_slice_in_dim(values, index * half, half, axis)


def fetch(weight, axis):
    core = lax.axis_index("core")
    direct = over_tensor(part(weight, core, axis))
    return direct, over_core(direct)


def reduce_parts(own, direct, via, axis):
    core = lax.axis_index("core")
    there = direct + over_core(via.astype(BF16)).astype(F32)
    from_core = over_core(part(own, 1 - core, axis).astype(BF16)).astype(F32)
    from_tensor = over_tensor(there.astype(BF16)).astype(F32)
    here = part(own, core, axis) + from_core + from_tensor
    total = lax.psum(here.astype(BF16), "pair")
    return ordered(core, total, over_core(total), axis).astype(F32)


def shards(
    inputs, counts, ln1_gain, ln1_bias, log_dt, log_a, freq, c_real, c_imag, skip_gain,
    w_value, w_gate, ln2_gain, ln2_bias, w_in, w_out, cotangent,
):
    _, length, width = inputs.shape
    core, side = lax.axis_index("core"), lax.axis_index("tensor")
    used_flag = (side < counts[0]).astype(F32)
    source = inputs.reshape(length, width).astype(F32)
    gain_first, bias_first = ln1_gain.astype(F32), ln1_bias.astype(F32)
    gain_second, bias_second = ln2_gain.astype(F32), ln2_bias.astype(F32)
    table = transform_table(length)
    fwd = jnp.asarray(table.astype(ml_dtypes.bfloat16))
    inv = jnp.asarray(np.ascontiguousarray((table.T / length).astype(ml_dtypes.bfloat16)))

    modes = log_a.shape[1]
    local = jnp.concatenate(
        [log_a.T, freq.T, c_real.T, c_imag.T, log_dt[None], skip_gain[None]], axis=0
    )
    params = ordered(side, local, over_tensor(local), 1)
    log_a_all, freq_all, real_all, imag_all = (params[i * modes : (i + 1) * modes] for i in range(4))
    log_dt_all, skip = params[4 * modes], params[4 * modes + 1 : 4 * modes + 2]

    value_parts, gate_parts = fetch(w_value, 1), fetch(w_gate, 1)
    in_parts, out_parts = (w_in,) + fetch(w_in, 1), (w_out,) + fetch(w_out, 0)
    value_w = ordered(side, w_value, ordered(core, *value_parts, 1), 1)
    gate_w = ordered(side, w_gate, ordered(core, *gate_parts, 1), 1)

    normed1_full, standard1, inv_std1 = norm_forward(source, gain_first, bias_first)
    normed1 = normed1_full.astype(BF16)
    z = modes_of(log_dt_all, log_a_all, freq_all, real_all, imag_all)
    kernel = make_kernel(z, length)
    mixed, act, spectrum, kernel_spectrum = conv_forward(normed1, kernel, skip, fwd, inv)

    value_proj = dot(act, value_w)
    gate_sig = jax.nn.sigmoid(dot(act, gate_w))
    residual = source + (value_proj * gate_sig).astype(BF16).astype(F32)
    normed2_full, standard2, inv_std2 = norm_forward(residual, gain_second, bias_second)
    normed2 = normed2_full.astype(BF16)
    grad_low = (used_flag * cotangent.reshape(length, width).astype(F32)).astype(BF16)
    grad_out = grad_low.astype(F32)
    ffn_out = 0.0
    grad_normed2 = 0.0
    in_grads, out_grads = [], []
    for w_i, w_o in zip(in_parts, out_parts):
        pre_act = dot(normed2, w_i)
        hidden = gelu(pre_act).astype(BF16)
        slope = gelu_slope(pre_act).astype(BF16)
        ffn_out = ffn_out + dot(hidden, w_o)
        out_grads.append(contract_rows(hidden, grad_low))
        grad_pre = (contract_cols(grad_low, w_o) * slope.astype(F32)).astype(BF16)
        in_grads.append(contract_rows(normed2, grad_pre))
        grad_normed2 = grad_normed2 + contract_cols(grad_pre, w_i)
    output = (used_flag * (residual + ffn_out)).astype(BF16).reshape(inputs.shape)
    out_total = reduce_parts(*out_grads, 0)
    in_total = reduce_parts(*in_grads, 1)

    grad_resid_part, gain_second_grad, bias_second_grad = norm_backward(
        grad_normed2, standard2, inv_std2, gain_second
    )
    grad_residual = grad_out + grad_resid_part
    grad_glu = grad_residual.astype(BF16).astype(F32)
    grad_value = (grad_glu * gate_sig).astype(BF16)
    grad_gate = (grad_glu * value_proj * gate_sig * (1.0 - gate_sig)).astype(BF16)
    grad_act = contract_cols(grad_value, value_w) + contract_cols(grad_gate, gate_w)

    def glu_total(grad):
        other = part(grad, 1 - side, 1)
        return reduce_parts(part(grad, side, 1), part(other, core, 1), part(other, 1 - core, 1), 1)

    value_total = glu_total(contract_rows(act, grad_value))
    gate_total = glu_total(contract_rows(act, grad_gate))

    grad_normed1, grad_kernel, skip_grad = conv_backward(
        grad_act, mixed, normed1, spectrum, kernel_spectrum, skip, fwd, inv
    )
    moments = make_moments(z[:4], grad_kernel)
    grad_source, gain_first_grad, bias_first_grad = norm_backward(
        grad_normed1, standard1, inv_std1, gain_first
    )
    input_grad = (grad_residual + grad_source).astype(BF16).reshape(inputs.shape)

    scale = 2.0 * jnp.exp(log_dt_all)[None, :]
    real_grad, imag_grad = scale * moments[0], -scale * moments[1]
    slope_r = scale * (real_all * moments[2] - imag_all * moments[3])
    slope_i = scale * (real_all * moments[3] + imag_all * moments[2])
    dt = jnp.exp(log_dt_all)[None, :]
    log_a_grad = -dt * jnp.exp(log_a_all) * slope_r
    freq_grad = -dt * slope_i
    log_dt_grad = jnp.sum(
        real_all * real_grad + imag_all * imag_grad + log_a_grad + freq_all * freq_grad,
        axis=0, keepdims=True,
    )
    small = jnp.concatenate(
        [log_a_grad, freq_grad, real_grad, imag_grad, log_dt_grad, skip_grad]
        + [g[None] for g in (gain_first_grad, bias_first_grad, gain_second_grad, bias_second_grad)],
        axis=0,
    )
    mine = part(small, side, 1) + over_tensor(part(small, 1 - side, 1))
    small = lax.psum(mine, ("pair", "core"))
    rows = small[4 * modes :]
    return (
        output,
        input_grad,
        rows[2],
        rows[3],
        rows[0],
        small[:modes].T,
        small[modes : 2 * modes].T,
        small[2 * modes : 3 * modes].T,
        small[3 * modes : 4 * modes].T,
        rows[1],
        value_total,
        gate_total,
        rows[4],
        rows[5],
        in_total,
        out_total,
    )


def solution(mesh):
    devices = mesh.devices
    cores = jax.sharding.Mesh(
        devices.reshape(devices.shape[0] // 2, 2, devices.shape[1]), ("pair", "core", "tensor")
    )
    batch, every = ("pair", "core"), ("pair", "core", "tensor")
    in_specs = (
        P(every, None, None), P(batch), P(), P(), P("tensor"), P("tensor", None), P("tensor", None),
        P("tensor", None), P("tensor", None), P("tensor"), P(None, "tensor"), P(None, "tensor"),
        P(), P(), P(None, "tensor"), P("tensor", None), P(every, None, None),
    )
    out_specs = (
        P(every, None, None), P(every, None, None), P("tensor"), P("tensor"), P("tensor"),
        P("tensor", None), P("tensor", None), P("tensor", None), P("tensor", None), P("tensor"),
        P(None, "tensor"), P(None, "tensor"), P("tensor"), P("tensor"), P(None, "tensor"),
        P("tensor", None),
    )
    return jax.shard_map(shards, mesh=cores, in_specs=in_specs, out_specs=out_specs, check_vma=False)
```

```python
import math

import ml_dtypes
import numpy as np

import jax
import jax.numpy as jnp
from jax import lax
from jax.experimental import pallas as pl
from jax.experimental.pallas import tpu as pltpu
from jax.sharding import PartitionSpec as P

VMEM_LIMIT = 56 * 1024 * 1024
F32, BF16 = jnp.float32, jnp.bfloat16
LANES = 128
MESH = pl.DeviceIdType.MESH
KERNEL_INNER = 64
MOMENT_INNER = 32
CB = 256
DFT_ROWS = 512
TOKEN_ROWS = 256
FFN_TILE = 512
GELU_A = 0.7978845608028654
GELU_B = 0.044715
norm_eps = 1e-05


def params_of(**extra):
    return pltpu.CompilerParams(vmem_limit_bytes=VMEM_LIMIT, **extra)


class CoreExchange:
    def __init__(self, pairs, send, recv):
        self.pairs, self.send, self.recv = pairs, send, recv
        self.other = {"core": 1 - lax.axis_index("core")}

    def greet(self):
        pl.semaphore_signal(
            pltpu.get_barrier_semaphore(), inc=1, device_id=self.other, device_id_type=MESH
        )

    def meet(self):
        pl.semaphore_wait(pltpu.get_barrier_semaphore(), 1)

    def copies(self, slot):
        return [
            pltpu.make_async_remote_copy(
                src_ref=mine.at[slot], dst_ref=theirs.at[slot],
                send_sem=self.send.at[i, slot], recv_sem=self.recv.at[i, slot],
                device_id=self.other, device_id_type=MESH,
            )
            for i, (mine, theirs) in enumerate(self.pairs)
        ]

    def start(self, slot):
        for copy in self.copies(slot):
            copy.start()

    def arrived(self, slot):
        for copy in self.copies(slot):
            copy.wait_recv()

    def sent(self, slots):
        for slot in range(slots):
            for copy in self.copies(slot):
                copy.wait_send()


def exchange_sems(pairs, slots):
    return [pltpu.SemaphoreType.DMA((pairs, slots))] * 2


def transform_table(length):
    f = np.arange(length, dtype=np.int64)[:, None]
    t = np.arange(length, dtype=np.int64)[None, :]
    turn = ((4 * f + 1) * t) % (4 * length)
    angle = turn * (2.0 * np.pi / (4 * length))
    return np.concatenate([np.cos(angle), -np.sin(angle)], axis=0)


def cmul(a, b):
    return a[0] * b[0] - a[1] * b[1], a[0] * b[1] + a[1] * b[0]


def log2_of(count):
    bits = count.bit_length() - 1
    assert 1 << bits == count
    return bits


def fill_powers(base, count, out_r, out_i, tmp, scale=None):
    bits = log2_of(count)
    p = base
    for i in range(bits):
        tmp[2 * i] = p[0]
        tmp[2 * i + 1] = p[1]
        p = cmul(p, p)
    if scale is not None:
        tmp[2 * bits] = scale[0]
        tmp[2 * bits + 1] = scale[1]
    row = lax.broadcasted_iota(jnp.int32, (8, LANES), 0)

    def mode(n, carry):
        def at(i):
            return tuple(
                jnp.broadcast_to(tmp[2 * i + j, pl.ds(n, 1), :], (8, LANES)) for j in range(2)
            )

        if scale is None:
            p = (jnp.ones((8, LANES), F32), jnp.zeros((8, LANES), F32))
        else:
            p = at(bits)
        for bit in range(3):
            q = cmul(p, at(bit))
            on = (row & (1 << bit)) != 0
            p = (jnp.where(on, q[0], p[0]), jnp.where(on, q[1], p[1]))
        parts = [p]
        for bit in range(3, bits):
            w = at(bit)
            parts += [cmul(x, w) for x in parts]
        for j, part in enumerate(parts):
            out_r[n, 8 * j : 8 * j + 8, :] = part[0]
            out_i[n, 8 * j : 8 * j + 8, :] = part[1]
        return carry

    lax.fori_loop(0, base[0].shape[0], mode, 0)
    return p


def split_params(packed_ref, log_dt_ref):
    rows = packed_ref[...].T
    modes = rows.shape[0] // 4
    log_a, freq, c_real, c_imag = (rows[i * modes : (i + 1) * modes] for i in range(4))
    step = jnp.exp(log_dt_ref[...])
    rate = jnp.exp(log_a)
    decay = jnp.exp(-(step * rate))
    turn = step * freq
    return step, rate, freq, c_real, c_imag, (decay * jnp.cos(turn), decay * jnp.sin(turn))


def kernel_body(packed_ref, log_dt_ref, k_ref, zr, zi, wr, wi, tmp):
    step, _, _, c_real, c_imag, z = split_params(packed_ref, log_dt_ref)
    inner = zr.shape[1]
    outer = wr.shape[1]
    z_inner = fill_powers(z, inner, zr, zi, tmp)
    fill_powers(z_inner, outer, wr, wi, tmp, (2.0 * step * c_real, 2.0 * step * c_imag))
    modes = c_real.shape[0]
    group = 2

    def rows(i, carry):
        d = i * group
        acc = [jnp.zeros((inner, LANES), F32) for _ in range(group)]
        for n in range(modes):
            a, b = zr[n], zi[n]
            for u in range(group):
                acc[u] = acc[u] + (
                    wr[n, pl.ds(d + u, 1), :] * a - wi[n, pl.ds(d + u, 1), :] * b
                )
        for u in range(group):
            at = pl.ds(pl.multiple_of((d + u) * inner, inner), inner)
            k_ref[at, :] = acc[u].astype(BF16)
        return carry

    lax.fori_loop(0, outer // group, rows, 0)


def power_scratch(modes, inner, outer):
    return (
        [pltpu.VMEM((modes, inner, LANES), F32)] * 2
        + [pltpu.VMEM((modes, outer, LANES), F32)] * 2
        + [pltpu.VMEM((20, modes, LANES), F32)]
    )


def make_kernel(packed, log_dt, length):
    channels, modes = packed.shape[0], packed.shape[1] // 4
    return pl.pallas_call(
        kernel_body,
        grid=(channels // LANES,),
        in_specs=[
            pl.BlockSpec((LANES, 4 * modes), lambda i: (i, 0)),
            pl.BlockSpec((1, LANES), lambda i: (0, i)),
        ],
        out_specs=pl.BlockSpec((length, LANES), lambda i: (0, i)),
        out_shape=jax.ShapeDtypeStruct((length, channels), BF16),
        scratch_shapes=power_scratch(modes, KERNEL_INNER, length // KERNEL_INNER),
        compiler_params=params_of(),
        name="make_kernel",
    )(packed, log_dt)


def moments_body(
    packed_ref, log_dt_ref, g_ref, out_ref, zr, zi, wr, wi, tmp, sums
):
    step, rate, freq, c_real, c_imag, z = split_params(packed_ref, log_dt_ref)
    inner, outer = zr.shape[1], wr.shape[1]
    z_inner = fill_powers(z, inner, zr, zi, tmp)
    fill_powers(z_inner, outer, wr, wi, tmp)
    modes = c_real.shape[0]
    pos = lax.broadcasted_iota(jnp.int32, (inner, LANES), 0).astype(F32)

    def mode(n, carry):
        zero = jnp.zeros((inner, LANES), F32)
        sr, si, tr, ti = zero, zero, zero, zero
        for d in reversed(range(outer)):
            v = g_ref[0, d * inner : (d + 1) * inner, :]
            sr = sr + v * wr[n, d : d + 1, :]
            si = si + v * wi[n, d : d + 1, :]
            if d > 0:
                tr = tr + sr
                ti = ti + si
        zn = (zr[n], zi[n])
        first = cmul(zn, (sr, si))
        second = cmul(zn, (pos * sr + float(inner) * tr, pos * si + float(inner) * ti))
        for j, v in enumerate(first + second):
            sums[j, pl.ds(n, 1), :] = jnp.sum(v, axis=0, keepdims=True)
        return carry

    lax.fori_loop(0, modes, mode, 0)
    scale = 2.0 * step
    real_grad, imag_grad = scale * sums[0], -scale * sums[1]
    slope_r = scale * (c_real * sums[2] - c_imag * sums[3])
    slope_i = scale * (c_real * sums[3] + c_imag * sums[2])
    log_a_grad = -step * rate * slope_r
    freq_grad = -step * slope_i
    log_dt_grad = jnp.sum(
        c_real * real_grad + c_imag * imag_grad + log_a_grad + freq * freq_grad,
        axis=0, keepdims=True,
    )
    for i, part in enumerate((log_a_grad, freq_grad, real_grad, imag_grad)):
        out_ref[i * modes : (i + 1) * modes, :] = part
    top = 4 * modes
    row = lax.broadcasted_iota(jnp.int32, (8, LANES), 0)
    out_ref[top : top + 8, :] = jnp.where(row == 0, log_dt_grad, 0.0)


def make_moments(packed, log_dt, g, at):
    half, modes = packed.shape[0], packed.shape[1] // 4
    length = g.shape[1]
    return pl.pallas_call(
        moments_body,
        grid=(half // LANES,),
        in_specs=[
            pl.BlockSpec((LANES, 4 * modes), lambda i: (i, 0)),
            pl.BlockSpec((1, LANES), lambda i: (0, i)),
            pl.BlockSpec((1, length, LANES), lambda i: (at, 0, i)),
        ],
        out_specs=pl.BlockSpec((4 * modes + 8, LANES), lambda i: (0, i)),
        scratch_shapes=power_scratch(modes, MOMENT_INNER, length // MOMENT_INNER)
        + [pltpu.VMEM((4, modes, LANES), F32)],
        out_shape=jax.ShapeDtypeStruct((4 * modes + 8, half), F32),
        compiler_params=params_of(),
        name="make_moments",
    )(packed, log_dt, g)


def gelu_both(v):
    sq = v * v
    th = jnp.tanh(v * (GELU_A + (GELU_A * GELU_B) * sq))
    rise = 0.5 + 0.5 * th
    slope = rise + v * (0.5 - 0.5 * th * th) * (GELU_A + (3.0 * GELU_A * GELU_B) * sq)
    return v * rise, slope


def gelu(v):
    return gelu_both(v)[0]


def gelu_slope(v):
    return gelu_both(v)[1]


def dot(a, b):
    return jnp.dot(a, b, preferred_element_type=F32)


def conv_body(
    where_ref, x_ref, k0, k1, k2, k3, skip_ref, fwd_ref, inv_ref,
    mixed_ref, act_ref, xs_ref, ks_ref, k, ys,
):
    n = x_ref.shape[0]
    block = pl.program_id(0)
    here = 2 * lax.rem(block // 2 + where_ref[0], 2) + lax.rem(block + where_ref[1], 2)
    for i, ref in enumerate((k0, k1, k2, k3)):
        @pl.when(here == i)
        def _():
            k[...] = ref[...]

    x = x_ref[...]
    kernel = k[...]
    for i in range(n // DFT_ROWS):
        re = pl.ds(i * DFT_ROWS, DFT_ROWS)
        im = pl.ds(n + i * DFT_ROWS, DFT_ROWS)
        xr, xi = dot(fwd_ref[re, :], x), dot(fwd_ref[im, :], x)
        kr, ki = dot(fwd_ref[re, :], kernel), dot(fwd_ref[im, :], kernel)
        xs_ref[re, :] = xr.astype(BF16)
        xs_ref[im, :] = xi.astype(BF16)
        ks_ref[re, :] = kr.astype(BF16)
        ks_ref[im, :] = ki.astype(BF16)
        ys[re, :] = (xr * kr - xi * ki).astype(BF16)
        ys[im, :] = (xr * ki + xi * kr).astype(BF16)
    y = ys[...]
    for i in range(n // TOKEN_ROWS):
        at = pl.ds(i * TOKEN_ROWS, TOKEN_ROWS)
        mixed = dot(inv_ref[at, :], y) + skip_ref[...] * x_ref[at, :].astype(F32)
        mixed_ref[at, :] = mixed
        act_ref[at, :] = gelu(mixed).astype(BF16)


def conv_forward(where, x, kernels, skip, fwd, inv):
    n, channels = x.shape

    def col(rows):
        return pl.BlockSpec((rows, CB), lambda i, w: (0, i))

    def whole(a):
        return pl.BlockSpec(a.shape, lambda i, w: (0, 0), pipeline_mode=pl.Buffered(1))

    return pl.pallas_call(
        conv_body,
        grid_spec=pltpu.PrefetchScalarGridSpec(
            num_scalar_prefetch=1,
            grid=(channels // CB,),
            in_specs=[col(n)] + [whole(k) for k in kernels] + [col(1), whole(fwd), whole(inv)],
            out_specs=[col(n), col(n), col(2 * n), col(2 * n)],
            scratch_shapes=[pltpu.VMEM((n, CB), BF16), pltpu.VMEM((2 * n, CB), BF16)],
        ),
        out_shape=[
            jax.ShapeDtypeStruct((n, channels), F32),
            jax.ShapeDtypeStruct((n, channels), BF16),
            jax.ShapeDtypeStruct((2 * n, channels), BF16),
            jax.ShapeDtypeStruct((2 * n, channels), BF16),
        ],
        compiler_params=params_of(),
        name="conv_forward",
    )(where, x, *kernels, skip, fwd, inv)


def back_body(
    ga_ref, mixed_ref, x_ref, xs_ref, ks_ref, skip_ref, fwd_ref, inv_ref,
    gn_ref, gk_ref, sg_ref, gm, gy, ax, ak, mine, theirs, send, recv,
):
    step = pl.program_id(0)
    first = step < 2
    cores = CoreExchange([(mine, theirs)], send, recv)
    pl.when(step == 0)(cores.greet)
    n = x_ref.shape[0]
    total = jnp.zeros((1, CB), F32)
    for i in range(n // TOKEN_ROWS):
        at = pl.ds(i * TOKEN_ROWS, TOKEN_ROWS)
        v = ga_ref[at, :] * gelu_slope(mixed_ref[at, :])
        gm[at, :] = v
        gy[at, :] = v.astype(BF16)
        total += jnp.sum(v * x_ref[at, :].astype(F32), axis=0, keepdims=True)
    sg_ref[...] = total
    g = gy[...]
    for i in range(n // DFT_ROWS):
        re = pl.ds(i * DFT_ROWS, DFT_ROWS)
        im = pl.ds(n + i * DFT_ROWS, DFT_ROWS)
        gr, gi = dot(fwd_ref[re, :], g), dot(fwd_ref[im, :], g)
        for src, dst in ((ks_ref, ax), (xs_ref, ak)):
            a, b = src[re, :].astype(F32), src[im, :].astype(F32)
            dst[re, :] = (a * gr + b * gi).astype(BF16)
            dst[im, :] = (a * gi - b * gr).astype(BF16)
    yx = ax[...]
    yk = ak[...]
    for i in range(n // TOKEN_ROWS):
        at = pl.ds(i * TOKEN_ROWS, TOKEN_ROWS)
        gk_ref[0, at, :] = dot(inv_ref[at, :], yk)
        gn_ref[at, :] = dot(inv_ref[at, :], yx) + skip_ref[...] * gm[at, :]
    pl.when(step == 0)(cores.meet)

    @pl.when(first)
    def _():
        mine[step] = gk_ref[0]
        cores.start(step)

    @pl.when(jnp.logical_not(first))
    def _():
        cores.arrived(step - 2)
        gk_ref[0] = gk_ref[0] + theirs[step - 2]

    @pl.when(step == 3)
    def _():
        cores.sent(2)


def conv_backward(ga, mixed, x, xs, ks, skip, fwd, inv):
    n, channels = x.shape

    def block(i):
        side = lax.rem(lax.axis_index("tensor") + 1 + i, 2)
        half = lax.rem(lax.axis_index("core") + 1 + i // 2, 2)
        return 2 * side + half

    def col(rows):
        return pl.BlockSpec((rows, CB), lambda i: (0, block(i)))

    def whole(a):
        return pl.BlockSpec(a.shape, lambda i: (0, 0), pipeline_mode=pl.Buffered(1))

    return pl.pallas_call(
        back_body,
        grid=(channels // CB,),
        in_specs=[col(n), col(n), col(n), col(2 * n), col(2 * n), col(1), whole(fwd), whole(inv)],
        out_specs=[col(n), pl.BlockSpec((1, n, CB), lambda i: (jnp.maximum(i - 2, 0), 0, 0)), col(1)],
        out_shape=[
            jax.ShapeDtypeStruct((n, channels), F32),
            jax.ShapeDtypeStruct((2, n, CB), F32),
            jax.ShapeDtypeStruct((1, channels), F32),
        ],
        scratch_shapes=[pltpu.VMEM((n, CB), F32), pltpu.VMEM((n, CB), BF16)]
        + [pltpu.VMEM((2 * n, CB), BF16)] * 2
        + [pltpu.VMEM((2, n, CB), F32)] * 2
        + exchange_sems(1, 2),
        compiler_params=params_of(collective_id=3, has_side_effects=True),
        name="conv_backward",
    )(ga, mixed, x, xs, ks, skip, fwd, inv)


def glu_body(
    act, source, value_w, gate_w, gain, bias, value_ref, sig_ref, residual_ref, n2_ref, n2t_ref
):
    value = dot(act[...], value_w[...])
    sig = 1.0 / (1.0 + jnp.exp(-dot(act[...], gate_w[...])))
    value_ref[...] = value.astype(BF16)
    sig_ref[...] = sig.astype(BF16)
    residual = source[...].astype(F32) + (value * sig).astype(BF16).astype(F32)
    residual_ref[...] = residual
    n2 = norm_forward(residual, gain[...], bias[...])[0].astype(BF16)
    n2_ref[...] = n2
    n2t_ref[...] = n2.T


def glu_kernel(act, source, value_w, gate_w, gain, bias):
    n, d = act.shape
    rows = pl.BlockSpec((TOKEN_ROWS, d), lambda i: (i, 0))

    def whole(a):
        return pl.BlockSpec(a.shape, lambda i: (0, 0), pipeline_mode=pl.Buffered(1))

    return pl.pallas_call(
        glu_body,
        grid=(n // TOKEN_ROWS,),
        in_specs=[rows, rows, whole(value_w), whole(gate_w), whole(gain), whole(bias)],
        out_specs=[rows] * 4 + [pl.BlockSpec((d, TOKEN_ROWS), lambda i: (0, i))],
        out_shape=[
            jax.ShapeDtypeStruct((n, d), BF16), jax.ShapeDtypeStruct((n, d), BF16),
            jax.ShapeDtypeStruct((n, d), F32), jax.ShapeDtypeStruct((n, d), BF16),
            jax.ShapeDtypeStruct((d, n), BF16),
        ],
        compiler_params=params_of(),
        name="glu_kernel",
    )(act, source, value_w, gate_w, gain, bias)


def glu_back_body(
    g_far, g_own, residual, cot, value, sig, act, value_w, gate_w, gain,
    resid_ref, ga_ref, gain_ref, bias_ref, there_ref, here_ref, gv, gt, mine, theirs, send, recv,
):
    step = pl.program_id(0)
    cores = CoreExchange([(mine, theirs)], send, recv)
    pl.when(step == 0)(cores.greet)
    chunks = act.shape[0] // TOKEN_ROWS
    width = gv.shape[2]

    @pl.when(step < chunks)
    def _():
        standard, inv_std = norm_forward(residual[...], 1.0, 0.0)[1:]
        part, gain_grad, bias_grad = norm_backward(
            g_far[...] + g_own[...], standard, inv_std, gain[...]
        )
        new = step == 0
        gain_ref[...] = jnp.where(new, 0.0, gain_ref[...]) + gain_grad[None]
        bias_ref[...] = jnp.where(new, 0.0, bias_ref[...]) + bias_grad[None]
        resid = cot[...].astype(F32) + part
        resid_ref[...] = resid
        grad = resid.astype(BF16).astype(F32)
        gate = sig[...].astype(F32)
        grad_value = (grad * gate).astype(BF16)
        grad_gate = (grad * value[...].astype(F32) * gate * (1.0 - gate)).astype(BF16)
        ga_ref[...] = contract_cols(grad_value, value_w[...]) + contract_cols(grad_gate, gate_w[...])
        at = pl.ds(pl.multiple_of(step * TOKEN_ROWS, TOKEN_ROWS), TOKEN_ROWS)
        for i in range(gv.shape[0]):
            gv[i, at, :] = grad_value[:, i * width : (i + 1) * width]
            gt[i, at, :] = grad_gate[:, i * width : (i + 1) * width]

    @pl.when(step >= chunks)
    def _():
        j = step - chunks
        side = lax.rem(lax.axis_index("tensor") + 1 + j, 2)
        half = lax.rem(lax.axis_index("core") + 1 + j // 2, 2)
        block = 2 * side + half
        grads = [contract_rows(act[...], gv[block]), contract_rows(act[...], gt[block])]
        pl.when(j == 0)(cores.meet)

        @pl.when(j < 2)
        def _():
            for i, g in enumerate(grads):
                mine[j, :, i * width : (i + 1) * width] = g.astype(BF16)
            cores.start(j)

        @pl.when(j == 2)
        def _():
            cores.arrived(0)
            for i, g in enumerate(grads):
                at = pl.ds(i * width, width)
                there_ref[:, at] = (g + theirs[0, :, at].astype(F32)).astype(BF16)

        @pl.when(j == 3)
        def _():
            cores.arrived(1)
            for i, g in enumerate(grads):
                at = pl.ds(i * width, width)
                here_ref[:, at] = g + theirs[1, :, at].astype(F32)
            cores.sent(2)


def glu_back_kernel(g_far, g_own, residual, cot, value, sig, act, value_w, gate_w, gain):
    n, d = act.shape
    chunks = n // TOKEN_ROWS
    width = d // 4

    def whole(a):
        return pl.BlockSpec(a.shape, lambda i: (0, 0), pipeline_mode=pl.Buffered(1))

    rows = pl.BlockSpec((TOKEN_ROWS, d), lambda i: (jnp.minimum(i, chunks - 1), 0))
    vector = pl.BlockSpec((1, d), lambda i: (0, 0))
    weight = pl.BlockSpec((d, 2 * width), lambda i: (0, 0))
    return pl.pallas_call(
        glu_back_body,
        grid=(chunks + 4,),
        in_specs=[rows] * 6 + [whole(act), whole(value_w), whole(gate_w), whole(gain)],
        out_specs=[rows, rows, vector, vector, weight, weight],
        scratch_shapes=[pltpu.VMEM((4, n, width), BF16)] * 2
        + [pltpu.VMEM((2, d, 2 * width), BF16)] * 2
        + exchange_sems(1, 2),
        out_shape=[
            jax.ShapeDtypeStruct((n, d), F32), jax.ShapeDtypeStruct((n, d), F32),
            jax.ShapeDtypeStruct((1, d), F32), jax.ShapeDtypeStruct((1, d), F32),
            jax.ShapeDtypeStruct((d, 2 * width), BF16), jax.ShapeDtypeStruct((d, 2 * width), F32),
        ],
        compiler_params=params_of(collective_id=2, has_side_effects=True),
        name="glu_back_kernel",
    )(g_far, g_own, residual, cot, value, sig, act, value_w, gate_w, gain)


def ffn_body(
    n2, n2t, gl, ia, ib, oa, ob, ffn, gn2, in_ref, out_ref,
    wi, wo, h, gp, in_mine, out_mine, in_theirs, out_theirs, send, recv,
):
    step, half = pl.program_id(0), in_mine.shape[0]
    first = step < half
    cores = CoreExchange([(in_mine, in_theirs), (out_mine, out_theirs)], send, recv)
    pl.when(step == 0)(cores.greet)

    @pl.when(first)
    def _():
        wi[...] = ia[...]
        wo[...] = oa[...]

    @pl.when(jnp.logical_not(first))
    def _():
        wi[...] = ib[...]
        wo[...] = ob[...]

    @pl.when(step == 0)
    def _():
        ffn[...] = jnp.zeros_like(ffn)
        gn2[...] = jnp.zeros_like(gn2)

    w1, w2 = wi[...], wo[...]
    for r in range(n2.shape[0] // TOKEN_ROWS):
        at = pl.ds(r * TOKEN_ROWS, TOKEN_ROWS)
        act, slope = gelu_both(dot(n2[at, :], w1))
        hidden = act.astype(BF16)
        grad_pre = (contract_cols(gl[at, :], w2) * slope).astype(BF16)
        h[at, :] = hidden
        gp[at, :] = grad_pre
        ffn[at, :] += dot(hidden, w2)
        gn2[at, :] += contract_cols(grad_pre, w1)
    out_grad = contract_rows(h[...], gl[...])
    in_grad = dot(n2t[...], gp[...])

    pl.when(step == 0)(cores.meet)

    @pl.when(first)
    def _():
        in_mine[step] = in_grad.astype(BF16)
        out_mine[step] = out_grad.astype(BF16)
        cores.start(step)

    @pl.when(jnp.logical_not(first))
    def _():
        cores.arrived(step - half)
        in_ref[...] = (in_grad + in_theirs[step - half].astype(F32)).astype(in_ref.dtype)
        out_ref[...] = (out_grad + out_theirs[step - half].astype(F32)).astype(out_ref.dtype)

    @pl.when(step == 2 * half - 1)
    def _():
        cores.sent(half)


def ffn_kernel(n2, n2t, gl, ins, outs, units, own):
    n, d = n2.shape
    half = units // FFN_TILE

    def whole(a):
        return pl.BlockSpec(a.shape, lambda s: (0, 0), pipeline_mode=pl.Buffered(1))

    def fst(s):
        at = jnp.minimum(s, half - 1)
        return at + (1 - lax.axis_index("core")) * half if own else at

    def snd(s):
        at = jnp.maximum(s - half, 0)
        return at + lax.axis_index("core") * half if own else at

    total = pl.BlockSpec((n, d), lambda s: (0, 0))
    dtype = F32 if own else BF16
    return pl.pallas_call(
        ffn_body,
        grid=(2 * half,),
        in_specs=[
            whole(n2), whole(n2t), whole(gl),
            pl.BlockSpec((d, FFN_TILE), lambda s: (0, fst(s))),
            pl.BlockSpec((d, FFN_TILE), lambda s: (0, snd(s))),
            pl.BlockSpec((FFN_TILE, d), lambda s: (fst(s), 0)),
            pl.BlockSpec((FFN_TILE, d), lambda s: (snd(s), 0)),
        ],
        out_specs=[
            total, total,
            pl.BlockSpec((d, FFN_TILE), lambda s: (0, jnp.maximum(s - half, 0))),
            pl.BlockSpec((FFN_TILE, d), lambda s: (jnp.maximum(s - half, 0), 0)),
        ],
        scratch_shapes=[
            pltpu.VMEM((d, FFN_TILE), BF16), pltpu.VMEM((FFN_TILE, d), BF16),
            pltpu.VMEM((n, FFN_TILE), BF16), pltpu.VMEM((n, FFN_TILE), BF16),
        ]
        + [pltpu.VMEM((half, d, FFN_TILE), BF16), pltpu.VMEM((half, FFN_TILE, d), BF16)] * 2
        + exchange_sems(2, half),
        out_shape=[
            jax.ShapeDtypeStruct((n, d), F32), jax.ShapeDtypeStruct((n, d), F32),
            jax.ShapeDtypeStruct((d, units), dtype), jax.ShapeDtypeStruct((units, d), dtype),
        ],
        compiler_params=params_of(collective_id=int(own), has_side_effects=True),
        name="ffn_kernel",
    )(n2, n2t, gl, *ins, *outs)


def norm_forward(values, norm_gain, norm_bias):
    center = values - jnp.mean(values, axis=-1, keepdims=True)
    inv_std = lax.rsqrt(jnp.mean(center * center, axis=-1, keepdims=True) + norm_eps)
    standard = center * inv_std
    return (standard * norm_gain + norm_bias, standard, inv_std)


def norm_backward(incoming, standard, inv_std, norm_gain):
    scaled = incoming * norm_gain
    value_grad = inv_std * (
        scaled
        - jnp.mean(scaled, axis=-1, keepdims=True)
        - standard * jnp.mean(scaled * standard, axis=-1, keepdims=True)
    )
    return (value_grad, jnp.sum(incoming * standard, axis=0), jnp.sum(incoming, axis=0))


def contract_rows(left, right):
    return lax.dot_general(left, right, (((0,), (0,)), ((), ())), preferred_element_type=F32)


def contract_cols(left, right):
    return lax.dot_general(left, right, (((1,), (1,)), ((), ())), preferred_element_type=F32)


SWAP = ((0, 1), (1, 0))


def over_core(values):
    return lax.ppermute(values, "core", SWAP)


def over_tensor(values):
    return lax.ppermute(values, "tensor", SWAP)


def over_pair(values, flip):
    size = lax.axis_size("pair")
    return lax.ppermute(values, "pair", [(p, p ^ flip) for p in range(size)])


def bit_groups():
    bits = log2_of(lax.axis_size("pair"))
    return [(0, 1)] + [(b, min(2, bits - b)) for b in range(1, bits, 2)]


def place_in(group):
    first, count = group
    return (lax.axis_index("pair") // (1 << first)) % (1 << count)


def flips_of(group):
    first, count = group
    return [j << first for j in range(1, 1 << count)]


def by_groups(values):
    sizes = [1 << count for _, count in bit_groups()]
    return values.reshape(*sizes, values.shape[0] // math.prod(sizes), values.shape[1])


def scatter_parts(total, i):
    me = place_in(bit_groups()[i])

    def at(place):
        return lax.dynamic_slice_in_dim(total, place, 1, i)

    return at(me), [at(me ^ j).astype(BF16) for j in range(1, total.shape[i])]


def gathered(keep, come, group, axis):
    me = place_in(group)
    parts = [keep] + come
    bit = 1
    while bit < len(parts):
        swapped = (me & bit) != 0
        parts = [jnp.where(swapped, parts[k ^ bit], parts[k]) for k in range(len(parts))]
        bit *= 2
    return jnp.concatenate(parts, axis=axis)


def ordered(index, mine, other, axis):
    first = jnp.where(index == 0, mine, other)
    second = jnp.where(index == 0, other, mine)
    return jnp.concatenate([first, second], axis=axis)


def part(values, index, axis):
    half = values.shape[axis] // 2
    return lax.dynamic_slice_in_dim(values, index * half, half, axis)


def together(*values):
    return lax.optimization_barrier(values)


class Reduction:
    def __init__(self, keep, arrivals, done=0):
        groups = range(len(bit_groups()))
        self.keep, self.flying, self.shared = keep, arrivals, None
        self.steps = [("scatter", i) for i in groups[done:]]
        self.steps += [("share", i) for i in reversed(groups)] + [("core", 0)]

    def advance(self):
        kind, i = self.steps.pop(0)
        if self.shared is not None:
            self.keep = gathered(self.keep, self.flying, bit_groups()[self.shared], self.shared)
        else:
            self.keep = sum((come.astype(F32) for come in self.flying), self.keep)
        if kind == "scatter":
            self.keep, self.boxes = scatter_parts(self.keep, i)
        else:
            self.keep = self.keep.astype(BF16)
            self.boxes, self.shared = [self.keep], i
        self.kind = kind, i

    def launch(self):
        kind, i = self.kind
        if kind == "core":
            return [over_core(self.boxes[0])]
        flips = flips_of(bit_groups()[i])
        boxes = self.boxes if kind == "scatter" else self.boxes * len(flips)
        return [over_pair(box, flip) for box, flip in zip(boxes, flips)]

    def result(self):
        return tuple(v.reshape(-1, v.shape[-1]) for v in (self.keep, self.flying[0]))


class SmallSum:
    def __init__(self, keep, arrivals):
        self.keep, self.flying = keep, arrivals
        self.steps = [flips_of(group) for group in bit_groups()] + [None]

    def advance(self):
        self.keep = sum(self.flying, self.keep)
        self.boxes, self.flips = [self.keep], self.steps.pop(0)

    def launch(self):
        if self.flips is None:
            return [over_core(self.boxes[0])]
        return [over_pair(self.boxes[0], flip) for flip in self.flips]

    def result(self):
        return self.keep, self.flying[0]


def proceed(main, *sums):
    sums = [s for s in sums if s.steps]
    if not sums:
        return main
    main, flying = together(main, [s.flying for s in sums])
    for s, come in zip(sums, flying):
        s.flying = come
        s.advance()
    main, boxes, keeps = together(main, [s.boxes for s in sums], [s.keep for s in sums])
    for s, box, keep in zip(sums, boxes, keeps):
        s.keep, s.boxes = keep, box
        s.flying = s.launch()
    return main


def shards(
    inputs, counts, ln1_gain, ln1_bias, log_dt, log_a, freq, c_real, c_imag, skip_gain,
    w_value, w_gate, ln2_gain, ln2_bias, w_in, w_out, cotangent,
):
    _, length, width = inputs.shape
    core, side = lax.axis_index("core"), lax.axis_index("tensor")
    where = jnp.stack([side, core]).astype(jnp.int32)
    used_flag = (side < counts[0]).astype(F32)
    source = inputs.reshape(length, width).astype(F32)
    gain_first, bias_first = ln1_gain.astype(F32), ln1_bias.astype(F32)
    gain_second, bias_second = ln2_gain.astype(F32), ln2_bias.astype(F32)
    table = transform_table(length)
    fwd = jnp.asarray(table.astype(ml_dtypes.bfloat16))
    inv = jnp.asarray(np.ascontiguousarray((table.T / length).astype(ml_dtypes.bfloat16)))

    packed = jnp.concatenate([log_a, freq, c_real, c_imag], axis=1)
    vectors = jnp.stack([log_dt, skip_gain])
    core_next, packed, vectors = together(core, packed, vectors)
    packed_other, vectors_other = over_tensor(packed), over_tensor(vectors)
    share = (0, min(2, log2_of(lax.axis_size("pair"))))
    place, flips = place_in(share), flips_of(share)

    def asked(weight):
        rows = weight.shape[0] // (len(flips) + 1)
        return over_tensor(lax.dynamic_slice_in_dim(weight, place * rows, rows, 0))

    def handed(rows):
        return [over_pair(rows, flip) for flip in flips]

    def joined(rows, come):
        return gathered(rows, come, share, 0)

    glu_mine = jnp.concatenate([part(w_value, core_next, 1), part(w_gate, core_next, 1)], axis=1)
    glu_rows = asked(glu_mine)
    in_rows, out_rows = asked(part(w_in, core_next, 1)), asked(part(w_out, core_next, 0))
    own, own_dt = part(packed, core, 0), part(vectors[:1], core, 1)
    own_kernel = make_kernel(own, own_dt, length)
    own_kernel, packed_other, glu_rows = together(own_kernel, packed_other, glu_rows)
    glu_come = handed(glu_rows)
    other, other_dt = part(packed_other, core, 0), part(vectors_other[:1], core, 1)
    other_kernel = make_kernel(other, other_dt, length)
    normed1_full, standard1, inv_std1 = norm_forward(source, gain_first, bias_first)
    normed1 = normed1_full.astype(BF16)
    skip = ordered(side, vectors[1:], vectors_other[1:], 1)
    other_kernel, in_rows, normed1 = together(other_kernel, in_rows, normed1)
    in_come = handed(in_rows)
    kernels = (own_kernel, over_core(own_kernel), other_kernel, over_core(other_kernel))
    conv = conv_forward(where, normed1, kernels, skip, fwd, inv)
    (mixed, act, spectrum, kernel_spectrum), glu_come, in_come, out_rows = together(
        conv, glu_come, in_come, out_rows
    )
    out_come = handed(out_rows)
    glu_direct = joined(glu_rows, glu_come)
    glu_via = over_core(glu_direct)
    cut = glu_direct.shape[1] // 2
    value_far = ordered(core, glu_direct[:, :cut], glu_via[:, :cut], 1)
    gate_far = ordered(core, glu_direct[:, cut:], glu_via[:, cut:], 1)
    value_w, gate_w = ordered(side, w_value, value_far, 1), ordered(side, w_gate, gate_far, 1)
    gain_second, bias_second = gain_second[None], bias_second[None]
    glu = glu_kernel(act, inputs.reshape(length, width), value_w, gate_w, gain_second, bias_second)
    (value_proj, gate_sig, residual, normed2, normed2_t), out_come = together(glu, out_come)
    grad_low = (used_flag * cotangent.reshape(length, width).astype(F32)).astype(BF16)
    in_direct, out_direct = joined(in_rows, in_come), joined(out_rows, out_come)
    units = in_direct.shape[1]
    far_ffn, far_normed2, there_in, there_out = ffn_kernel(
        normed2, normed2_t, grad_low, (over_core(in_direct), in_direct),
        (over_core(out_direct), out_direct), units, False,
    )
    keep, boxes = scatter_parts(by_groups(there_in), 0)
    normed2, there_out, boxes, keep = together(normed2, there_out, boxes, keep)
    out_come, in_come = over_tensor(there_out), over_pair(boxes[0], 1)
    own_sums = ffn_kernel(normed2, normed2_t, grad_low, (w_in, w_in), (w_out, w_out), units, True)
    own_sums, out_come, in_come = together(own_sums, out_come, in_come)
    own_ffn, own_normed2, here_in, here_out = own_sums
    there_in = (keep.astype(F32) + in_come.astype(F32)).astype(BF16)
    here_in, boxes = scatter_parts(by_groups(here_in), 0)
    out_sum = Reduction(by_groups(here_out), [by_groups(out_come)])
    out_sum.advance()
    own_normed2, there_in, boxes, here_in, out_sum.boxes, out_sum.keep = together(
        own_normed2, there_in, boxes, here_in, out_sum.boxes, out_sum.keep
    )
    out_sum.flying = out_sum.launch()
    in_come = over_tensor(there_in)
    back = glu_back_kernel(
        far_normed2, own_normed2, residual, grad_low, value_proj, gate_sig, act, value_w, gate_w,
        gain_second,
    )
    back, out_sum.flying, in_come = together(back, out_sum.flying, in_come)
    grad_residual, grad_act, gain_second_grad, bias_second_grad, there_glu, here_glu = back
    here_in = here_in + in_come.astype(F32)
    out_sum.advance()
    grad_act, there_glu, here_glu, out_sum.boxes, out_sum.keep, here_in, boxes = together(
        grad_act, there_glu, here_glu, out_sum.boxes, out_sum.keep, here_in, boxes
    )
    out_sum.flying = out_sum.launch()
    in_sum = Reduction(here_in, [over_pair(boxes[0], 1)], 1)
    glu_sum = Reduction(by_groups(here_glu), [by_groups(over_tensor(there_glu))])

    conv = conv_backward(
        grad_act, mixed, normed1, spectrum, kernel_spectrum, skip, fwd, inv
    )
    grad_normed1, grad_kernel, skip_grad = conv = proceed(conv, out_sum, glu_sum, in_sum)
    moments_far = make_moments(other, other_dt, grad_kernel, 0)
    moments_far, grad_kernel = proceed((moments_far, grad_kernel), out_sum, glu_sum, in_sum)
    moments = make_moments(own, own_dt, grad_kernel, 1)
    moments = proceed(moments, out_sum, glu_sum, in_sum)
    grad_normed1, moments = together(grad_normed1, moments)
    grad_source, gain_first_grad, bias_first_grad = norm_backward(
        grad_normed1, standard1, inv_std1, gain_first
    )
    input_grad = (grad_residual + grad_source).astype(BF16).reshape(inputs.shape)
    output = (used_flag * (residual + (far_ffn + own_ffn))).astype(BF16).reshape(inputs.shape)

    rows = jnp.concatenate(
        [skip_grad, gain_first_grad[None], bias_first_grad[None], gain_second_grad, bias_second_grad]
        + [jnp.zeros((3, width), F32)],
        axis=0,
    )

    def shared(at):
        half = part(rows, at, 1)
        return part(half, core, 1) + over_core(part(half, 1 - core, 1))

    small_keep = jnp.concatenate([moments, shared(side)], axis=0)
    small_box = jnp.concatenate([moments_far, shared(1 - side)], axis=0)
    small = SmallSum(small_keep, [over_tensor(small_box)])
    token = small_keep
    while out_sum.steps or in_sum.steps or glu_sum.steps or small.steps:
        token = proceed(token, out_sum, in_sum, glu_sum, small)

    def whole_of(pieces, axis):
        return ordered(core, *pieces, axis).astype(F32)

    small = ordered(core, *small.result(), 1)
    out_total = whole_of(out_sum.result(), 0)
    in_total = whole_of(in_sum.result(), 1)
    glu_mine, glu_other = glu_sum.result()
    cols = glu_mine.shape[1] // 2
    value_total = whole_of((glu_mine[:, :cols], glu_other[:, :cols]), 1)
    gate_total = whole_of((glu_mine[:, cols:], glu_other[:, cols:]), 1)

    modes = log_a.shape[1]
    top = 4 * modes
    return (
        output,
        input_grad,
        small[top + 9],
        small[top + 10],
        small[top],
        small[:modes].T,
        small[modes : 2 * modes].T,
        small[2 * modes : 3 * modes].T,
        small[3 * modes : 4 * modes].T,
        small[top + 8],
        value_total,
        gate_total,
        small[top + 11],
        small[top + 12],
        in_total,
        out_total,
    )


def solution(mesh):
    devices = mesh.devices
    cores = jax.sharding.Mesh(
        devices.reshape(devices.shape[0] // 2, 2, devices.shape[1]), ("pair", "core", "tensor")
    )
    batch, every = ("pair", "core"), ("pair", "core", "tensor")
    in_specs = (
        P(every, None, None), P(batch), P(), P(), P("tensor"), P("tensor", None), P("tensor", None),
        P("tensor", None), P("tensor", None), P("tensor"), P(None, "tensor"), P(None, "tensor"),
        P(), P(), P(None, "tensor"), P("tensor", None), P(every, None, None),
    )
    out_specs = (
        P(every, None, None), P(every, None, None), P("tensor"), P("tensor"), P("tensor"),
        P("tensor", None), P("tensor", None), P("tensor", None), P("tensor", None), P("tensor"),
        P(None, "tensor"), P(None, "tensor"), P("tensor"), P("tensor"), P(None, "tensor"),
        P("tensor", None),
    )
    return jax.shard_map(shards, mesh=cores, in_specs=in_specs, out_specs=out_specs, check_vma=False)
```

```python
import functools

import ml_dtypes
import numpy as np

import jax
import jax.numpy as jnp
from jax import lax
from jax.experimental import pallas as pl
from jax.experimental.pallas import tpu as pltpu
from jax.sharding import PartitionSpec as P

VMEM_LIMIT = 56 * 1024 * 1024
F32, BF16 = jnp.float32, jnp.bfloat16
LANES = 128
MESH = pl.DeviceIdType.MESH
KERNEL_INNER = 64
MOMENT_INNER = 32
CB = 256
DFT_ROWS = 512
TOKEN_ROWS = 256
FFN_TILE = 512
GELU_A = 0.7978845608028654
GELU_B = 0.044715
norm_eps = 1e-05


def params_of(**extra):
    return pltpu.CompilerParams(vmem_limit_bytes=VMEM_LIMIT, **extra)


class CoreExchange:
    def __init__(self, pairs, send, recv):
        self.pairs, self.send, self.recv = pairs, send, recv
        self.other = {"core": 1 - lax.axis_index("core")}

    def greet(self):
        pl.semaphore_signal(
            pltpu.get_barrier_semaphore(), inc=1, device_id=self.other, device_id_type=MESH
        )

    def meet(self):
        pl.semaphore_wait(pltpu.get_barrier_semaphore(), 1)

    def copies(self, slot):
        return [
            pltpu.make_async_remote_copy(
                src_ref=mine.at[slot], dst_ref=theirs.at[slot],
                send_sem=self.send.at[i, slot], recv_sem=self.recv.at[i, slot],
                device_id=self.other, device_id_type=MESH,
            )
            for i, (mine, theirs) in enumerate(self.pairs)
        ]

    def start(self, slot):
        for copy in self.copies(slot):
            copy.start()

    def arrived(self, slot):
        for copy in self.copies(slot):
            copy.wait_recv()

    def sent(self, slots):
        for slot in range(slots):
            for copy in self.copies(slot):
                copy.wait_send()


def exchange_sems(pairs, slots):
    return [pltpu.SemaphoreType.DMA((pairs, slots))] * 2


def transform_table(length):
    f = np.arange(length, dtype=np.int64)[:, None]
    t = np.arange(length, dtype=np.int64)[None, :]
    turn = ((4 * f + 1) * t) % (4 * length)
    angle = turn * (2.0 * np.pi / (4 * length))
    return np.concatenate([np.cos(angle), -np.sin(angle)], axis=0)


def cmul(a, b):
    return a[0] * b[0] - a[1] * b[1], a[0] * b[1] + a[1] * b[0]


def log2_of(count):
    bits = count.bit_length() - 1
    assert 1 << bits == count
    return bits


def fill_powers(base, count, out_r, out_i, tmp, scale=None):
    bits = log2_of(count)
    p = base
    for i in range(bits):
        tmp[2 * i] = p[0]
        tmp[2 * i + 1] = p[1]
        p = cmul(p, p)
    if scale is not None:
        tmp[2 * bits] = scale[0]
        tmp[2 * bits + 1] = scale[1]
    row = lax.broadcasted_iota(jnp.int32, (8, LANES), 0)

    def mode(n, carry):
        def at(i):
            return tuple(
                jnp.broadcast_to(tmp[2 * i + j, pl.ds(n, 1), :], (8, LANES)) for j in range(2)
            )

        if scale is None:
            p = (jnp.ones((8, LANES), F32), jnp.zeros((8, LANES), F32))
        else:
            p = at(bits)
        for bit in range(3):
            q = cmul(p, at(bit))
            on = (row & (1 << bit)) != 0
            p = (jnp.where(on, q[0], p[0]), jnp.where(on, q[1], p[1]))
        parts = [p]
        for bit in range(3, bits):
            w = at(bit)
            parts += [cmul(x, w) for x in parts]
        for j, part in enumerate(parts):
            out_r[n, 8 * j : 8 * j + 8, :] = part[0]
            out_i[n, 8 * j : 8 * j + 8, :] = part[1]
        return carry

    lax.fori_loop(0, base[0].shape[0], mode, 0)
    return p


def split_params(packed_ref, log_dt_ref):
    rows = packed_ref[...].T
    modes = rows.shape[0] // 4
    log_a, freq, c_real, c_imag = (rows[i * modes : (i + 1) * modes] for i in range(4))
    step = jnp.exp(log_dt_ref[...])
    rate = jnp.exp(log_a)
    decay = jnp.exp(-(step * rate))
    turn = step * freq
    return step, rate, freq, c_real, c_imag, (decay * jnp.cos(turn), decay * jnp.sin(turn))


def kernel_body(packed_ref, log_dt_ref, k_ref, zr, zi, wr, wi, tmp):
    step, _, _, c_real, c_imag, z = split_params(packed_ref, log_dt_ref)
    inner = zr.shape[1]
    outer = wr.shape[1]
    z_inner = fill_powers(z, inner, zr, zi, tmp)
    fill_powers(z_inner, outer, wr, wi, tmp, (2.0 * step * c_real, 2.0 * step * c_imag))
    modes = c_real.shape[0]
    group = 2

    def rows(i, carry):
        d = i * group
        acc = [jnp.zeros((inner, LANES), F32) for _ in range(group)]
        for n in range(modes):
            a, b = zr[n], zi[n]
            for u in range(group):
                acc[u] = acc[u] + (
                    wr[n, pl.ds(d + u, 1), :] * a - wi[n, pl.ds(d + u, 1), :] * b
                )
        for u in range(group):
            at = pl.ds(pl.multiple_of((d + u) * inner, inner), inner)
            k_ref[at, :] = acc[u].astype(BF16)
        return carry

    lax.fori_loop(0, outer // group, rows, 0)


def power_scratch(modes, inner, outer):
    return (
        [pltpu.VMEM((modes, inner, LANES), F32)] * 2
        + [pltpu.VMEM((modes, outer, LANES), F32)] * 2
        + [pltpu.VMEM((20, modes, LANES), F32)]
    )


def make_kernel(packed, log_dt, length):
    channels, modes = packed.shape[0], packed.shape[1] // 4
    return pl.pallas_call(
        kernel_body,
        grid=(channels // LANES,),
        in_specs=[
            pl.BlockSpec((LANES, 4 * modes), lambda i: (i, 0)),
            pl.BlockSpec((1, LANES), lambda i: (0, i)),
        ],
        out_specs=pl.BlockSpec((length, LANES), lambda i: (0, i)),
        out_shape=jax.ShapeDtypeStruct((length, channels), BF16),
        scratch_shapes=power_scratch(modes, KERNEL_INNER, length // KERNEL_INNER),
        compiler_params=params_of(),
        name="make_kernel",
    )(packed, log_dt)


def moments_block(packed_ref, log_dt_ref, g_ref, out_ref, zr, zi, wr, wi, tmp, sums):
    step, rate, freq, c_real, c_imag, z = split_params(packed_ref, log_dt_ref)
    inner, outer = zr.shape[1], wr.shape[1]
    z_inner = fill_powers(z, inner, zr, zi, tmp)
    fill_powers(z_inner, outer, wr, wi, tmp)
    modes = c_real.shape[0]
    pos = lax.broadcasted_iota(jnp.int32, (inner, LANES), 0).astype(F32)

    def mode(n, carry):
        zero = jnp.zeros((inner, LANES), F32)
        sr, si, tr, ti = zero, zero, zero, zero
        for d in reversed(range(outer)):
            v = g_ref[d * inner : (d + 1) * inner, :]
            sr = sr + v * wr[n, d : d + 1, :]
            si = si + v * wi[n, d : d + 1, :]
            if d > 0:
                tr = tr + sr
                ti = ti + si
        zn = (zr[n], zi[n])
        first = cmul(zn, (sr, si))
        second = cmul(zn, (pos * sr + float(inner) * tr, pos * si + float(inner) * ti))
        for j, v in enumerate(first + second):
            sums[j, pl.ds(n, 1), :] = jnp.sum(v, axis=0, keepdims=True)
        return carry

    lax.fori_loop(0, modes, mode, 0)
    scale = 2.0 * step
    real_grad, imag_grad = scale * sums[0], -scale * sums[1]
    slope_r = scale * (c_real * sums[2] - c_imag * sums[3])
    slope_i = scale * (c_real * sums[3] + c_imag * sums[2])
    log_a_grad = -step * rate * slope_r
    freq_grad = -step * slope_i
    log_dt_grad = jnp.sum(
        c_real * real_grad + c_imag * imag_grad + log_a_grad + freq * freq_grad,
        axis=0, keepdims=True,
    )
    for i, part in enumerate((log_a_grad, freq_grad, real_grad, imag_grad)):
        out_ref[i * modes : (i + 1) * modes, :] = part
    top = 4 * modes
    row = lax.broadcasted_iota(jnp.int32, (8, LANES), 0)
    out_ref[top : top + 8, :] = jnp.where(row == 0, log_dt_grad, 0.0)


def gelu_both(v):
    sq = v * v
    th = jnp.tanh(v * (GELU_A + (GELU_A * GELU_B) * sq))
    rise = 0.5 + 0.5 * th
    slope = rise + v * (0.5 - 0.5 * th * th) * (GELU_A + (3.0 * GELU_A * GELU_B) * sq)
    return v * rise, slope


def gelu(v):
    return gelu_both(v)[0]


def gelu_slope(v):
    return gelu_both(v)[1]


def dot(a, b):
    return jnp.dot(a, b, preferred_element_type=F32)


def conv_body(
    where_ref, x_ref, k0, k1, k2, k3, skip_ref, fwd_ref, inv_ref,
    mixed_ref, act_ref, xs_ref, ks_ref, k, ys,
):
    n = x_ref.shape[0]
    block = pl.program_id(0)
    here = 2 * lax.rem(block // 2 + where_ref[0], 2) + lax.rem(block + where_ref[1], 2)
    for i, ref in enumerate((k0, k1, k2, k3)):
        @pl.when(here == i)
        def _():
            k[...] = ref[...]

    x = x_ref[...]
    kernel = k[...]
    for i in range(n // DFT_ROWS):
        re = pl.ds(i * DFT_ROWS, DFT_ROWS)
        im = pl.ds(n + i * DFT_ROWS, DFT_ROWS)
        xr, xi = dot(fwd_ref[re, :], x), dot(fwd_ref[im, :], x)
        kr, ki = dot(fwd_ref[re, :], kernel), dot(fwd_ref[im, :], kernel)
        xs_ref[re, :] = xr.astype(BF16)
        xs_ref[im, :] = xi.astype(BF16)
        ks_ref[re, :] = kr.astype(BF16)
        ks_ref[im, :] = ki.astype(BF16)
        ys[re, :] = (xr * kr - xi * ki).astype(BF16)
        ys[im, :] = (xr * ki + xi * kr).astype(BF16)
    y = ys[...]
    for i in range(n // TOKEN_ROWS):
        at = pl.ds(i * TOKEN_ROWS, TOKEN_ROWS)
        mixed = dot(inv_ref[at, :], y) + skip_ref[...] * x_ref[at, :].astype(F32)
        mixed_ref[at, :] = mixed
        act_ref[at, :] = gelu(mixed).astype(BF16)


def conv_forward(where, x, kernels, skip, fwd, inv):
    n, channels = x.shape

    def col(rows):
        return pl.BlockSpec((rows, CB), lambda i, w: (0, i))

    def whole(a):
        return pl.BlockSpec(a.shape, lambda i, w: (0, 0), pipeline_mode=pl.Buffered(1))

    return pl.pallas_call(
        conv_body,
        grid_spec=pltpu.PrefetchScalarGridSpec(
            num_scalar_prefetch=1,
            grid=(channels // CB,),
            in_specs=[col(n)] + [whole(k) for k in kernels] + [col(1), whole(fwd), whole(inv)],
            out_specs=[col(n), col(n), col(2 * n), col(2 * n)],
            scratch_shapes=[pltpu.VMEM((n, CB), BF16), pltpu.VMEM((2 * n, CB), BF16)],
        ),
        out_shape=[
            jax.ShapeDtypeStruct((n, channels), F32),
            jax.ShapeDtypeStruct((n, channels), BF16),
            jax.ShapeDtypeStruct((2 * n, channels), BF16),
            jax.ShapeDtypeStruct((2 * n, channels), BF16),
        ],
        compiler_params=params_of(),
        name="conv_forward",
    )(where, x, *kernels, skip, fwd, inv)


def back_body(
    ga_ref, mixed_ref, x_ref, xs_ref, ks_ref, skip_ref, fwd_ref, inv_ref,
    gn_ref, gk_ref, sg_ref, gm, gy, ax, ak, mine, theirs, send, recv,
):
    step = pl.program_id(0)
    first = step < 2
    cores = CoreExchange([(mine, theirs)], send, recv)
    pl.when(step == 0)(cores.greet)
    n = x_ref.shape[0]
    total = jnp.zeros((1, CB), F32)
    for i in range(n // TOKEN_ROWS):
        at = pl.ds(i * TOKEN_ROWS, TOKEN_ROWS)
        v = ga_ref[at, :] * gelu_slope(mixed_ref[at, :])
        gm[at, :] = v
        gy[at, :] = v.astype(BF16)
        total += jnp.sum(v * x_ref[at, :].astype(F32), axis=0, keepdims=True)
    sg_ref[...] = total
    g = gy[...]
    for i in range(n // DFT_ROWS):
        re = pl.ds(i * DFT_ROWS, DFT_ROWS)
        im = pl.ds(n + i * DFT_ROWS, DFT_ROWS)
        gr, gi = dot(fwd_ref[re, :], g), dot(fwd_ref[im, :], g)
        for src, dst in ((ks_ref, ax), (xs_ref, ak)):
            a, b = src[re, :].astype(F32), src[im, :].astype(F32)
            dst[re, :] = (a * gr + b * gi).astype(BF16)
            dst[im, :] = (a * gi - b * gr).astype(BF16)
    yx = ax[...]
    yk = ak[...]
    for i in range(n // TOKEN_ROWS):
        at = pl.ds(i * TOKEN_ROWS, TOKEN_ROWS)
        gk_ref[0, at, :] = dot(inv_ref[at, :], yk)
        gn_ref[at, :] = dot(inv_ref[at, :], yx) + skip_ref[...] * gm[at, :]
    pl.when(step == 0)(cores.meet)

    @pl.when(first)
    def _():
        mine[step] = gk_ref[0]
        cores.start(step)

    @pl.when(jnp.logical_not(first))
    def _():
        cores.arrived(step - 2)
        gk_ref[0] = gk_ref[0] + theirs[step - 2]

    @pl.when(step == 3)
    def _():
        cores.sent(2)


def conv_backward(ga, mixed, x, xs, ks, skip, fwd, inv):
    n, channels = x.shape

    def block(i):
        side = lax.rem(lax.axis_index("tensor") + 1 + i, 2)
        half = lax.rem(lax.axis_index("core") + 1 + i // 2, 2)
        return 2 * side + half

    def col(rows):
        return pl.BlockSpec((rows, CB), lambda i: (0, block(i)))

    def whole(a):
        return pl.BlockSpec(a.shape, lambda i: (0, 0), pipeline_mode=pl.Buffered(1))

    return pl.pallas_call(
        back_body,
        grid=(channels // CB,),
        in_specs=[col(n), col(n), col(n), col(2 * n), col(2 * n), col(1), whole(fwd), whole(inv)],
        out_specs=[col(n), pl.BlockSpec((1, n, CB), lambda i: (jnp.maximum(i - 2, 0), 0, 0)), col(1)],
        out_shape=[
            jax.ShapeDtypeStruct((n, channels), F32),
            jax.ShapeDtypeStruct((2, n, CB), F32),
            jax.ShapeDtypeStruct((1, channels), F32),
        ],
        scratch_shapes=[pltpu.VMEM((n, CB), F32), pltpu.VMEM((n, CB), BF16)]
        + [pltpu.VMEM((2 * n, CB), BF16)] * 2
        + [pltpu.VMEM((2, n, CB), F32)] * 2
        + exchange_sems(1, 2),
        compiler_params=params_of(collective_id=3, has_side_effects=True),
        name="conv_backward",
    )(ga, mixed, x, xs, ks, skip, fwd, inv)


def glu_body(
    act, source, value_w, gate_w, gain, bias, value_ref, sig_ref, residual_ref, n2_ref, n2t_ref
):
    value = dot(act[...], value_w[...])
    sig = 1.0 / (1.0 + jnp.exp(-dot(act[...], gate_w[...])))
    value_ref[...] = value.astype(BF16)
    sig_ref[...] = sig.astype(BF16)
    residual = source[...].astype(F32) + (value * sig).astype(BF16).astype(F32)
    residual_ref[...] = residual
    n2 = norm_forward(residual, gain[...], bias[...])[0].astype(BF16)
    n2_ref[...] = n2
    n2t_ref[...] = n2.T


def glu_kernel(act, source, value_w, gate_w, gain, bias):
    n, d = act.shape
    rows = pl.BlockSpec((TOKEN_ROWS, d), lambda i: (i, 0))

    def whole(a):
        return pl.BlockSpec(a.shape, lambda i: (0, 0), pipeline_mode=pl.Buffered(1))

    return pl.pallas_call(
        glu_body,
        grid=(n // TOKEN_ROWS,),
        in_specs=[rows, rows, whole(value_w), whole(gate_w), whole(gain), whole(bias)],
        out_specs=[rows] * 4 + [pl.BlockSpec((d, TOKEN_ROWS), lambda i: (0, i))],
        out_shape=[
            jax.ShapeDtypeStruct((n, d), BF16), jax.ShapeDtypeStruct((n, d), BF16),
            jax.ShapeDtypeStruct((n, d), F32), jax.ShapeDtypeStruct((n, d), BF16),
            jax.ShapeDtypeStruct((d, n), BF16),
        ],
        compiler_params=params_of(),
        name="glu_kernel",
    )(act, source, value_w, gate_w, gain, bias)


def glu_back_body(
    g_far, g_own, residual, cot, value, sig, act, value_w, gate_w, gain,
    resid_ref, ga_ref, gain_ref, bias_ref, there_ref, here_ref, gv, gt, mine, theirs, send, recv,
):
    step = pl.program_id(0)
    cores = CoreExchange([(mine, theirs)], send, recv)
    pl.when(step == 0)(cores.greet)
    chunks = act.shape[0] // TOKEN_ROWS
    width = gv.shape[2]

    @pl.when(step < chunks)
    def _():
        standard, inv_std = norm_forward(residual[...], 1.0, 0.0)[1:]
        part, gain_grad, bias_grad = norm_backward(
            g_far[...] + g_own[...], standard, inv_std, gain[...]
        )
        new = step == 0
        gain_ref[...] = jnp.where(new, 0.0, gain_ref[...]) + gain_grad[None]
        bias_ref[...] = jnp.where(new, 0.0, bias_ref[...]) + bias_grad[None]
        resid = cot[...].astype(F32) + part
        resid_ref[...] = resid
        grad = resid.astype(BF16).astype(F32)
        gate = sig[...].astype(F32)
        grad_value = (grad * gate).astype(BF16)
        grad_gate = (grad * value[...].astype(F32) * gate * (1.0 - gate)).astype(BF16)
        ga_ref[...] = contract_cols(grad_value, value_w[...]) + contract_cols(grad_gate, gate_w[...])
        at = pl.ds(pl.multiple_of(step * TOKEN_ROWS, TOKEN_ROWS), TOKEN_ROWS)
        for i in range(gv.shape[0]):
            gv[i, at, :] = grad_value[:, i * width : (i + 1) * width]
            gt[i, at, :] = grad_gate[:, i * width : (i + 1) * width]

    @pl.when(step >= chunks)
    def _():
        j = step - chunks
        side = lax.rem(lax.axis_index("tensor") + 1 + j, 2)
        half = lax.rem(lax.axis_index("core") + 1 + j // 2, 2)
        block = 2 * side + half
        grads = [contract_rows(act[...], gv[block]), contract_rows(act[...], gt[block])]
        pl.when(j == 0)(cores.meet)

        @pl.when(j < 2)
        def _():
            for i, g in enumerate(grads):
                mine[j, :, i * width : (i + 1) * width] = g.astype(BF16)
            cores.start(j)

        @pl.when(j == 2)
        def _():
            cores.arrived(0)
            for i, g in enumerate(grads):
                at = pl.ds(i * width, width)
                there_ref[:, at] = (g + theirs[0, :, at].astype(F32)).astype(BF16)

        @pl.when(j == 3)
        def _():
            cores.arrived(1)
            for i, g in enumerate(grads):
                at = pl.ds(i * width, width)
                here_ref[:, at] = g + theirs[1, :, at].astype(F32)
            cores.sent(2)


def glu_back_kernel(g_far, g_own, residual, cot, value, sig, act, value_w, gate_w, gain):
    n, d = act.shape
    chunks = n // TOKEN_ROWS
    width = d // 4

    def whole(a):
        return pl.BlockSpec(a.shape, lambda i: (0, 0), pipeline_mode=pl.Buffered(1))

    rows = pl.BlockSpec((TOKEN_ROWS, d), lambda i: (jnp.minimum(i, chunks - 1), 0))
    vector = pl.BlockSpec((1, d), lambda i: (0, 0))
    weight = pl.BlockSpec((d, 2 * width), lambda i: (0, 0))
    return pl.pallas_call(
        glu_back_body,
        grid=(chunks + 4,),
        in_specs=[rows] * 6 + [whole(act), whole(value_w), whole(gate_w), whole(gain)],
        out_specs=[rows, rows, vector, vector, weight, weight],
        scratch_shapes=[pltpu.VMEM((4, n, width), BF16)] * 2
        + [pltpu.VMEM((2, d, 2 * width), BF16)] * 2
        + exchange_sems(1, 2),
        out_shape=[
            jax.ShapeDtypeStruct((n, d), F32), jax.ShapeDtypeStruct((n, d), F32),
            jax.ShapeDtypeStruct((1, d), F32), jax.ShapeDtypeStruct((1, d), F32),
            jax.ShapeDtypeStruct((d, 2 * width), BF16), jax.ShapeDtypeStruct((d, 2 * width), F32),
        ],
        compiler_params=params_of(collective_id=2, has_side_effects=True),
        name="glu_back_kernel",
    )(g_far, g_own, residual, cot, value, sig, act, value_w, gate_w, gain)


def ffn_body(
    n2, n2t, gl, ia, ib, oa, ob, ffn, gn2, in_ref, out_ref,
    wi, wo, h, gp, in_mine, out_mine, in_theirs, out_theirs, send, recv,
):
    step, half = pl.program_id(0), in_mine.shape[0]
    first = step < half
    cores = CoreExchange([(in_mine, in_theirs), (out_mine, out_theirs)], send, recv)
    pl.when(step == 0)(cores.greet)

    @pl.when(first)
    def _():
        wi[...] = ia[...]
        wo[...] = oa[...]

    @pl.when(jnp.logical_not(first))
    def _():
        wi[...] = ib[...]
        wo[...] = ob[...]

    @pl.when(step == 0)
    def _():
        ffn[...] = jnp.zeros_like(ffn)
        gn2[...] = jnp.zeros_like(gn2)

    w1, w2 = wi[...], wo[...]
    for r in range(n2.shape[0] // TOKEN_ROWS):
        at = pl.ds(r * TOKEN_ROWS, TOKEN_ROWS)
        act, slope = gelu_both(dot(n2[at, :], w1))
        hidden = act.astype(BF16)
        grad_pre = (contract_cols(gl[at, :], w2) * slope).astype(BF16)
        h[at, :] = hidden
        gp[at, :] = grad_pre
        ffn[at, :] += dot(hidden, w2)
        gn2[at, :] += contract_cols(grad_pre, w1)
    out_grad = contract_rows(h[...], gl[...])
    in_grad = dot(n2t[...], gp[...])

    pl.when(step == 0)(cores.meet)

    @pl.when(first)
    def _():
        in_mine[step] = in_grad.astype(BF16)
        out_mine[step] = out_grad.astype(BF16)
        cores.start(step)

    @pl.when(jnp.logical_not(first))
    def _():
        cores.arrived(step - half)
        in_ref[...] = (in_grad + in_theirs[step - half].astype(F32)).astype(in_ref.dtype)
        out_ref[...] = (out_grad + out_theirs[step - half].astype(F32)).astype(out_ref.dtype)

    @pl.when(step == 2 * half - 1)
    def _():
        cores.sent(half)


def ffn_kernel(n2, n2t, gl, ins, outs, units, own):
    n, d = n2.shape
    half = units // FFN_TILE

    def whole(a):
        return pl.BlockSpec(a.shape, lambda s: (0, 0), pipeline_mode=pl.Buffered(1))

    def fst(s):
        at = jnp.minimum(s, half - 1)
        return at + (1 - lax.axis_index("core")) * half if own else at

    def snd(s):
        at = jnp.maximum(s - half, 0)
        return at + lax.axis_index("core") * half if own else at

    total = pl.BlockSpec((n, d), lambda s: (0, 0))
    dtype = F32 if own else BF16
    return pl.pallas_call(
        ffn_body,
        grid=(2 * half,),
        in_specs=[
            whole(n2), whole(n2t), whole(gl),
            pl.BlockSpec((d, FFN_TILE), lambda s: (0, fst(s))),
            pl.BlockSpec((d, FFN_TILE), lambda s: (0, snd(s))),
            pl.BlockSpec((FFN_TILE, d), lambda s: (fst(s), 0)),
            pl.BlockSpec((FFN_TILE, d), lambda s: (snd(s), 0)),
        ],
        out_specs=[
            total, total,
            pl.BlockSpec((d, FFN_TILE), lambda s: (0, jnp.maximum(s - half, 0))),
            pl.BlockSpec((FFN_TILE, d), lambda s: (jnp.maximum(s - half, 0), 0)),
        ],
        scratch_shapes=[
            pltpu.VMEM((d, FFN_TILE), BF16), pltpu.VMEM((FFN_TILE, d), BF16),
            pltpu.VMEM((n, FFN_TILE), BF16), pltpu.VMEM((n, FFN_TILE), BF16),
        ]
        + [pltpu.VMEM((half, d, FFN_TILE), BF16), pltpu.VMEM((half, FFN_TILE, d), BF16)] * 2
        + exchange_sems(2, half),
        out_shape=[
            jax.ShapeDtypeStruct((n, d), F32), jax.ShapeDtypeStruct((n, d), F32),
            jax.ShapeDtypeStruct((d, units), dtype), jax.ShapeDtypeStruct((units, d), dtype),
        ],
        compiler_params=params_of(collective_id=int(own), has_side_effects=True),
        name="ffn_kernel",
    )(n2, n2t, gl, *ins, *outs)


def norm_forward(values, norm_gain, norm_bias):
    center = values - jnp.mean(values, axis=-1, keepdims=True)
    inv_std = lax.rsqrt(jnp.mean(center * center, axis=-1, keepdims=True) + norm_eps)
    standard = center * inv_std
    return (standard * norm_gain + norm_bias, standard, inv_std)


def norm_backward(incoming, standard, inv_std, norm_gain):
    scaled = incoming * norm_gain
    value_grad = inv_std * (
        scaled
        - jnp.mean(scaled, axis=-1, keepdims=True)
        - standard * jnp.mean(scaled * standard, axis=-1, keepdims=True)
    )
    return (value_grad, jnp.sum(incoming * standard, axis=0), jnp.sum(incoming, axis=0))


def contract_rows(left, right):
    return lax.dot_general(left, right, (((0,), (0,)), ((), ())), preferred_element_type=F32)


def contract_cols(left, right):
    return lax.dot_general(left, right, (((1,), (1,)), ((), ())), preferred_element_type=F32)


class Posts:
    def __init__(self, bits, send, recv):
        self.bits, self.send, self.recv, self.used = bits, send, recv, 0
        self.place = lax.axis_index("pair")
        self.started = []

    def bit(self, b):
        return lax.rem(lax.div(self.place, 1 << b), 2)

    def device(self, link):
        if isinstance(link, str):
            return {link: 1 - lax.axis_index(link)}
        return {"pair": self.place + (1 - 2 * self.bit(link)) * (1 << link)}

    def block(self, flipped):
        at = 0
        for b in range(self.bits):
            here = 1 - self.bit(b) if flipped >> b & 1 else self.bit(b)
            at = at + here * (1 << (self.bits - 1 if b == 0 else b - 1))
        return at

    def slot(self):
        self.used += 1
        return self.used - 1

    def copy(self, src, dst, slot, link):
        return pltpu.make_async_remote_copy(
            src_ref=src, dst_ref=dst, send_sem=self.send.at[slot], recv_sem=self.recv.at[slot],
            device_id=self.device(link), device_id_type=MESH,
        )

    def post(self, src, dst, slot, link):
        copy = self.copy(src, dst, slot, link)
        copy.start()
        self.started.append(copy)

    def await_(self, dst, slot, link):
        self.copy(dst, dst, slot, link).wait_recv()

    def greet(self):
        links = list(range(self.bits)) + ["core", "tensor"]
        barrier = pltpu.get_barrier_semaphore()
        for link in links:
            pl.semaphore_signal(barrier, inc=1, device_id=self.device(link), device_id_type=MESH)
        pl.semaphore_wait(barrier, len(links))

    def finish(self):
        for copy in self.started:
            copy.wait_send()


def scatter_steps(posts, acc, bits, order, boxes, come):
    def at(known, flipped):
        place = 0
        for i, b in enumerate(bits):
            here = posts.bit(b)
            if b in known:
                bit = 1 - here if known[b] else here
            else:
                bit = flipped >> i & 1
            place = place + bit * (1 << i)
        return place

    done = {}
    used = 0
    for n, b in enumerate(order):
        rest = [bits.index(i) for i in order[n + 1 :]]
        combos = [sum((c >> k & 1) << i for k, i in enumerate(rest)) for c in range(1 << len(rest))]
        slots = []
        for c, combo in enumerate(combos):
            slot = posts.slot()
            boxes[used + c] = acc[at({**done, b: True}, combo)].astype(BF16)
            posts.post(boxes.at[used + c], come.at[used + c], slot, b)
            slots.append(slot)
        yield
        done[b] = False
        for c, combo in enumerate(combos):
            posts.await_(come.at[used + c], slots[c], b)
            keep = at(done, combo)
            acc[keep] = acc[keep] + come[used + c].astype(F32)
        used += len(combos)
    posts.result = at(done, 0)


def gather_steps(posts, own, whole, local):
    core = lax.axis_index("core")
    count = 1 << posts.bits
    slots = {(rel, link): posts.slot() for rel in range(count) for link in ("bit", "core")}
    first = pltpu.make_async_copy(own, whole.at[core, posts.block(0)], local)
    first.start()

    def pass_on(src, rel, bits):
        dst = whole.at[core, posts.block(rel)]
        for b in bits:
            posts.post(src, dst, slots[rel ^ (1 << b), "bit"], b)
        posts.post(src, dst, slots[rel, "core"], "core")

    pass_on(own, 0, reversed(range(posts.bits)))
    for b in reversed(range(posts.bits)):
        higher = [sum((c >> k & 1) << (b + 1 + k) for k in range(posts.bits - 1 - b)) for c in range(1 << (posts.bits - 1 - b))]
        for rest in higher:
            yield
            rel = rest | 1 << b
            block = whole.at[core, posts.block(rel)]
            posts.await_(block, slots[rel, "bit"], b)
            pass_on(block, rel, reversed(range(b)))
    yield
    first.wait()
    for rel in range(count):
        posts.await_(whole.at[1 - core, posts.block(rel)], slots[rel, "core"], "core")


def finish_body(
    in_keep, in_come, out_keep, out_come, glu_keep, glu_come, packed, log_dt, gk, rows_mine,
    rows_other, in_all, out_all, glu_all, small_all,
    zr, zi, wr, wi, tmp, sums, moments, rows_come, in_own, out_own, glu_own, out_acc, glu_acc,
    out_boxes, out_got, glu_boxes, glu_got, small, small_far, small_got, local, send, recv, *, bits
):
    posts = Posts(bits, send, recv)
    posts.greet()
    near, far = list(range(1, bits)), list(range(2, bits))

    def in_steps():
        in_own[...] = sum((come[...].astype(F32) for come in in_come), in_keep[...]).astype(BF16)
        yield from gather_steps(posts, in_own, in_all, local.at[0])

    def out_steps():
        out_acc[...] = out_keep[...] + out_come[...].astype(F32)
        yield from scatter_steps(posts, out_acc, far, far, out_boxes, out_got)
        out_own[...] = out_acc[posts.result].astype(BF16)
        yield from gather_steps(posts, out_own, out_all, local.at[1])

    def glu_steps():
        glu_acc[...] = glu_keep[...] + glu_come[...].astype(F32)
        yield from scatter_steps(posts, glu_acc, near + [0], [0] + near, glu_boxes, glu_got)
        glu_own[...] = glu_acc[posts.result].astype(BF16)
        yield from gather_steps(posts, glu_own, glu_all, local.at[2])

    def small_steps():
        slot = posts.slot()
        posts.post(rows_other, rows_come, slot, "core")
        yield
        posts.await_(rows_come, slot, "core")
        top = moments.shape[1]
        for j, ref in ((0, small_far), (1, small)):
            ref[:top, :] = moments[j]
            ref[top:, :] = rows_mine[j] + rows_come[j]
        slot = posts.slot()
        posts.post(small_far, small_got.at[0], slot, "tensor")
        yield
        posts.await_(small_got.at[0], slot, "tensor")
        small[...] = small[...] + small_got[0]
        for b in range(bits):
            slot = posts.slot()
            small_all[b] = small[...]
            posts.post(small_all.at[b], small_got.at[1 + b], slot, b)
            yield
            posts.await_(small_got.at[1 + b], slot, b)
            small[...] = small[...] + small_got[1 + b]
        slot = posts.slot()
        small_all[bits] = small[...]
        posts.post(small_all.at[bits], small_got.at[1 + bits], slot, "core")
        yield
        posts.await_(small_got.at[1 + bits], slot, "core")
        small_all[bits + 1] = small_got[1 + bits]

    def block(j, i):
        at = pl.ds(i * LANES, LANES)
        moments_block(
            packed.at[j, at, :], log_dt.at[j, :, at], gk.at[j, :, at], moments.at[j, :, at],
            zr, zi, wr, wi, tmp, sums,
        )

    work = [(j, i) for j in range(2) for i in range(packed.shape[1] // LANES)]
    flows = [in_steps(), glu_steps(), out_steps()]
    late = small_steps()
    for flow in flows:
        next(flow, None)
    next(late)
    while flows or late is not None:
        if work:
            block(*work.pop(0))
        flows = [flow for flow in flows if next(flow, posts) is not posts]
        if not work and late is not None and next(late, posts) is posts:
            late = None
    posts.finish()


def finish_kernel(in_keep, in_come, out_keep, out_come, glu_keep, glu_come, packed, log_dt, gk, rows_mine, rows_other):
    bits = log2_of(lax.axis_size("pair"))
    blocks = 1 << bits
    half, modes = packed.shape[1], packed.shape[2] // 4
    length = gk.shape[1]
    rows, d = in_keep.shape
    cols = glu_keep.shape[2]
    kept = len(range(2, bits))
    small_rows = 4 * modes + 8 + rows_mine.shape[1]
    vmem = pl.BlockSpec(memory_space=pltpu.VMEM)
    hbm = pl.BlockSpec(memory_space=pl.ANY)
    copies = 3 * 2 * blocks + (1 << kept) + blocks + bits + 8
    operands = (
        in_keep, in_come, out_keep, out_come, glu_keep, glu_come, packed, log_dt, gk, rows_mine, rows_other
    )
    small = pltpu.VMEM((small_rows, half), F32)
    return pl.pallas_call(
        functools.partial(finish_body, bits=bits),
        in_specs=jax.tree.map(lambda _: vmem, operands),
        out_specs=[hbm, hbm, hbm, vmem],
        out_shape=[
            jax.ShapeDtypeStruct((2, blocks, rows, d), BF16),
            jax.ShapeDtypeStruct((2, blocks, rows, d), BF16),
            jax.ShapeDtypeStruct((2, blocks, rows, cols), BF16),
            jax.ShapeDtypeStruct((bits + 2, small_rows, half), F32),
        ],
        scratch_shapes=power_scratch(modes, MOMENT_INNER, length // MOMENT_INNER)
        + [
            pltpu.VMEM((4, modes, LANES), F32),
            pltpu.VMEM((2, 4 * modes + 8, half), F32),
            pltpu.VMEM(rows_mine.shape, F32),
            pltpu.VMEM((rows, d), BF16), pltpu.VMEM((rows, d), BF16), pltpu.VMEM((rows, cols), BF16),
            pltpu.VMEM(out_keep.shape, F32), pltpu.VMEM(glu_keep.shape, F32),
        ]
        + [pltpu.VMEM((max((1 << kept) - 1, 1), rows, d), BF16)] * 2
        + [pltpu.VMEM((blocks - 1, rows, cols), BF16)] * 2
        + [small, small, pltpu.VMEM((bits + 2, small_rows, half), F32)]
        + [pltpu.SemaphoreType.DMA((3,))]
        + [pltpu.SemaphoreType.DMA((copies,))] * 2,
        compiler_params=params_of(collective_id=4, has_side_effects=True),
        name="finish_kernel",
    )(*operands)


SWAP = ((0, 1), (1, 0))


def over_core(values):
    return lax.ppermute(values, "core", SWAP)


def over_tensor(values):
    return lax.ppermute(values, "tensor", SWAP)


def over_pair(values, flip):
    size = lax.axis_size("pair")
    return lax.ppermute(values, "pair", [(p, p ^ flip) for p in range(size)])


def place_in(group):
    first, count = group
    return (lax.axis_index("pair") // (1 << first)) % (1 << count)


def flips_of(group):
    first, count = group
    return [j << first for j in range(1, 1 << count)]


def pair_bits():
    return log2_of(lax.axis_size("pair"))


def by_bits(values):
    bits = pair_bits()
    return values.reshape(*[2] * bits, values.shape[0] >> bits, values.shape[1])


def split_over(total, bit):
    axis = 0 if bit == 0 else pair_bits() - bit
    return part(total, place_in((bit, 1)), axis), part(total, 1 - place_in((bit, 1)), axis).astype(BF16)


def gathered(keep, come, group, axis):
    me = place_in(group)
    parts = [keep] + come
    bit = 1
    while bit < len(parts):
        swapped = (me & bit) != 0
        parts = [jnp.where(swapped, parts[k ^ bit], parts[k]) for k in range(len(parts))]
        bit *= 2
    return jnp.concatenate(parts, axis=axis)


def ordered(index, mine, other, axis):
    first = jnp.where(index == 0, mine, other)
    second = jnp.where(index == 0, other, mine)
    return jnp.concatenate([first, second], axis=axis)


def part(values, index, axis):
    half = values.shape[axis] // 2
    return lax.dynamic_slice_in_dim(values, index * half, half, axis)


def together(*values):
    return lax.optimization_barrier(values)


def shards(
    inputs, counts, ln1_gain, ln1_bias, log_dt, log_a, freq, c_real, c_imag, skip_gain,
    w_value, w_gate, ln2_gain, ln2_bias, w_in, w_out, cotangent,
):
    _, length, width = inputs.shape
    core, side = lax.axis_index("core"), lax.axis_index("tensor")
    where = jnp.stack([side, core]).astype(jnp.int32)
    used_flag = (side < counts[0]).astype(F32)
    source = inputs.reshape(length, width).astype(F32)
    gain_first, bias_first = ln1_gain.astype(F32), ln1_bias.astype(F32)
    gain_second, bias_second = ln2_gain.astype(F32), ln2_bias.astype(F32)
    table = transform_table(length)
    fwd = jnp.asarray(table.astype(ml_dtypes.bfloat16))
    inv = jnp.asarray(np.ascontiguousarray((table.T / length).astype(ml_dtypes.bfloat16)))

    packed = jnp.concatenate([log_a, freq, c_real, c_imag], axis=1)
    vectors = jnp.stack([log_dt, skip_gain])
    core_next, packed, vectors = together(core, packed, vectors)
    packed_other, vectors_other = over_tensor(packed), over_tensor(vectors)
    share = (0, min(2, pair_bits()))
    place, flips = place_in(share), flips_of(share)

    def asked(weight):
        rows = weight.shape[0] // (len(flips) + 1)
        return over_tensor(lax.dynamic_slice_in_dim(weight, place * rows, rows, 0))

    def handed(rows):
        return [over_pair(rows, flip) for flip in flips]

    def joined(rows, come):
        return gathered(rows, come, share, 0)

    glu_mine = jnp.concatenate([part(w_value, core_next, 1), part(w_gate, core_next, 1)], axis=1)
    glu_rows = asked(glu_mine)
    in_rows, out_rows = asked(part(w_in, core_next, 1)), asked(part(w_out, core_next, 0))
    own, own_dt = part(packed, core, 0), part(vectors[:1], core, 1)
    own_kernel = make_kernel(own, own_dt, length)
    own_kernel, packed_other, glu_rows = together(own_kernel, packed_other, glu_rows)
    glu_come = handed(glu_rows)
    other, other_dt = part(packed_other, core, 0), part(vectors_other[:1], core, 1)
    other_kernel = make_kernel(other, other_dt, length)
    normed1_full, standard1, inv_std1 = norm_forward(source, gain_first, bias_first)
    normed1 = normed1_full.astype(BF16)
    skip = ordered(side, vectors[1:], vectors_other[1:], 1)
    other_kernel, in_rows, normed1 = together(other_kernel, in_rows, normed1)
    in_come = handed(in_rows)
    kernels = (own_kernel, over_core(own_kernel), other_kernel, over_core(other_kernel))
    conv = conv_forward(where, normed1, kernels, skip, fwd, inv)
    (mixed, act, spectrum, kernel_spectrum), glu_come, in_come, out_rows = together(
        conv, glu_come, in_come, out_rows
    )
    out_come = handed(out_rows)
    glu_direct = joined(glu_rows, glu_come)
    glu_via = over_core(glu_direct)
    cut = glu_direct.shape[1] // 2
    value_far = ordered(core, glu_direct[:, :cut], glu_via[:, :cut], 1)
    gate_far = ordered(core, glu_direct[:, cut:], glu_via[:, cut:], 1)
    value_w, gate_w = ordered(side, w_value, value_far, 1), ordered(side, w_gate, gate_far, 1)
    gain_second, bias_second = gain_second[None], bias_second[None]
    glu = glu_kernel(act, inputs.reshape(length, width), value_w, gate_w, gain_second, bias_second)
    (value_proj, gate_sig, residual, normed2, normed2_t), out_come = together(glu, out_come)
    grad_low = (used_flag * cotangent.reshape(length, width).astype(F32)).astype(BF16)
    in_direct, out_direct = joined(in_rows, in_come), joined(out_rows, out_come)
    units = in_direct.shape[1]
    far_ffn, far_normed2, there_in, there_out = ffn_kernel(
        normed2, normed2_t, grad_low, (over_core(in_direct), in_direct),
        (over_core(out_direct), out_direct), units, False,
    )
    keep, box = split_over(by_bits(there_in), 0)
    normed2, there_out, box, keep = together(normed2, there_out, box, keep)
    out_come, in_come = over_tensor(there_out), over_pair(box, 1)
    own_sums = ffn_kernel(normed2, normed2_t, grad_low, (w_in, w_in), (w_out, w_out), units, True)
    own_sums, out_come, in_come = together(own_sums, out_come, in_come)
    own_ffn, own_normed2, here_in, here_out = own_sums
    there_in = (keep.astype(F32) + in_come.astype(F32)).astype(BF16)
    here_in, in_box = split_over(by_bits(here_in), 0)
    here_out, out_box = split_over(by_bits(here_out) + by_bits(out_come).astype(F32), 1)
    own_normed2, there_in, in_box, out_box, here_in, here_out = together(
        own_normed2, there_in, in_box, out_box, here_in, here_out
    )
    in_come = [over_tensor(there_in), over_pair(in_box, 1)]
    out_come = over_pair(out_box, 2)
    back = glu_back_kernel(
        far_normed2, own_normed2, residual, grad_low, value_proj, gate_sig, act, value_w, gate_w,
        gain_second,
    )
    back, out_come, in_come = together(back, out_come, in_come)
    grad_residual, grad_act, gain_second_grad, bias_second_grad, there_glu, here_glu = back
    here_out, out_box = split_over(here_out + out_come.astype(F32), 0)
    here_in = sum((come.astype(F32) for come in in_come), here_in)
    here_in = here_in.reshape(-1, *here_in.shape[-2:])
    others = (1, pair_bits() - 1)
    in_flips, place = flips_of(others), place_in(others)

    def in_part(at):
        return lax.dynamic_index_in_dim(here_in, at, 0, False)

    in_boxes = [in_part(place ^ (flip >> 1)).astype(BF16) for flip in in_flips]
    here_in = in_part(place)
    grad_act, there_glu, out_box, in_boxes, here_out, here_in = together(
        grad_act, there_glu, out_box, in_boxes, here_out, here_in
    )
    glu_come, out_come = over_tensor(there_glu), over_pair(out_box, 1)
    in_come = [over_pair(box, flip) for box, flip in zip(in_boxes, in_flips)]
    conv = conv_backward(
        grad_act, mixed, normed1, spectrum, kernel_spectrum, skip, fwd, inv
    )
    conv, glu_come, out_come, in_come = together(conv, glu_come, out_come, in_come)
    grad_normed1, grad_kernel, skip_grad = conv
    grad_source, gain_first_grad, bias_first_grad = norm_backward(
        grad_normed1, standard1, inv_std1, gain_first
    )
    input_grad = (grad_residual + grad_source).astype(BF16).reshape(inputs.shape)
    output = (used_flag * (residual + (far_ffn + own_ffn))).astype(BF16).reshape(inputs.shape)

    rows = jnp.concatenate(
        [skip_grad, gain_first_grad[None], bias_first_grad[None], gain_second_grad, bias_second_grad]
        + [jnp.zeros((3, width), F32)],
        axis=0,
    )

    def quarter(far, theirs):
        return part(part(rows, (side + far) % 2, 1), (core + theirs) % 2, 1)

    in_all, out_all, glu_all, small = finish_kernel(
        here_in, in_come, here_out.reshape(-1, *here_out.shape[-2:]),
        out_come.reshape(-1, *out_come.shape[-2:]),
        here_glu.reshape(2 * len(in_flips) + 2, -1, here_glu.shape[1]),
        glu_come.reshape(2 * len(in_flips) + 2, -1, glu_come.shape[1]),
        jnp.stack([other, own]), jnp.stack([other_dt, own_dt]), grad_kernel,
        jnp.stack([quarter(1, 0), quarter(0, 0)]), jnp.stack([quarter(1, 1), quarter(0, 1)]),
    )
    small = ordered(core, small[-2], small[-1], 1)
    out_total = out_all.reshape(-1, width).astype(F32)
    in_all = in_all.reshape(2, width, -1)
    in_total = jnp.concatenate([in_all[0], in_all[1]], axis=1).astype(F32)
    glu_all = glu_all.reshape(2, width, -1)
    cut = glu_all.shape[2] // 2
    value_total = jnp.concatenate([glu_all[0, :, :cut], glu_all[1, :, :cut]], axis=1).astype(F32)
    gate_total = jnp.concatenate([glu_all[0, :, cut:], glu_all[1, :, cut:]], axis=1).astype(F32)

    modes = log_a.shape[1]
    top = 4 * modes
    return (
        output,
        input_grad,
        small[top + 9],
        small[top + 10],
        small[top],
        small[:modes].T,
        small[modes : 2 * modes].T,
        small[2 * modes : 3 * modes].T,
        small[3 * modes : 4 * modes].T,
        small[top + 8],
        value_total,
        gate_total,
        small[top + 11],
        small[top + 12],
        in_total,
        out_total,
    )


def solution(mesh):
    devices = mesh.devices
    cores = jax.sharding.Mesh(
        devices.reshape(devices.shape[0] // 2, 2, devices.shape[1]), ("pair", "core", "tensor")
    )
    batch, every = ("pair", "core"), ("pair", "core", "tensor")
    in_specs = (
        P(every, None, None), P(batch), P(), P(), P("tensor"), P("tensor", None), P("tensor", None),
        P("tensor", None), P("tensor", None), P("tensor"), P(None, "tensor"), P(None, "tensor"),
        P(), P(), P(None, "tensor"), P("tensor", None), P(every, None, None),
    )
    out_specs = (
        P(every, None, None), P(every, None, None), P("tensor"), P("tensor"), P("tensor"),
        P("tensor", None), P("tensor", None), P("tensor", None), P("tensor", None), P("tensor"),
        P(None, "tensor"), P(None, "tensor"), P("tensor"), P("tensor"), P(None, "tensor"),
        P("tensor", None),
    )
    return jax.shard_map(shards, mesh=cores, in_specs=in_specs, out_specs=out_specs, check_vma=False)
```

```python
import functools

import ml_dtypes
import numpy as np

import jax
import jax.numpy as jnp
from jax import lax
from jax.experimental import pallas as pl
from jax.experimental.pallas import tpu as pltpu
from jax.sharding import PartitionSpec as P

VMEM_LIMIT = 60 * 1024 * 1024
F32, BF16 = jnp.float32, jnp.bfloat16
LANES = 128
MESH = pl.DeviceIdType.MESH
KERNEL_INNER = 64
MOMENT_INNER = 32
CB = 256
DFT_ROWS = 512
TOKEN_ROWS = 256
FFN_TILE = 512
GELU_A = 0.7978845608028654
GELU_B = 0.044715
norm_eps = 1e-05


def params_of(**extra):
    return pltpu.CompilerParams(vmem_limit_bytes=VMEM_LIMIT, **extra)


class CoreExchange:
    def __init__(self, pairs, send, recv):
        self.pairs, self.send, self.recv = pairs, send, recv
        self.other = {"core": 1 - lax.axis_index("core")}

    def greet(self):
        pl.semaphore_signal(
            pltpu.get_barrier_semaphore(), inc=1, device_id=self.other, device_id_type=MESH
        )

    def meet(self):
        pl.semaphore_wait(pltpu.get_barrier_semaphore(), 1)

    def copies(self, slot):
        return [
            pltpu.make_async_remote_copy(
                src_ref=mine.at[slot], dst_ref=theirs.at[slot],
                send_sem=self.send.at[i, slot], recv_sem=self.recv.at[i, slot],
                device_id=self.other, device_id_type=MESH,
            )
            for i, (mine, theirs) in enumerate(self.pairs)
        ]

    def start(self, slot):
        for copy in self.copies(slot):
            copy.start()

    def arrived(self, slot):
        for copy in self.copies(slot):
            copy.wait_recv()

    def sent(self, slots):
        for slot in range(slots):
            for copy in self.copies(slot):
                copy.wait_send()


class Posts:
    def __init__(self, bits, send, recv):
        self.bits, self.send, self.recv, self.used = bits, send, recv, 0
        self.place = lax.axis_index("pair")
        self.started = []

    def bit(self, b):
        return lax.rem(lax.div(self.place, 1 << b), 2)

    def device(self, link):
        if isinstance(link, str):
            return {link: 1 - lax.axis_index(link)}
        return {"pair": self.place + (1 - 2 * self.bit(link)) * (1 << link)}

    def block(self, flipped):
        at = 0
        for b in range(self.bits):
            here = 1 - self.bit(b) if flipped >> b & 1 else self.bit(b)
            at = at + here * (1 << (self.bits - 1 if b == 0 else b - 1))
        return at

    def slot(self):
        self.used += 1
        return self.used - 1

    def copy(self, src, dst, slot, link):
        return pltpu.make_async_remote_copy(
            src_ref=src, dst_ref=dst, send_sem=self.send.at[slot], recv_sem=self.recv.at[slot],
            device_id=self.device(link), device_id_type=MESH,
        )

    def post(self, src, dst, slot, link):
        copy = self.copy(src, dst, slot, link)
        copy.start()
        self.started.append(copy)

    def await_(self, dst, slot, link):
        self.copy(dst, dst, slot, link).wait_recv()

    def greet(self, links):
        for link in links:
            pl.semaphore_signal(
                pltpu.get_barrier_semaphore(), inc=1, device_id=self.device(link),
                device_id_type=MESH,
            )

    def meet(self, count):
        pl.semaphore_wait(pltpu.get_barrier_semaphore(), count)

    def finish(self):
        for copy in self.started:
            copy.wait_send()


def exchange_sems(pairs, slots):
    return [pltpu.SemaphoreType.DMA((pairs, slots))] * 2


def transform_table(length):
    f = np.arange(length, dtype=np.int64)[:, None]
    t = np.arange(length, dtype=np.int64)[None, :]
    turn = ((4 * f + 1) * t) % (4 * length)
    angle = turn * (2.0 * np.pi / (4 * length))
    return np.concatenate([np.cos(angle), -np.sin(angle)], axis=0)


def cmul(a, b):
    return a[0] * b[0] - a[1] * b[1], a[0] * b[1] + a[1] * b[0]


def log2_of(count):
    bits = count.bit_length() - 1
    assert 1 << bits == count
    return bits


def fill_powers(base, count, out_r, out_i, tmp, scale=None):
    bits = log2_of(count)
    p = base
    for i in range(bits):
        tmp[2 * i] = p[0]
        tmp[2 * i + 1] = p[1]
        p = cmul(p, p)
    if scale is not None:
        tmp[2 * bits] = scale[0]
        tmp[2 * bits + 1] = scale[1]
    row = lax.broadcasted_iota(jnp.int32, (8, LANES), 0)

    def mode(n, carry):
        def at(i):
            return tuple(
                jnp.broadcast_to(tmp[2 * i + j, pl.ds(n, 1), :], (8, LANES)) for j in range(2)
            )

        if scale is None:
            p = (jnp.ones((8, LANES), F32), jnp.zeros((8, LANES), F32))
        else:
            p = at(bits)
        for bit in range(3):
            q = cmul(p, at(bit))
            on = (row & (1 << bit)) != 0
            p = (jnp.where(on, q[0], p[0]), jnp.where(on, q[1], p[1]))
        parts = [p]
        for bit in range(3, bits):
            w = at(bit)
            parts += [cmul(x, w) for x in parts]
        for j, part in enumerate(parts):
            out_r[n, 8 * j : 8 * j + 8, :] = part[0]
            out_i[n, 8 * j : 8 * j + 8, :] = part[1]
        return carry

    lax.fori_loop(0, base[0].shape[0], mode, 0)
    return p


def split_params(packed_ref, log_dt_ref):
    rows = packed_ref[...]
    modes = rows.shape[0] // 4
    log_a, freq, c_real, c_imag = (rows[i * modes : (i + 1) * modes] for i in range(4))
    step = jnp.exp(log_dt_ref[...])
    rate = jnp.exp(log_a)
    decay = jnp.exp(-(step * rate))
    turn = step * freq
    return step, rate, freq, c_real, c_imag, (decay * jnp.cos(turn), decay * jnp.sin(turn))


def kernel_block(packed_ref, log_dt_ref, k_ref, zr, zi, wr, wi, tmp):
    step, _, _, c_real, c_imag, z = split_params(packed_ref, log_dt_ref)
    inner = KERNEL_INNER
    outer = k_ref.shape[0] // inner
    modes = c_real.shape[0]
    z_inner = fill_powers(z, inner, zr, zi, tmp)
    fill_powers(z_inner, outer, wr, wi, tmp, (2.0 * step * c_real, 2.0 * step * c_imag))
    group = 2

    def rows(i, carry):
        d = i * group
        acc = [jnp.zeros((inner, LANES), F32) for _ in range(group)]
        for n in range(modes):
            a, b = zr[n], zi[n]
            for u in range(group):
                acc[u] = acc[u] + (
                    wr[n, pl.ds(d + u, 1), :] * a - wi[n, pl.ds(d + u, 1), :] * b
                )
        for u in range(group):
            at = pl.ds(pl.multiple_of((d + u) * inner, inner), inner)
            k_ref[at, :] = acc[u].astype(BF16)
        return carry

    lax.fori_loop(0, outer // group, rows, 0)


def power_scratch(modes, inner, outer):
    return (
        [pltpu.VMEM((modes, inner, LANES), F32)] * 2
        + [pltpu.VMEM((modes, outer, LANES), F32)] * 2
        + [pltpu.VMEM((20, modes, LANES), F32)]
    )


def moments_block(packed_ref, log_dt_ref, g_ref, out_ref, zr, zi, wr, wi, tmp, sums):
    step, rate, freq, c_real, c_imag, z = split_params(packed_ref, log_dt_ref)
    inner, outer = zr.shape[1], wr.shape[1]
    z_inner = fill_powers(z, inner, zr, zi, tmp)
    fill_powers(z_inner, outer, wr, wi, tmp)
    modes = c_real.shape[0]
    pos = lax.broadcasted_iota(jnp.int32, (inner, LANES), 0).astype(F32)

    def mode(n, carry):
        zero = jnp.zeros((inner, LANES), F32)
        sr, si, tr, ti = zero, zero, zero, zero
        for d in reversed(range(outer)):
            v = g_ref[d * inner : (d + 1) * inner, :]
            sr = sr + v * wr[n, d : d + 1, :]
            si = si + v * wi[n, d : d + 1, :]
            if d > 0:
                tr = tr + sr
                ti = ti + si
        zn = (zr[n], zi[n])
        first = cmul(zn, (sr, si))
        second = cmul(zn, (pos * sr + float(inner) * tr, pos * si + float(inner) * ti))
        for j, v in enumerate(first + second):
            sums[j, pl.ds(n, 1), :] = jnp.sum(v, axis=0, keepdims=True)
        return carry

    lax.fori_loop(0, modes, mode, 0)
    scale = 2.0 * step
    real_grad, imag_grad = scale * sums[0], -scale * sums[1]
    slope_r = scale * (c_real * sums[2] - c_imag * sums[3])
    slope_i = scale * (c_real * sums[3] + c_imag * sums[2])
    log_a_grad = -step * rate * slope_r
    freq_grad = -step * slope_i
    log_dt_grad = jnp.sum(
        c_real * real_grad + c_imag * imag_grad + log_a_grad + freq * freq_grad,
        axis=0, keepdims=True,
    )
    for i, part in enumerate((log_a_grad, freq_grad, real_grad, imag_grad)):
        out_ref[i * modes : (i + 1) * modes, :] = part
    top = 4 * modes
    row = lax.broadcasted_iota(jnp.int32, (8, LANES), 0)
    out_ref[top : top + 8, :] = jnp.where(row == 0, log_dt_grad, 0.0)


def gelu_both(v):
    sq = v * v
    th = jnp.tanh(v * (GELU_A + (GELU_A * GELU_B) * sq))
    rise = 0.5 + 0.5 * th
    slope = rise + v * (0.5 - 0.5 * th * th) * (GELU_A + (3.0 * GELU_A * GELU_B) * sq)
    return v * rise, slope


def gelu(v):
    return gelu_both(v)[0]


def gelu_slope(v):
    return gelu_both(v)[1]


def dot(a, b):
    return jnp.dot(a, b, preferred_element_type=F32)


def conv_block(x, k, skip, fwd_ref, inv_ref, mixed_ref, act_ref, xs_ref, ks_ref, ys):
    n = x.shape[0]
    for i in range(n // DFT_ROWS):
        re = pl.ds(i * DFT_ROWS, DFT_ROWS)
        im = pl.ds(n + i * DFT_ROWS, DFT_ROWS)
        xr, xi = dot(fwd_ref[re, :], x), dot(fwd_ref[im, :], x)
        kr, ki = dot(fwd_ref[re, :], k), dot(fwd_ref[im, :], k)
        xs_ref[re, :] = xr.astype(BF16)
        xs_ref[im, :] = xi.astype(BF16)
        ks_ref[re, :] = kr.astype(BF16)
        ks_ref[im, :] = ki.astype(BF16)
        ys[re, :] = (xr * kr - xi * ki).astype(BF16)
        ys[im, :] = (xr * ki + xi * kr).astype(BF16)
    y = ys[...]
    for i in range(n // TOKEN_ROWS):
        at = pl.ds(i * TOKEN_ROWS, TOKEN_ROWS)
        mixed = dot(inv_ref[at, :], y) + skip * x[i * TOKEN_ROWS : (i + 1) * TOKEN_ROWS].astype(F32)
        mixed_ref[at, :] = mixed
        act_ref[at, :] = gelu(mixed).astype(BF16)


def front_body(
    inputs, cot, counts, gains, log_dt, skip, log_a, freq, c_real, c_imag, fwd_hbm, inv_hbm,
    w_value, w_gate, w_in, w_out,
    packed_ref, vec_ref, skip_ref, grad_ref, x_out, mixed_out, act_out, xs_out, ks_out,
    value_direct, value_via, gate_direct, gate_via, in_direct, in_via, out_direct, out_via,
    zr, zi, wr, wi, tmp, fwd, inv, packed, vec, got_vec, nx, k, mixed, act, xs, ks, ys,
    local, send, recv, *, bits
):
    posts = Posts(bits, send, recv)
    core, side = lax.axis_index("core"), lax.axis_index("tensor")
    half = packed.shape[2]
    modes = log_a.shape[0]
    posts.greet([0, 1, "core", "tensor"])
    tables = [
        pltpu.make_async_copy(src, dst, local.at[i])
        for i, (src, dst) in enumerate(((fwd_hbm, fwd), (inv_hbm, inv)))
    ]
    for copy in tables:
        copy.start()
    mine = pl.ds(pl.multiple_of(core * half, half), half)
    for i, ref in enumerate((log_a, freq, c_real, c_imag)):
        packed[1, i * modes : (i + 1) * modes, :] = ref[:, mine]
    vec[0:1, :] = log_dt[...]
    vec[1:2, :] = skip[...]
    posts.meet(4)

    def exchange(src, dst, link):
        slot = posts.slot()
        posts.post(src, dst, slot, link)
        return lambda: posts.await_(dst, slot, link)

    params_come = [
        exchange(packed.at[1], packed.at[0], "tensor"), exchange(vec, got_vec, "tensor")
    ]
    rows = value_direct.shape[0] // 4
    place = 2 * posts.bit(1) + posts.bit(0)

    def quarter(at, part=None):
        first, count = (0, rows) if part is None else (part * (rows // 2), rows // 2)
        return pl.ds(pl.multiple_of(at * rows + first, rows // 2), count)

    def cols(count):
        return pl.ds(pl.multiple_of(core * count, count), count)

    near, up, across = (place + 1 - 2 * posts.bit(0)), (place + 2 - 4 * posts.bit(1)), 3 - place
    out_row = pl.multiple_of(core * (4 * rows) + place * rows, rows)
    sources = [
        [(w_value.at[quarter(place), cols(half)], value_direct, value_via),
         (w_gate.at[quarter(place), cols(half)], gate_direct, gate_via)],
        [(w_in.at[quarter(place), cols(in_direct.shape[1])], in_direct, in_via)],
        [(w_out.at[pl.ds(out_row, rows), :], out_direct, out_via)],
    ]

    def fetch_steps(items):
        slots = []
        for src, direct, via in items:
            took = [posts.slot() for _ in range(9)]
            slots.append(took)
            posts.post(src, direct.at[quarter(place)], took[0], "tensor")
        yield
        for (src, direct, via), took in zip(items, slots):
            own = direct.at[quarter(place)]
            posts.await_(own, took[0], "tensor")
            posts.post(own, own, took[1], 0)
            posts.post(own, own, took[2], 1)
            posts.post(own, via.at[quarter(place)], took[5], "core")
        yield
        for (src, direct, via), took in zip(items, slots):
            for link, at, slot, on, over, piece in (
                (0, near, 1, 3, 1, 0), (1, up, 2, 4, 0, 1)
            ):
                come = direct.at[quarter(at)]
                posts.await_(come, took[slot], link)
                passed = direct.at[quarter(at, piece)]
                posts.post(passed, passed, took[on], over)
                posts.post(come, via.at[quarter(at)], took[5 + slot], "core")
        yield
        for (src, direct, via), took in zip(items, slots):
            for slot, link, piece in ((3, 1, 0), (4, 0, 1)):
                posts.await_(direct.at[quarter(across, piece)], took[slot], link)
            come = direct.at[quarter(across)]
            posts.post(come, via.at[quarter(across)], took[8], "core")
        yield
        for (src, direct, via), took in zip(items, slots):
            for at, slot in ((place, 5), (near, 6), (up, 7), (across, 8)):
                posts.await_(via.at[quarter(at)], took[slot], "core")

    flows = [fetch_steps(items) for items in sources]
    for flow in flows:
        next(flow)

    def kernel_of(j, log_dt):
        for i in range(half // LANES):
            at = pl.ds(i * LANES, LANES)
            kernel_block(packed.at[1 - j, :, at], log_dt.at[:, at], k.at[2 * j, :, at], zr, zi, wr, wi, tmp)

    vec_ref[1] = vec[0:1, mine]
    kernel_of(0, vec_ref.at[1])
    kernels_come = [exchange(k.at[0], k.at[1], "core")]
    for come in params_come:
        come()
    vec_ref[0] = got_vec[0:1, mine]
    next(flows[0])
    kernel_of(1, vec_ref.at[0])
    kernels_come.append(exchange(k.at[2], k.at[3], "core"))
    next(flows[1])
    for i in range(nx.shape[0] // TOKEN_ROWS):
        at = pl.ds(i * TOKEN_ROWS, TOKEN_ROWS)
        source = inputs[at, :].astype(F32)
        nx[at, :] = norm_forward(source, gains[0:1, :], gains[1:2, :])[0].astype(BF16)
    used = (side < counts[0]).astype(F32)
    grad_ref[...] = (used * cot[...].astype(F32)).astype(BF16)
    width = vec.shape[1]
    for ref, at in ((vec, side), (got_vec, 1 - side)):
        skip_ref[:, pl.ds(pl.multiple_of(at * width, width), width)] = ref[1:2, :]
    stores = [
        pltpu.make_async_copy(nx, x_out, local.at[2]),
        pltpu.make_async_copy(packed, packed_ref, local.at[3]),
    ]
    for copy in stores:
        copy.start()
    for copy in tables:
        copy.wait()
    next(flows[0])
    plan = ((0, flows[2]), (2, flows[1]), (1, flows[0]), (3, flows[2]))
    for n, (j, flow) in enumerate(plan):
        there = lax.rem(side + j // 2, 2)
        which = lax.rem(core + j % 2, 2)
        at = pl.ds(pl.multiple_of((2 * there + which) * half, half), half)
        if j % 2:
            kernels_come[j // 2]()
        params = vec if j < 2 else got_vec
        skip = params[1:2, pl.ds(pl.multiple_of(which * half, half), half)]
        conv_block(
            nx[:, at], k[j], skip, fwd, inv, mixed.at[j], act.at[j], xs.at[j], ks.at[j], ys
        )
        for i, (src, dst) in enumerate(
            ((mixed.at[j], mixed_out.at[j]), (act.at[j], act_out.at[:, at]),
             (xs.at[j], xs_out.at[j]), (ks.at[j], ks_out.at[j]))
        ):
            copy = pltpu.make_async_copy(src, dst, local.at[4 + 4 * j + i])
            copy.start()
            stores.append(copy)
        next(flow)
    for flow in (flows[0], flows[1], flows[1], flows[2], flows[2]):
        next(flow, None)
    for copy in stores:
        copy.wait()
    posts.finish()


def front_kernel(
    inputs, cot, counts, gains, log_dt, skip, log_a, freq, c_real, c_imag, fwd, inv,
    w_value, w_gate, w_in, w_out,
):
    bits = log2_of(lax.axis_size("pair"))
    n, d = inputs.shape
    modes = log_a.shape[0]
    half = d // 4
    units = w_in.shape[1] // 2
    vmem = pl.BlockSpec(memory_space=pltpu.VMEM)
    hbm = pl.BlockSpec(memory_space=pl.ANY)
    shape = jax.ShapeDtypeStruct
    return pl.pallas_call(
        functools.partial(front_body, bits=bits),
        in_specs=[vmem] * 2 + [pl.BlockSpec(memory_space=pltpu.SMEM)] + [vmem] * 7 + [hbm] * 6,
        out_specs=[hbm, vmem, vmem, vmem] + [hbm] * 13,
        out_shape=[
            shape((2, 4 * modes, half), F32), shape((2, 1, half), F32), shape((1, d), F32),
            shape((n, d), BF16), shape((n, d), BF16), shape((4, n, half), F32), shape((n, d), BF16),
            shape((4, 2 * n, half), BF16), shape((4, 2 * n, half), BF16),
        ]
        + [shape((d, half), BF16)] * 4
        + [shape((d, units), BF16)] * 2
        + [shape((units, d), BF16)] * 2,
        scratch_shapes=power_scratch(modes, KERNEL_INNER, n // KERNEL_INNER)
        + [
            pltpu.VMEM(fwd.shape, BF16), pltpu.VMEM(inv.shape, BF16),
            pltpu.VMEM((2, 4 * modes, half), F32),
            pltpu.VMEM((2, d // 2), F32), pltpu.VMEM((2, d // 2), F32),
            pltpu.VMEM((n, d), BF16), pltpu.VMEM((4, n, half), BF16),
            pltpu.VMEM((4, n, half), F32), pltpu.VMEM((4, n, half), BF16),
            pltpu.VMEM((4, 2 * n, half), BF16), pltpu.VMEM((4, 2 * n, half), BF16),
            pltpu.VMEM((2 * n, half), BF16),
            pltpu.SemaphoreType.DMA((20,)),
            pltpu.SemaphoreType.DMA((40,)), pltpu.SemaphoreType.DMA((40,)),
        ],
        compiler_params=params_of(collective_id=5, has_side_effects=True),
        name="front_kernel",
    )(
        inputs, cot, counts, gains, log_dt, skip, log_a, freq, c_real, c_imag, fwd, inv,
        w_value, w_gate, w_in, w_out,
    )


def conv_back_block(ga, mixed, x, xs, ks, skip, fwd, inv, gm, gy, ax, ak, put_gn, put_gk):
    n = x.shape[0]
    total = jnp.zeros((1, x.shape[1]), F32)
    for i in range(n // TOKEN_ROWS):
        at = pl.ds(i * TOKEN_ROWS, TOKEN_ROWS)
        v = ga[at, :] * gelu_slope(mixed[at, :])
        gm[at, :] = v
        gy[at, :] = v.astype(BF16)
        total += jnp.sum(v * x[at, :].astype(F32), axis=0, keepdims=True)
    g = gy[...]
    for i in range(n // DFT_ROWS):
        re = pl.ds(i * DFT_ROWS, DFT_ROWS)
        im = pl.ds(n + i * DFT_ROWS, DFT_ROWS)
        gr, gi = dot(fwd[re, :], g), dot(fwd[im, :], g)
        for src, dst in ((ks, ax), (xs, ak)):
            a, b = src[re, :].astype(F32), src[im, :].astype(F32)
            dst[re, :] = (a * gr + b * gi).astype(BF16)
            dst[im, :] = (a * gi - b * gr).astype(BF16)
    yx = ax[...]
    yk = ak[...]
    for i in range(n // TOKEN_ROWS):
        at = pl.ds(i * TOKEN_ROWS, TOKEN_ROWS)
        put_gk(at, dot(inv[at, :], yk))
        put_gn(at, dot(inv[at, :], yx) + skip * gm[at, :])
    return total


def project_all(left, own, direct, via, out):
    core, side = lax.axis_index("core"), lax.axis_index("tensor")
    width = direct.shape[1]
    far = (1 - side) * 2 * width
    for ref, first, count in (
        (own, side * 2 * width, 2 * width), (direct, far + core * width, width),
        (via, far + (1 - core) * width, width),
    ):
        out[:, pl.ds(pl.multiple_of(first, width), count)] = dot(left, ref[...])


def glu_body(
    act, source, value_own, value_direct, value_via, gate_own, gate_direct, gate_via, gains,
    value_ref, sig_ref, residual_ref, n2_ref, n2t_ref, values, gates,
):
    project_all(act[...], value_own, value_direct, value_via, values)
    project_all(act[...], gate_own, gate_direct, gate_via, gates)
    value = values[...]
    sig = 1.0 / (1.0 + jnp.exp(-gates[...]))
    value_ref[...] = value.astype(BF16)
    sig_ref[...] = sig.astype(BF16)
    residual = source[...].astype(F32) + (value * sig).astype(BF16).astype(F32)
    residual_ref[...] = residual
    n2 = norm_forward(residual, gains[2:3, :], gains[3:4, :])[0].astype(BF16)
    n2_ref[...] = n2
    n2t_ref[...] = n2.T


def glu_kernel(act, source, weights, gains):
    n, d = act.shape
    rows = pl.BlockSpec((TOKEN_ROWS, d), lambda i: (i, 0))

    def whole(a):
        return pl.BlockSpec(a.shape, lambda i: (0, 0), pipeline_mode=pl.Buffered(1))

    return pl.pallas_call(
        glu_body,
        grid=(n // TOKEN_ROWS,),
        in_specs=[rows, rows] + [whole(w) for w in weights] + [whole(gains)],
        out_specs=[rows] * 4 + [pl.BlockSpec((d, TOKEN_ROWS), lambda i: (0, i))],
        out_shape=[
            jax.ShapeDtypeStruct((n, d), BF16), jax.ShapeDtypeStruct((n, d), BF16),
            jax.ShapeDtypeStruct((n, d), F32), jax.ShapeDtypeStruct((n, d), BF16),
            jax.ShapeDtypeStruct((d, n), BF16),
        ],
        scratch_shapes=[pltpu.VMEM((TOKEN_ROWS, d), F32)] * 2,
        compiler_params=params_of(),
        name="glu_kernel",
    )(act, source, *weights, gains)


def glu_back_body(
    g_far, g_own, residual, cot, value, sig, act, value_own, value_direct, value_via,
    gate_own, gate_direct, gate_via, gains,
    there_keep, there_come, in_box, here_out, out_come,
    resid_ref, ga_ref, gain_ref, bias_ref, there_ref, here_ref, in_x, in_y, out_z,
    gv, gt, mine, theirs, in_a, in_b, out_a, out_b, out_box, local, send, recv, *, bits
):
    step = pl.program_id(0)
    posts = Posts(bits, send, recv)
    links = [0, 1, "core", "tensor"]
    slots = {name: posts.slot() for name in ("x", "y", "z")}
    swap = [posts.slot(), posts.slot()]

    def transfers():
        return [
            posts.copy(in_box, in_x, slots["x"], 0),
            posts.copy(in_a, in_y, slots["y"], "tensor"),
            posts.copy(out_box, out_z, slots["z"], 1),
        ]

    @pl.when(step == 0)
    def _():
        posts.greet(links)
        other = 1 - posts.bit(1)
        loads = [
            pltpu.make_async_copy(src, dst, local.at[i])
            for i, (src, dst) in enumerate((
                (there_keep, in_a), (there_come, in_b),
                (here_out.at[:, other], out_a), (out_come.at[:, other], out_b),
            ))
        ]
        for copy in loads:
            copy.start()
        posts.meet(len(links))
        sends = transfers()
        sends[0].start()
        for copy in loads[:2]:
            copy.wait()
        in_a[...] = (in_a[...].astype(F32) + in_b[...].astype(F32)).astype(BF16)
        sends[1].start()
        for copy in loads[2:]:
            copy.wait()
        out_box[...] = (out_a[...] + out_b[...].astype(F32)).astype(BF16)
        sends[2].start()

    chunks = act.shape[0] // TOKEN_ROWS
    width = gv.shape[2]

    @pl.when(step < chunks)
    def _():
        standard, inv_std = norm_forward(residual[...], 1.0, 0.0)[1:]
        part, gain_grad, bias_grad = norm_backward(
            g_far[...] + g_own[...], standard, inv_std, gains[2:3, :]
        )
        new = step == 0
        gain_ref[...] = jnp.where(new, 0.0, gain_ref[...]) + gain_grad[None]
        bias_ref[...] = jnp.where(new, 0.0, bias_ref[...]) + bias_grad[None]
        resid = cot[...].astype(F32) + part
        resid_ref[...] = resid
        grad = resid.astype(BF16).astype(F32)
        gate = sig[...].astype(F32)
        grad_value = (grad * gate).astype(BF16)
        grad_gate = (grad * value[...].astype(F32) * gate * (1.0 - gate)).astype(BF16)
        at = pl.ds(pl.multiple_of(step * TOKEN_ROWS, TOKEN_ROWS), TOKEN_ROWS)
        for i in range(gv.shape[0]):
            gv[i, at, :] = grad_value[:, i * width : (i + 1) * width]
            gt[i, at, :] = grad_gate[:, i * width : (i + 1) * width]
        core, side = lax.axis_index("core"), lax.axis_index("tensor")
        far = 2 * (1 - side)
        total = 0.0
        for grads, own, direct, via in (
            (gv, value_own, value_direct, value_via), (gt, gate_own, gate_direct, gate_via)
        ):
            ours = jnp.concatenate([grads[2 * side, at, :], grads[2 * side + 1, at, :]], axis=1)
            total += contract_cols(ours, own[...])
            total += contract_cols(grads[far + core, at, :], direct[...])
            total += contract_cols(grads[far + 1 - core, at, :], via[...])
        ga_ref[...] = total

    @pl.when(step >= chunks)
    def _():
        j = step - chunks
        side = lax.rem(lax.axis_index("tensor") + 1 + j, 2)
        half = lax.rem(lax.axis_index("core") + 1 + j // 2, 2)
        block = 2 * side + half
        grads = [contract_rows(act[...], gv[block]), contract_rows(act[...], gt[block])]
        for slot in range(2):
            @pl.when(j == slot)
            def _():
                for i, g in enumerate(grads):
                    mine[slot, :, i * width : (i + 1) * width] = g.astype(BF16)
                posts.copy(mine.at[slot], theirs.at[slot], swap[slot], "core").start()

        @pl.when(j == 2)
        def _():
            posts.await_(theirs.at[0], swap[0], "core")
            for i, g in enumerate(grads):
                at = pl.ds(i * width, width)
                there_ref[:, at] = (g + theirs[0, :, at].astype(F32)).astype(BF16)

        @pl.when(j == 3)
        def _():
            posts.await_(theirs.at[1], swap[1], "core")
            for i, g in enumerate(grads):
                at = pl.ds(i * width, width)
                here_ref[:, at] = g + theirs[1, :, at].astype(F32)
            for slot in range(2):
                posts.copy(mine.at[slot], theirs.at[slot], swap[slot], "core").wait_send()
            for copy in transfers():
                copy.wait()


def glu_back_kernel(
    g_far, g_own, residual, cot, value, sig, act, weights, gains,
    there_keep, there_come, in_box, here_out, out_come,
):
    bits = log2_of(lax.axis_size("pair"))
    n, d = act.shape
    chunks = n // TOKEN_ROWS
    width = d // 4
    hbm = pl.BlockSpec(memory_space=pl.ANY)
    extra = (there_keep, there_come, in_box, here_out, out_come)
    split = (here_out.shape[0],) + here_out.shape[2:]

    def whole(a):
        return pl.BlockSpec(a.shape, lambda i: (0, 0), pipeline_mode=pl.Buffered(1))

    rows = pl.BlockSpec((TOKEN_ROWS, d), lambda i: (jnp.minimum(i, chunks - 1), 0))
    vector = pl.BlockSpec((1, d), lambda i: (0, 0))
    weight = pl.BlockSpec((d, 2 * width), lambda i: (0, 0))
    return pl.pallas_call(
        functools.partial(glu_back_body, bits=bits),
        grid=(chunks + 4,),
        in_specs=[rows] * 6 + [whole(act)] + [whole(w) for w in weights] + [whole(gains)] + [hbm] * 5,
        out_specs=[rows, rows, vector, vector, weight, weight] + [hbm] * 3,
        scratch_shapes=[pltpu.VMEM((4, n, width), BF16)] * 2
        + [pltpu.VMEM((2, d, 2 * width), BF16)] * 2
        + [pltpu.VMEM(there_keep.shape, BF16)] * 2
        + [pltpu.VMEM(split, F32), pltpu.VMEM(split, BF16), pltpu.VMEM(split, BF16)]
        + [pltpu.SemaphoreType.DMA((4,))]
        + [pltpu.SemaphoreType.DMA((5,))] * 2,
        out_shape=[
            jax.ShapeDtypeStruct((n, d), F32), jax.ShapeDtypeStruct((n, d), F32),
            jax.ShapeDtypeStruct((1, d), F32), jax.ShapeDtypeStruct((1, d), F32),
            jax.ShapeDtypeStruct((d, 2 * width), BF16), jax.ShapeDtypeStruct((d, 2 * width), F32),
            jax.ShapeDtypeStruct(in_box.shape, BF16), jax.ShapeDtypeStruct(in_box.shape, BF16),
            jax.ShapeDtypeStruct(split, BF16),
        ],
        compiler_params=params_of(collective_id=2, has_side_effects=True),
        name="glu_back_kernel",
    )(g_far, g_own, residual, cot, value, sig, act, *weights, gains, *extra)


def ffn_body(
    n2, n2t, gl, ia, ib, oa, ob, ffn, gn2, box_ref, keep_ref, out_ref,
    wi, wo, h, gp, total, in_mine, out_mine, in_theirs, out_theirs, send, recv,
):
    step, half = pl.program_id(0), in_mine.shape[0]
    first = step < half
    cores = CoreExchange([(in_mine, in_theirs), (out_mine, out_theirs)], send, recv)
    pl.when(step == 0)(cores.greet)

    @pl.when(first)
    def _():
        wi[...] = ia[...]
        wo[...] = oa[...]

    @pl.when(jnp.logical_not(first))
    def _():
        wi[...] = ib[...]
        wo[...] = ob[...]

    @pl.when(step == 0)
    def _():
        ffn[...] = jnp.zeros_like(ffn)
        gn2[...] = jnp.zeros_like(gn2)

    w1, w2 = wi[...], wo[...]
    for r in range(n2.shape[0] // TOKEN_ROWS):
        at = pl.ds(r * TOKEN_ROWS, TOKEN_ROWS)
        act, slope = gelu_both(dot(n2[at, :], w1))
        hidden = act.astype(BF16)
        grad_pre = (contract_cols(gl[at, :], w2) * slope).astype(BF16)
        h[at, :] = hidden
        gp[at, :] = grad_pre
        ffn[at, :] += dot(hidden, w2)
        gn2[at, :] += contract_cols(grad_pre, w1)
    out_grad = contract_rows(h[...], gl[...])
    in_grad = dot(n2t[...], gp[...])

    pl.when(step == 0)(cores.meet)

    @pl.when(first)
    def _():
        in_mine[step] = in_grad.astype(BF16)
        out_mine[step] = out_grad.astype(BF16)
        cores.start(step)

    @pl.when(jnp.logical_not(first))
    def _():
        cores.arrived(step - half)
        total[...] = in_grad + in_theirs[step - half].astype(F32)
        near, rows = lax.rem(lax.axis_index("pair"), 2), keep_ref.shape[0]
        for ref, at in ((keep_ref, near), (box_ref, 1 - near)):
            part = pl.ds(pl.multiple_of(at * rows, rows), rows)
            ref[...] = total[part, :].astype(ref.dtype)
        out_ref[...] = (out_grad + out_theirs[step - half].astype(F32)).astype(out_ref.dtype)

    @pl.when(step == 2 * half - 1)
    def _():
        cores.sent(half)


def ffn_kernel(n2, n2t, gl, ins, outs, units, own):
    n, d = n2.shape
    half = units // FFN_TILE

    def whole(a):
        return pl.BlockSpec(a.shape, lambda s: (0, 0), pipeline_mode=pl.Buffered(1))

    def fst(s):
        at = jnp.minimum(s, half - 1)
        return at + (1 - lax.axis_index("core")) * half if own else at

    def snd(s):
        at = jnp.maximum(s - half, 0)
        return at + lax.axis_index("core") * half if own else at

    total = pl.BlockSpec((n, d), lambda s: (0, 0))
    dtype = F32 if own else BF16
    return pl.pallas_call(
        ffn_body,
        grid=(2 * half,),
        in_specs=[
            whole(n2), whole(n2t), whole(gl),
            pl.BlockSpec((d, FFN_TILE), lambda s: (0, fst(s))),
            pl.BlockSpec((d, FFN_TILE), lambda s: (0, snd(s))),
            pl.BlockSpec((FFN_TILE, d), lambda s: (fst(s), 0)),
            pl.BlockSpec((FFN_TILE, d), lambda s: (snd(s), 0)),
        ],
        out_specs=[
            total, total,
            pl.BlockSpec((d // 2, FFN_TILE), lambda s: (0, jnp.maximum(s - half, 0))),
            pl.BlockSpec((d // 2, FFN_TILE), lambda s: (0, jnp.maximum(s - half, 0))),
            pl.BlockSpec((FFN_TILE, d), lambda s: (jnp.maximum(s - half, 0), 0)),
        ],
        scratch_shapes=[
            pltpu.VMEM((d, FFN_TILE), BF16), pltpu.VMEM((FFN_TILE, d), BF16),
            pltpu.VMEM((n, FFN_TILE), BF16), pltpu.VMEM((n, FFN_TILE), BF16),
            pltpu.VMEM((d, FFN_TILE), F32),
        ]
        + [pltpu.VMEM((half, d, FFN_TILE), BF16), pltpu.VMEM((half, FFN_TILE, d), BF16)] * 2
        + exchange_sems(2, half),
        out_shape=[
            jax.ShapeDtypeStruct((n, d), F32), jax.ShapeDtypeStruct((n, d), F32),
            jax.ShapeDtypeStruct((d // 2, units), BF16), jax.ShapeDtypeStruct((d // 2, units), dtype),
            jax.ShapeDtypeStruct((units, d), dtype),
        ],
        compiler_params=params_of(collective_id=int(own), has_side_effects=True),
        name="ffn_kernel",
    )(n2, n2t, gl, *ins, *outs)


def norm_forward(values, norm_gain, norm_bias):
    center = values - jnp.mean(values, axis=-1, keepdims=True)
    inv_std = lax.rsqrt(jnp.mean(center * center, axis=-1, keepdims=True) + norm_eps)
    standard = center * inv_std
    return (standard * norm_gain + norm_bias, standard, inv_std)


def norm_backward(incoming, standard, inv_std, norm_gain):
    scaled = incoming * norm_gain
    value_grad = inv_std * (
        scaled
        - jnp.mean(scaled, axis=-1, keepdims=True)
        - standard * jnp.mean(scaled * standard, axis=-1, keepdims=True)
    )
    return (value_grad, jnp.sum(incoming * standard, axis=0), jnp.sum(incoming, axis=0))


def contract_rows(left, right):
    return lax.dot_general(left, right, (((0,), (0,)), ((), ())), preferred_element_type=F32)


def contract_cols(left, right):
    return lax.dot_general(left, right, (((1,), (1,)), ((), ())), preferred_element_type=F32)


def scatter_steps(posts, acc, bits, order, boxes, come):
    def at(known, flipped):
        place = 0
        for i, b in enumerate(bits):
            here = posts.bit(b)
            if b in known:
                bit = 1 - here if known[b] else here
            else:
                bit = flipped >> i & 1
            place = place + bit * (1 << i)
        return place

    done = {}
    used = 0
    for n, b in enumerate(order):
        rest = [bits.index(i) for i in order[n + 1 :]]
        combos = [sum((c >> k & 1) << i for k, i in enumerate(rest)) for c in range(1 << len(rest))]
        slots = []
        for c, combo in enumerate(combos):
            slot = posts.slot()
            boxes[used + c] = acc[at({**done, b: True}, combo)].astype(BF16)
            posts.post(boxes.at[used + c], come.at[used + c], slot, b)
            slots.append(slot)
        yield
        done[b] = False
        for c, combo in enumerate(combos):
            posts.await_(come.at[used + c], slots[c], b)
            keep = at(done, combo)
            acc[keep] = acc[keep] + come[used + c].astype(F32)
        used += len(combos)
    posts.result = at(done, 0)


def gather_steps(posts, own, whole, local, order):
    core = lax.axis_index("core")
    count = 1 << posts.bits
    slots = {(rel, link): posts.slot() for rel in range(count) for link in ("bit", "core")}
    first = pltpu.make_async_copy(own, whole.at[core, posts.block(0)], local)
    first.start()

    def pass_on(src, rel, bits):
        dst = whole.at[core, posts.block(rel)]
        for b in bits:
            posts.post(src, dst, slots[rel ^ (1 << b), "bit"], b)
        posts.post(src, dst, slots[rel, "core"], "core")

    pass_on(own, 0, order)
    for n, b in enumerate(order):
        for c in range(1 << n):
            yield
            rel = sum((c >> k & 1) << order[k] for k in range(n)) | 1 << b
            block = whole.at[core, posts.block(rel)]
            posts.await_(block, slots[rel, "bit"], b)
            pass_on(block, rel, order[n + 1 :])
    yield
    first.wait()
    for rel in range(count):
        posts.await_(whole.at[1 - core, posts.block(rel)], slots[rel, "core"], "core")


def back_body(
    ga_hbm, mixed_hbm, x_hbm, xs_hbm, ks_hbm, fwd_hbm, inv_hbm, source_hbm, resid_hbm,
    in_keep, in_x, in_y, out_keep, out_come, out_z, glu_keep, glu_box,
    skip, gains, gain2, bias2, packed, log_dt,
    input_ref, in_all, out_all, glu_all, small_all,
    ga, fwd, inv, mixed, x, xs, ks, gm, gy, ax, ak, gk, gk_mine, gk_theirs, source, resid, staged,
    zr, zi, wr, wi, tmp, sums, moments, rows, rows_mine, rows_other, rows_come,
    in_acc, in_a, in_b, out_acc, out_a, out_b, glu_acc, glu_come, in_own, out_own, glu_own,
    in_boxes, in_got, out_boxes, out_got, glu_boxes, glu_got, small, small_far, small_got,
    local, send, recv, *, bits
):
    posts = Posts(bits, send, recv)
    links = list(range(bits)) + ["core", "tensor"]
    posts.greet(links)
    core, side = lax.axis_index("core"), lax.axis_index("tensor")
    n, width = mixed.shape[1:]
    used = [3]

    def load(src, dst):
        copy = pltpu.make_async_copy(src, dst, local.at[used[0]])
        used[0] += 1
        copy.start()
        return copy

    def columns(i):
        there = lax.rem(side + 1 + i, 2)
        which = lax.rem(core + 1 + i // 2, 2)
        return pl.ds(pl.multiple_of((2 * there + which) * width, width), width)

    def load_block(i):
        j, slot = 2 * ((i + 1) % 2) + 1 - i // 2, i % 2
        return [
            load(mixed_hbm.at[j], mixed.at[slot]), load(x_hbm.at[:, columns(i)], x.at[slot]),
            load(xs_hbm.at[j], xs.at[slot]), load(ks_hbm.at[j], ks.at[slot]),
        ]

    mine = posts.bit(1)
    in_loads = [load(in_keep, in_acc), load(in_x, in_a), load(in_y, in_b)]
    out_loads = [
        load(out_keep.at[:, mine], out_acc), load(out_come.at[:, mine], out_a), load(out_z, out_b)
    ]
    ga_load = load(ga_hbm, ga)
    block_loads = load_block(0)
    tables = [load(fwd_hbm, fwd), load(inv_hbm, inv)]
    glu_load = load(glu_keep, glu_acc)
    posts.meet(len(links))
    near, far = list(range(1, bits)), list(range(2, bits))

    def in_steps():
        for copy in in_loads:
            copy.wait()
        in_acc[...] = in_acc[...] + in_a[...].astype(F32) + in_b[...].astype(F32)
        yield from scatter_steps(posts, in_acc, near, near, in_boxes, in_got)
        in_own[...] = in_acc[posts.result].astype(BF16)
        yield from gather_steps(posts, in_own, in_all, local.at[0], list(reversed(range(bits))))

    def out_steps():
        for copy in out_loads:
            copy.wait()
        out_acc[...] = out_acc[...] + out_a[...].astype(F32) + out_b[...].astype(F32)
        yield from scatter_steps(posts, out_acc, far + [0], [0] + far, out_boxes, out_got)
        out_own[...] = out_acc[posts.result].astype(BF16)
        yield from gather_steps(posts, out_own, out_all, local.at[1], list(reversed(range(bits))))

    def glu_steps():
        slot = posts.slot()
        posts.post(glu_box, glu_come, slot, "tensor")
        yield
        posts.await_(glu_come, slot, "tensor")
        glu_load.wait()
        glu_acc[...] = glu_acc[...] + glu_come[...].astype(F32)
        yield from scatter_steps(posts, glu_acc, near + [0], [0] + near, glu_boxes, glu_got)
        glu_own[...] = glu_acc[posts.result].astype(BF16)
        yield from gather_steps(posts, glu_own, glu_all, local.at[2], GLU_ORDER(bits))

    def small_steps():
        for j in range(2):
            for half, ref in ((core, rows_mine), (1 - core, rows_other)):
                there = lax.rem(side + 1 + j, 2)
                at = pl.multiple_of((2 * there + half) * width, width)
                ref[j] = rows[:, pl.ds(at, width)]
        slot = posts.slot()
        posts.post(rows_other, rows_come, slot, "core")
        yield
        posts.await_(rows_come, slot, "core")
        top = moments.shape[1]
        for j, ref in ((0, small_far), (1, small)):
            ref[:top, :] = moments[j]
            ref[top:, :] = rows_mine[j] + rows_come[j]
        slot = posts.slot()
        posts.post(small_far, small_got.at[0], slot, "tensor")
        yield
        posts.await_(small_got.at[0], slot, "tensor")
        small[...] = small[...] + small_got[0]
        for b in range(bits):
            slot = posts.slot()
            small_all[b] = small[...]
            posts.post(small_all.at[b], small_got.at[1 + b], slot, b)
            yield
            posts.await_(small_got.at[1 + b], slot, b)
            small[...] = small[...] + small_got[1 + b]
        slot = posts.slot()
        small_all[bits] = small[...]
        posts.post(small_all.at[bits], small_got.at[1 + bits], slot, "core")
        yield
        posts.await_(small_got.at[1 + bits], slot, "core")
        small_all[bits + 1] = small_got[1 + bits]

    flows = {"in": in_steps(), "out": out_steps(), "glu": glu_steps()}
    done = object()

    def advance(*names):
        for name in names:
            if name in flows and next(flows[name], done) is done:
                del flows[name]

    advance("glu", "in", "out")
    rows[...] = jnp.zeros_like(rows)
    rows[3:4, :] = gain2[...]
    rows[4:5, :] = bias2[...]
    ga_load.wait()
    slots = [posts.slot(), posts.slot()]
    for i in range(4):
        slot = i % 2
        for copy in block_loads:
            copy.wait()
        if i < 3:
            block_loads = load_block(i + 1)
        if i == 0:
            for copy in tables:
                copy.wait()
        at = columns(i)

        def put_gn(tokens, value, at=at):
            ga[tokens, at] = value

        def put_gk(tokens, value, i=i):
            if i < 2:
                gk_mine[i, tokens, :] = value.astype(BF16)
            else:
                gk[i - 2, tokens, :] = value

        rows[0:1, at] = conv_back_block(
            ga.at[:, at], mixed.at[slot], x.at[slot], xs.at[slot], ks.at[slot], skip[:, at],
            fwd, inv, gm, gy, ax, ak, put_gn, put_gk,
        )
        if i < 2:
            posts.post(gk_mine.at[i], gk_theirs.at[i], slots[i], "core")
        else:
            posts.await_(gk_theirs.at[i - 2], slots[i - 2], "core")
            gk[i - 2] = gk[i - 2] + gk_theirs[i - 2].astype(F32)
        if i in BACK_ROUNDS:
            advance(*BACK_ROUNDS[i])

    chunks = n // TOKEN_ROWS

    def load_rows(r):
        at = pl.ds(r * TOKEN_ROWS, TOKEN_ROWS)
        return [load(source_hbm.at[at], source.at[r % 2]), load(resid_hbm.at[at], resid.at[r % 2])]

    row_loads = load_rows(0)
    stores = []
    for r in range(chunks):
        for copy in row_loads:
            copy.wait()
        if r + 1 < chunks:
            row_loads = load_rows(r + 1)
        at = pl.ds(r * TOKEN_ROWS, TOKEN_ROWS)
        standard, inv_std = norm_forward(source[r % 2].astype(F32), 1.0, 0.0)[1:]
        part, gain_grad, bias_grad = norm_backward(ga[at, :], standard, inv_std, gains[0:1, :])
        rows[1:2, :] = rows[1:2, :] + gain_grad[None]
        rows[2:3, :] = rows[2:3, :] + bias_grad[None]
        staged[r] = (resid[r % 2] + part).astype(BF16)
        stores.append(load(staged.at[r], input_ref.at[at]))
    advance(*BACK_ROUNDS["norm"])

    def block(j, i):
        at = pl.ds(i * LANES, LANES)
        moments_block(
            packed.at[j, :, at], log_dt.at[j, :, at], gk.at[j, :, at], moments.at[j, :, at],
            zr, zi, wr, wi, tmp, sums,
        )

    for j in range(2):
        for i in range(width // LANES):
            block(j, i)
            advance("in", "out", "glu")
    flows["small"] = small_steps()
    while flows:
        advance("small", "in", "out", "glu")
    for copy in stores:
        copy.wait()
    posts.finish()


def back_kernel(
    ga, mixed, x, xs, ks, fwd, inv, source, resid, in_keep, in_x, in_y, out_keep, out_come, out_z,
    glu_keep, glu_box, skip, gains, gain2, bias2, packed, log_dt,
):
    bits = log2_of(lax.axis_size("pair"))
    blocks = 1 << bits
    width, modes = packed.shape[2], packed.shape[1] // 4
    n, d = ga.shape
    block_rows, cols = glu_keep.shape[1:]
    kept = in_keep.shape[0]
    small_rows = 4 * modes + 8 + 8
    vmem = pl.BlockSpec(memory_space=pltpu.VMEM)
    hbm = pl.BlockSpec(memory_space=pl.ANY)
    big = pltpu.VMEM((block_rows, d), BF16)
    small = pltpu.VMEM((small_rows, width), F32)
    rows = pltpu.VMEM((2, 8, width), F32)
    copies = 3 * 2 * blocks + 2 * kept + blocks + bits + 12
    shape = jax.ShapeDtypeStruct
    return pl.pallas_call(
        functools.partial(back_body, bits=bits),
        in_specs=[hbm] * 17 + [vmem] * 6,
        out_specs=[hbm] * 4 + [vmem],
        out_shape=[
            shape((n, d), BF16), shape((2, blocks, block_rows, d), BF16),
            shape((2, blocks, block_rows, d), BF16), shape((2, blocks, block_rows, cols), BF16),
            shape((bits + 2, small_rows, width), F32),
        ],
        scratch_shapes=[
            pltpu.VMEM((n, d), F32), pltpu.VMEM(fwd.shape, BF16), pltpu.VMEM(inv.shape, BF16),
            pltpu.VMEM((2, n, width), F32), pltpu.VMEM((2, n, width), BF16),
            pltpu.VMEM((2, 2 * n, width), BF16), pltpu.VMEM((2, 2 * n, width), BF16),
            pltpu.VMEM((n, width), F32), pltpu.VMEM((n, width), BF16),
            pltpu.VMEM((2 * n, width), BF16), pltpu.VMEM((2 * n, width), BF16),
            pltpu.VMEM((2, n, width), F32), pltpu.VMEM((2, n, width), BF16),
            pltpu.VMEM((2, n, width), BF16),
            pltpu.VMEM((2, TOKEN_ROWS, d), BF16), pltpu.VMEM((2, TOKEN_ROWS, d), F32),
            pltpu.VMEM((n // TOKEN_ROWS, TOKEN_ROWS, d), BF16),
        ]
        + power_scratch(modes, MOMENT_INNER, n // MOMENT_INNER)
        + [
            pltpu.VMEM((4, modes, LANES), F32), pltpu.VMEM((2, 4 * modes + 8, width), F32),
            pltpu.VMEM((8, d), F32), rows, rows, rows,
            pltpu.VMEM(in_keep.shape, F32), pltpu.VMEM(in_keep.shape, BF16),
            pltpu.VMEM(in_keep.shape, BF16),
            pltpu.VMEM(in_keep.shape, F32), pltpu.VMEM(in_keep.shape, BF16),
            pltpu.VMEM(in_keep.shape, BF16),
            pltpu.VMEM(glu_keep.shape, F32), pltpu.VMEM(glu_keep.shape, BF16),
            big, big, pltpu.VMEM((block_rows, cols), BF16),
        ]
        + [pltpu.VMEM((kept - 1, block_rows, d), BF16)] * 4
        + [pltpu.VMEM((blocks - 1, block_rows, cols), BF16)] * 2
        + [small, small, pltpu.VMEM((bits + 2, small_rows, width), F32)]
        + [pltpu.SemaphoreType.DMA((48,))]
        + [pltpu.SemaphoreType.DMA((copies,))] * 2,
        compiler_params=params_of(collective_id=4, has_side_effects=True),
        name="back_kernel",
    )(
        ga, mixed, x, xs, ks, fwd, inv, source, resid, in_keep, in_x, in_y, out_keep, out_come, out_z,
        glu_keep, glu_box, skip, gains, gain2, bias2, packed, log_dt,
    )


def GLU_ORDER(bits):
    return list(reversed(range(bits)))


BACK_ROUNDS = {1: ("in", "out"), 3: ("glu", "in"), "norm": ("out", "in", "glu")}


SWAP = ((0, 1), (1, 0))


def over_core(values):
    return lax.ppermute(values, "core", SWAP)


def over_tensor(values):
    return lax.ppermute(values, "tensor", SWAP)


def over_pair(values, flip):
    size = lax.axis_size("pair")
    return lax.ppermute(values, "pair", [(p, p ^ flip) for p in range(size)])


def place_in(group):
    first, count = group
    return (lax.axis_index("pair") // (1 << first)) % (1 << count)


def flips_of(group):
    first, count = group
    return [j << first for j in range(1, 1 << count)]


def pair_bits():
    return log2_of(lax.axis_size("pair"))


def by_bits(values):
    bits = pair_bits()
    return values.reshape(*[2] * bits, values.shape[0] >> bits, values.shape[1])


def split_over(total, bit):
    axis = 0 if bit == 0 else pair_bits() - bit
    return part(total, place_in((bit, 1)), axis), part(total, 1 - place_in((bit, 1)), axis).astype(BF16)


def gathered(keep, come, group, axis):
    me = place_in(group)
    parts = [keep] + come
    bit = 1
    while bit < len(parts):
        swapped = (me & bit) != 0
        parts = [jnp.where(swapped, parts[k ^ bit], parts[k]) for k in range(len(parts))]
        bit *= 2
    return jnp.concatenate(parts, axis=axis)


def ordered(index, mine, other, axis):
    first = jnp.where(index == 0, mine, other)
    second = jnp.where(index == 0, other, mine)
    return jnp.concatenate([first, second], axis=axis)


def part(values, index, axis):
    half = values.shape[axis] // 2
    return lax.dynamic_slice_in_dim(values, index * half, half, axis)


def together(*values):
    return lax.optimization_barrier(values)


def shards(
    inputs, counts, ln1_gain, ln1_bias, log_dt, log_a, freq, c_real, c_imag, skip_gain,
    w_value, w_gate, ln2_gain, ln2_bias, w_in, w_out, cotangent,
):
    _, length, width = inputs.shape
    core, side = lax.axis_index("core"), lax.axis_index("tensor")
    source = inputs.reshape(length, width)
    gains = jnp.stack([ln1_gain, ln1_bias, ln2_gain, ln2_bias]).astype(F32)
    table = transform_table(length)
    fwd = jnp.asarray(table.astype(ml_dtypes.bfloat16))
    inv = jnp.asarray(np.ascontiguousarray((table.T / length).astype(ml_dtypes.bfloat16)))
    (
        packed, log_dts, skip, grad_low, normed1, mixed, act, spectrum, kernel_spectrum,
        value_direct, value_via, gate_direct, gate_via, in_direct, in_via, out_direct, out_via,
    ) = front_kernel(
        source, cotangent.reshape(length, width), counts, gains, log_dt[None], skip_gain[None],
        log_a.T, freq.T, c_real.T, c_imag.T, fwd, inv, w_value, w_gate, w_in, w_out,
    )
    glu_weights = (w_value, value_direct, value_via, w_gate, gate_direct, gate_via)
    value_proj, gate_sig, residual, normed2, normed2_t = glu_kernel(act, source, glu_weights, gains)
    units = in_direct.shape[1]
    far_ffn, far_normed2, there_box, there_keep, there_out = ffn_kernel(
        normed2, normed2_t, grad_low, (in_via, in_direct), (out_via, out_direct), units, False
    )
    normed2, there_out, there_box = together(normed2, there_out, there_box)
    out_come, there_come = over_tensor(there_out), over_pair(there_box, 1)
    own_sums = ffn_kernel(normed2, normed2_t, grad_low, (w_in, w_in), (w_out, w_out), units, True)
    own_sums, out_come, there_come = together(own_sums, out_come, there_come)
    own_ffn, own_normed2, in_box, in_keep, here_out = own_sums
    blocks = lax.axis_size("pair")
    split = (blocks // 2, 2, width // blocks, width)
    here_out, out_come = here_out.reshape(split), out_come.reshape(split)
    (
        grad_residual, grad_act, gain_second_grad, bias_second_grad, there_glu, here_glu,
        in_x, in_y, out_z,
    ) = glu_back_kernel(
        far_normed2, own_normed2, residual, grad_low, value_proj, gate_sig, act, glu_weights, gains,
        there_keep, there_come, in_box, here_out, out_come,
    )
    halved = (blocks // 2, width // blocks, width)
    by_block = (blocks, width // blocks, -1)
    input_grad, in_all, out_all, glu_all, small = back_kernel(
        grad_act, mixed, normed1, spectrum, kernel_spectrum, fwd, inv, source, grad_residual,
        in_keep.reshape(halved), in_x.reshape(halved), in_y.reshape(halved),
        here_out, out_come, out_z, here_glu.reshape(by_block), there_glu.reshape(by_block),
        skip, gains, gain_second_grad, bias_second_grad, packed, log_dts,
    )
    used_flag = (side < counts[0]).astype(F32)
    output = (used_flag * (residual + (far_ffn + own_ffn))).astype(BF16).reshape(inputs.shape)
    input_grad = input_grad.reshape(inputs.shape)
    small = ordered(core, small[-2], small[-1], 1)
    out_total = out_all.reshape(-1, width).astype(F32)
    in_all = in_all.reshape(2, width, -1)
    in_total = jnp.concatenate([in_all[0], in_all[1]], axis=1).astype(F32)
    glu_all = glu_all.reshape(2, width, -1)
    cut = glu_all.shape[2] // 2
    value_total = jnp.concatenate([glu_all[0, :, :cut], glu_all[1, :, :cut]], axis=1).astype(F32)
    gate_total = jnp.concatenate([glu_all[0, :, cut:], glu_all[1, :, cut:]], axis=1).astype(F32)

    modes = log_a.shape[1]
    top = 4 * modes
    return (
        output,
        input_grad,
        small[top + 9],
        small[top + 10],
        small[top],
        small[:modes].T,
        small[modes : 2 * modes].T,
        small[2 * modes : 3 * modes].T,
        small[3 * modes : 4 * modes].T,
        small[top + 8],
        value_total,
        gate_total,
        small[top + 11],
        small[top + 12],
        in_total,
        out_total,
    )


def solution(mesh):
    devices = mesh.devices
    cores = jax.sharding.Mesh(
        devices.reshape(devices.shape[0] // 2, 2, devices.shape[1]), ("pair", "core", "tensor")
    )
    batch, every = ("pair", "core"), ("pair", "core", "tensor")
    in_specs = (
        P(every, None, None), P(batch), P(), P(), P("tensor"), P("tensor", None), P("tensor", None),
        P("tensor", None), P("tensor", None), P("tensor"), P(None, "tensor"), P(None, "tensor"),
        P(), P(), P(None, "tensor"), P("tensor", None), P(every, None, None),
    )
    out_specs = (
        P(every, None, None), P(every, None, None), P("tensor"), P("tensor"), P("tensor"),
        P("tensor", None), P("tensor", None), P("tensor", None), P("tensor", None), P("tensor"),
        P(None, "tensor"), P(None, "tensor"), P("tensor"), P("tensor"), P(None, "tensor"),
        P("tensor", None),
    )
    return jax.shard_map(shards, mesh=cores, in_specs=in_specs, out_specs=out_specs, check_vma=False)
```

```python
import functools

import ml_dtypes
import numpy as np

import jax
import jax.numpy as jnp
from jax import lax
from jax.experimental import pallas as pl
from jax.experimental.pallas import tpu as pltpu
from jax.sharding import PartitionSpec as P

VMEM_LIMIT = 60 * 1024 * 1024
F32, BF16 = jnp.float32, jnp.bfloat16
LANES = 128
MESH = pl.DeviceIdType.MESH
KERNEL_INNER = 64
MOMENT_INNER = 32
CB = 256
DFT_ROWS = 512
TOKEN_ROWS = 256
FFN_TILE = 512
GELU_A = 0.7978845608028654
GELU_B = 0.044715
norm_eps = 1e-05


def params_of(**extra):
    return pltpu.CompilerParams(vmem_limit_bytes=VMEM_LIMIT, **extra)


class CoreExchange:
    def __init__(self, pairs, send, recv):
        self.pairs, self.send, self.recv = pairs, send, recv
        self.other = {"core": 1 - lax.axis_index("core")}

    def greet(self):
        pl.semaphore_signal(
            pltpu.get_barrier_semaphore(), inc=1, device_id=self.other, device_id_type=MESH
        )

    def meet(self):
        pl.semaphore_wait(pltpu.get_barrier_semaphore(), 1)

    def copies(self, slot):
        return [
            pltpu.make_async_remote_copy(
                src_ref=mine.at[slot], dst_ref=theirs.at[slot],
                send_sem=self.send.at[i, slot], recv_sem=self.recv.at[i, slot],
                device_id=self.other, device_id_type=MESH,
            )
            for i, (mine, theirs) in enumerate(self.pairs)
        ]

    def start(self, slot):
        for copy in self.copies(slot):
            copy.start()

    def arrived(self, slot):
        for copy in self.copies(slot):
            copy.wait_recv()

    def sent(self, slots):
        for slot in range(slots):
            for copy in self.copies(slot):
                copy.wait_send()


class Posts:
    def __init__(self, bits, send, recv):
        self.bits, self.send, self.recv, self.used = bits, send, recv, 0
        self.place = lax.axis_index("pair")
        self.started = []

    def bit(self, b):
        return lax.rem(lax.div(self.place, 1 << b), 2)

    def device(self, link):
        if isinstance(link, str):
            return {link: 1 - lax.axis_index(link)}
        return {"pair": self.place + (1 - 2 * self.bit(link)) * (1 << link)}

    def block(self, flipped):
        at = 0
        for b in range(self.bits):
            here = 1 - self.bit(b) if flipped >> b & 1 else self.bit(b)
            at = at + here * (1 << (self.bits - 1 if b == 0 else b - 1))
        return at

    def slot(self):
        self.used += 1
        return self.used - 1

    def copy(self, src, dst, slot, link):
        return pltpu.make_async_remote_copy(
            src_ref=src, dst_ref=dst, send_sem=self.send.at[slot], recv_sem=self.recv.at[slot],
            device_id=self.device(link), device_id_type=MESH,
        )

    def post(self, src, dst, slot, link):
        copy = self.copy(src, dst, slot, link)
        copy.start()
        self.started.append(copy)

    def await_(self, dst, slot, link):
        self.copy(dst, dst, slot, link).wait_recv()

    def greet(self, links):
        for link in links:
            pl.semaphore_signal(
                pltpu.get_barrier_semaphore(), inc=1, device_id=self.device(link),
                device_id_type=MESH,
            )

    def meet(self, count):
        pl.semaphore_wait(pltpu.get_barrier_semaphore(), count)

    def finish(self):
        for copy in self.started:
            copy.wait_send()


def exchange_sems(pairs, slots):
    return [pltpu.SemaphoreType.DMA((pairs, slots))] * 2


def transform_table(length):
    f = np.arange(length, dtype=np.int64)[:, None]
    t = np.arange(length, dtype=np.int64)[None, :]
    turn = ((4 * f + 1) * t) % (4 * length)
    angle = turn * (2.0 * np.pi / (4 * length))
    return np.concatenate([np.cos(angle), -np.sin(angle)], axis=0)


def cmul(a, b):
    return a[0] * b[0] - a[1] * b[1], a[0] * b[1] + a[1] * b[0]


def log2_of(count):
    bits = count.bit_length() - 1
    assert 1 << bits == count
    return bits


def fill_powers(base, count, out_r, out_i, tmp, scale=None):
    bits = log2_of(count)
    p = base
    for i in range(bits):
        tmp[2 * i] = p[0]
        tmp[2 * i + 1] = p[1]
        p = cmul(p, p)
    if scale is not None:
        tmp[2 * bits] = scale[0]
        tmp[2 * bits + 1] = scale[1]
    row = lax.broadcasted_iota(jnp.int32, (8, LANES), 0)

    def mode(n, carry):
        def at(i):
            return tuple(
                jnp.broadcast_to(tmp[2 * i + j, pl.ds(n, 1), :], (8, LANES)) for j in range(2)
            )

        if scale is None:
            p = (jnp.ones((8, LANES), F32), jnp.zeros((8, LANES), F32))
        else:
            p = at(bits)
        for bit in range(3):
            q = cmul(p, at(bit))
            on = (row & (1 << bit)) != 0
            p = (jnp.where(on, q[0], p[0]), jnp.where(on, q[1], p[1]))
        parts = [p]
        for bit in range(3, bits):
            w = at(bit)
            parts += [cmul(x, w) for x in parts]
        for j, part in enumerate(parts):
            out_r[n, 8 * j : 8 * j + 8, :] = part[0]
            out_i[n, 8 * j : 8 * j + 8, :] = part[1]
        return carry

    lax.fori_loop(0, base[0].shape[0], mode, 0)
    return p


def split_params(packed_ref, log_dt_ref):
    rows = packed_ref[...]
    modes = rows.shape[0] // 4
    log_a, freq, c_real, c_imag = (rows[i * modes : (i + 1) * modes] for i in range(4))
    step = jnp.exp(log_dt_ref[...])
    rate = jnp.exp(log_a)
    decay = jnp.exp(-(step * rate))
    turn = step * freq
    return step, rate, freq, c_real, c_imag, (decay * jnp.cos(turn), decay * jnp.sin(turn))


def kernel_block(packed_ref, log_dt_ref, k_ref, zr, zi, wr, wi, tmp):
    step, _, _, c_real, c_imag, z = split_params(packed_ref, log_dt_ref)
    inner = KERNEL_INNER
    outer = k_ref.shape[0] // inner
    modes = c_real.shape[0]
    z_inner = fill_powers(z, inner, zr, zi, tmp)
    fill_powers(z_inner, outer, wr, wi, tmp, (2.0 * step * c_real, 2.0 * step * c_imag))
    group = 2

    def rows(i, carry):
        d = i * group
        acc = [jnp.zeros((inner, LANES), F32) for _ in range(group)]
        for n in range(modes):
            a, b = zr[n], zi[n]
            for u in range(group):
                acc[u] = acc[u] + (
                    wr[n, pl.ds(d + u, 1), :] * a - wi[n, pl.ds(d + u, 1), :] * b
                )
        for u in range(group):
            at = pl.ds(pl.multiple_of((d + u) * inner, inner), inner)
            k_ref[at, :] = acc[u].astype(BF16)
        return carry

    lax.fori_loop(0, outer // group, rows, 0)


def power_scratch(modes, inner, outer):
    return (
        [pltpu.VMEM((modes, inner, LANES), F32)] * 2
        + [pltpu.VMEM((modes, outer, LANES), F32)] * 2
        + [pltpu.VMEM((20, modes, LANES), F32)]
    )


def moments_block(packed_ref, log_dt_ref, g_ref, out_ref, zr, zi, wr, wi, tmp, sums):
    step, rate, freq, c_real, c_imag, z = split_params(packed_ref, log_dt_ref)
    inner, outer = zr.shape[1], wr.shape[1]
    z_inner = fill_powers(z, inner, zr, zi, tmp)
    fill_powers(z_inner, outer, wr, wi, tmp)
    modes = c_real.shape[0]
    pos = lax.broadcasted_iota(jnp.int32, (inner, LANES), 0).astype(F32)

    def mode(n, carry):
        zero = jnp.zeros((inner, LANES), F32)
        sr, si, tr, ti = zero, zero, zero, zero
        for d in reversed(range(outer)):
            v = g_ref[d * inner : (d + 1) * inner, :]
            sr = sr + v * wr[n, d : d + 1, :]
            si = si + v * wi[n, d : d + 1, :]
            if d > 0:
                tr = tr + sr
                ti = ti + si
        zn = (zr[n], zi[n])
        first = cmul(zn, (sr, si))
        second = cmul(zn, (pos * sr + float(inner) * tr, pos * si + float(inner) * ti))
        for j, v in enumerate(first + second):
            sums[j, pl.ds(n, 1), :] = jnp.sum(v, axis=0, keepdims=True)
        return carry

    lax.fori_loop(0, modes, mode, 0)
    scale = 2.0 * step
    real_grad, imag_grad = scale * sums[0], -scale * sums[1]
    slope_r = scale * (c_real * sums[2] - c_imag * sums[3])
    slope_i = scale * (c_real * sums[3] + c_imag * sums[2])
    log_a_grad = -step * rate * slope_r
    freq_grad = -step * slope_i
    log_dt_grad = jnp.sum(
        c_real * real_grad + c_imag * imag_grad + log_a_grad + freq * freq_grad,
        axis=0, keepdims=True,
    )
    for i, part in enumerate((log_a_grad, freq_grad, real_grad, imag_grad)):
        out_ref[i * modes : (i + 1) * modes, :] = part
    top = 4 * modes
    row = lax.broadcasted_iota(jnp.int32, (8, LANES), 0)
    out_ref[top : top + 8, :] = jnp.where(row == 0, log_dt_grad, 0.0)


def gelu_both(v):
    sq = v * v
    th = jnp.tanh(v * (GELU_A + (GELU_A * GELU_B) * sq))
    rise = 0.5 + 0.5 * th
    slope = rise + v * (0.5 - 0.5 * th * th) * (GELU_A + (3.0 * GELU_A * GELU_B) * sq)
    return v * rise, slope


def gelu(v):
    return gelu_both(v)[0]


def gelu_slope(v):
    return gelu_both(v)[1]


def dot(a, b):
    return jnp.dot(a, b, preferred_element_type=F32)


def conv_block(x, k, skip, fwd_ref, inv_ref, mixed_ref, act_ref, xs_ref, ks_ref, ys):
    n = x.shape[0]
    for i in range(n // DFT_ROWS):
        re = pl.ds(i * DFT_ROWS, DFT_ROWS)
        im = pl.ds(n + i * DFT_ROWS, DFT_ROWS)
        xr, xi = dot(fwd_ref[re, :], x), dot(fwd_ref[im, :], x)
        kr, ki = dot(fwd_ref[re, :], k), dot(fwd_ref[im, :], k)
        xs_ref[re, :] = xr.astype(BF16)
        xs_ref[im, :] = xi.astype(BF16)
        ks_ref[re, :] = kr.astype(BF16)
        ks_ref[im, :] = ki.astype(BF16)
        ys[re, :] = (xr * kr - xi * ki).astype(BF16)
        ys[im, :] = (xr * ki + xi * kr).astype(BF16)
    y = ys[...]
    for i in range(n // TOKEN_ROWS):
        at = pl.ds(i * TOKEN_ROWS, TOKEN_ROWS)
        mixed = dot(inv_ref[at, :], y) + skip * x[i * TOKEN_ROWS : (i + 1) * TOKEN_ROWS].astype(F32)
        mixed_ref[at, :] = mixed
        act_ref[at, :] = gelu(mixed).astype(BF16)


def front_body(
    inputs, cot, counts, gains, log_dt, skip, log_a, freq, c_real, c_imag, fwd_hbm, inv_hbm,
    w_value, w_gate, w_in, w_out,
    packed_ref, vec_ref, skip_ref, grad_ref, x_out, mixed_out, act_out, xs_out, ks_out,
    value_out, sig_out, residual_out, n2_out, n2t_out,
    value_direct, value_via, gate_direct, gate_via, in_direct, in_via, out_direct, out_via,
    zr, zi, wr, wi, tmp, fwd, inv, packed, vec, got_vec, nx, k, mixed, act, xs, ks, ys,
    owns, fars, values, gates, value_s, sig_s, residual_s, n2_s, n2t_s,
    local, send, recv, *, bits
):
    posts = Posts(bits, send, recv)
    core, side = lax.axis_index("core"), lax.axis_index("tensor")
    half = packed.shape[2]
    modes = log_a.shape[0]
    posts.greet([0, 1, "core", "tensor"])
    tables = [
        pltpu.make_async_copy(src, dst, local.at[i])
        for i, (src, dst) in enumerate(
            ((fwd_hbm, fwd), (inv_hbm, inv), (w_value, owns.at[0]), (w_gate, owns.at[1]))
        )
    ]
    for copy in tables:
        copy.start()
    mine = pl.ds(pl.multiple_of(core * half, half), half)
    for i, ref in enumerate((log_a, freq, c_real, c_imag)):
        packed[1, i * modes : (i + 1) * modes, :] = ref[:, mine]
    vec[0:1, :] = log_dt[...]
    vec[1:2, :] = skip[...]
    posts.meet(4)

    def exchange(src, dst, link):
        slot = posts.slot()
        posts.post(src, dst, slot, link)
        return lambda: posts.await_(dst, slot, link)

    params_come = [
        exchange(packed.at[1], packed.at[0], "tensor"), exchange(vec, got_vec, "tensor")
    ]
    rows = value_direct.shape[0] // 4
    place = 2 * posts.bit(1) + posts.bit(0)

    def quarter(at, part=None):
        first, count = (0, rows) if part is None else (part * (rows // 2), rows // 2)
        return pl.ds(pl.multiple_of(at * rows + first, rows // 2), count)

    def cols(count):
        return pl.ds(pl.multiple_of(core * count, count), count)

    near, up, across = (place + 1 - 2 * posts.bit(0)), (place + 2 - 4 * posts.bit(1)), 3 - place
    out_row = pl.multiple_of(core * (4 * rows) + place * rows, rows)
    sources = [
        [(w_value.at[quarter(place), cols(half)], value_direct, value_via),
         (w_gate.at[quarter(place), cols(half)], gate_direct, gate_via)],
        [(w_in.at[quarter(place), cols(in_direct.shape[1])], in_direct, in_via)],
        [(w_out.at[pl.ds(out_row, rows), :], out_direct, out_via)],
    ]

    def fetch_steps(items):
        slots = []
        for src, direct, via in items:
            took = [posts.slot() for _ in range(9)]
            slots.append(took)
            posts.post(src, direct.at[quarter(place)], took[0], "tensor")
        yield
        for (src, direct, via), took in zip(items, slots):
            own = direct.at[quarter(place)]
            posts.await_(own, took[0], "tensor")
            posts.post(own, own, took[1], 0)
            posts.post(own, own, took[2], 1)
            posts.post(own, via.at[quarter(place)], took[5], "core")
        yield
        for (src, direct, via), took in zip(items, slots):
            for link, at, slot, on, over, piece in (
                (0, near, 1, 3, 1, 0), (1, up, 2, 4, 0, 1)
            ):
                come = direct.at[quarter(at)]
                posts.await_(come, took[slot], link)
                passed = direct.at[quarter(at, piece)]
                posts.post(passed, passed, took[on], over)
                posts.post(come, via.at[quarter(at)], took[5 + slot], "core")
        yield
        for (src, direct, via), took in zip(items, slots):
            for slot, link, piece in ((3, 1, 0), (4, 0, 1)):
                posts.await_(direct.at[quarter(across, piece)], took[slot], link)
            come = direct.at[quarter(across)]
            posts.post(come, via.at[quarter(across)], took[8], "core")
        yield
        for (src, direct, via), took in zip(items, slots):
            for at, slot in ((place, 5), (near, 6), (up, 7), (across, 8)):
                posts.await_(via.at[quarter(at)], took[slot], "core")

    flows = [fetch_steps(items) for items in sources]
    for flow in flows:
        next(flow)

    def kernel_of(j, log_dt, between=lambda: None):
        for i in range(half // LANES):
            if i:
                between()
            at = pl.ds(i * LANES, LANES)
            kernel_block(packed.at[1 - j, :, at], log_dt.at[:, at], k.at[2 * j, :, at], zr, zi, wr, wi, tmp)

    vec_ref[1] = vec[0:1, mine]
    kernel_of(0, vec_ref.at[1])
    kernels_come = [exchange(k.at[0], k.at[1], "core")]
    for come in params_come:
        come()
    vec_ref[0] = got_vec[0:1, mine]
    kernel_of(1, vec_ref.at[0], lambda: next(flows[0]))
    kernels_come.append(exchange(k.at[2], k.at[3], "core"))
    for i in range(nx.shape[0] // TOKEN_ROWS):
        at = pl.ds(i * TOKEN_ROWS, TOKEN_ROWS)
        source = inputs[at, :].astype(F32)
        nx[at, :] = norm_forward(source, gains[0:1, :], gains[1:2, :])[0].astype(BF16)
    used = (side < counts[0]).astype(F32)
    grad_ref[...] = (used * cot[...].astype(F32)).astype(BF16)
    width = vec.shape[1]
    for ref, at in ((vec, side), (got_vec, 1 - side)):
        skip_ref[:, pl.ds(pl.multiple_of(at * width, width), width)] = ref[1:2, :]
    stores = [
        pltpu.make_async_copy(nx, x_out, local.at[4]),
        pltpu.make_async_copy(packed, packed_ref, local.at[5]),
    ]
    for copy in stores:
        copy.start()
    for copy in tables:
        copy.wait()
    next(flows[0])
    next(flows[1])
    plan = ((0, None), (2, flows[2]), (1, flows[1]), (3, flows[0]))
    for n, (j, flow) in enumerate(plan):
        there = lax.rem(side + j // 2, 2)
        which = lax.rem(core + j % 2, 2)
        at = pl.ds(pl.multiple_of((2 * there + which) * half, half), half)
        if j % 2:
            kernels_come[j // 2]()
        params = vec if j < 2 else got_vec
        skip = params[1:2, pl.ds(pl.multiple_of(which * half, half), half)]
        conv_block(
            nx[:, at], k[j], skip, fwd, inv, mixed.at[j], act.at[:, at], xs.at[j], ks.at[j], ys
        )
        for i, (src, dst) in enumerate(
            ((mixed.at[j], mixed_out.at[j]), (xs.at[j], xs_out.at[j]), (ks.at[j], ks_out.at[j]))
        ):
            copy = pltpu.make_async_copy(src, dst, local.at[6 + 3 * j + i])
            copy.start()
            stores.append(copy)
        if flow is not None:
            next(flow)
    next(flows[0], None)
    loads = [
        pltpu.make_async_copy(src, fars.at[i], local.at[18 + i])
        for i, src in enumerate((value_direct, value_via, gate_direct, gate_via))
    ]
    for copy in loads:
        copy.start()
    stores.append(pltpu.make_async_copy(act, act_out, local.at[22]))
    stores[-1].start()
    for copy in loads:
        copy.wait()
    services = {0: [flows[2]], 1: [flows[1]], 2: [], 3: []}
    for r in range(nx.shape[0] // TOKEN_ROWS):
        at = pl.ds(r * TOKEN_ROWS, TOKEN_ROWS)
        left = act[at, :]
        project_all(left, owns.at[0], fars.at[0], fars.at[1], values)
        project_all(left, owns.at[1], fars.at[2], fars.at[3], gates)
        value = values[...]
        sig = 1.0 / (1.0 + jnp.exp(-gates[...]))
        value_s[r] = value.astype(BF16)
        sig_s[r] = sig.astype(BF16)
        residual = inputs[at, :].astype(F32) + (value * sig).astype(BF16).astype(F32)
        residual_s[r] = residual
        n2 = norm_forward(residual, gains[2:3, :], gains[3:4, :])[0].astype(BF16)
        n2_s[r] = n2
        n2t_s[r] = n2.T
        for i, (src, dst) in enumerate((
            (value_s, value_out.at[at]), (sig_s, sig_out.at[at]), (residual_s, residual_out.at[at]),
            (n2_s, n2_out.at[at]), (n2t_s, n2t_out.at[:, at]),
        )):
            copy = pltpu.make_async_copy(src.at[r], dst, local.at[23 + 5 * r + i])
            copy.start()
            stores.append(copy)
        for flow in services[r]:
            next(flow)
    for flow in (flows[1], flows[2], flows[2]):
        next(flow, None)
    for copy in stores:
        copy.wait()
    posts.finish()


def front_kernel(
    inputs, cot, counts, gains, log_dt, skip, log_a, freq, c_real, c_imag, fwd, inv,
    w_value, w_gate, w_in, w_out,
):
    bits = log2_of(lax.axis_size("pair"))
    n, d = inputs.shape
    modes = log_a.shape[0]
    half = d // 4
    units = w_in.shape[1] // 2
    chunks = n // TOKEN_ROWS
    vmem = pl.BlockSpec(memory_space=pltpu.VMEM)
    hbm = pl.BlockSpec(memory_space=pl.ANY)
    shape = jax.ShapeDtypeStruct
    return pl.pallas_call(
        functools.partial(front_body, bits=bits),
        in_specs=[vmem] * 2 + [pl.BlockSpec(memory_space=pltpu.SMEM)] + [vmem] * 7 + [hbm] * 6,
        out_specs=[hbm, vmem, vmem, vmem] + [hbm] * 18,
        out_shape=[
            shape((2, 4 * modes, half), F32), shape((2, 1, half), F32), shape((1, d), F32),
            shape((n, d), BF16), shape((n, d), BF16), shape((4, n, half), F32), shape((n, d), BF16),
            shape((4, 2 * n, half), BF16), shape((4, 2 * n, half), BF16),
            shape((n, d), BF16), shape((n, d), BF16), shape((n, d), F32), shape((n, d), BF16),
            shape((d, n), BF16),
        ]
        + [shape((d, half), BF16)] * 4
        + [shape((d, units), BF16)] * 2
        + [shape((units, d), BF16)] * 2,
        scratch_shapes=power_scratch(modes, KERNEL_INNER, n // KERNEL_INNER)
        + [
            pltpu.VMEM(fwd.shape, BF16), pltpu.VMEM(inv.shape, BF16),
            pltpu.VMEM((2, 4 * modes, half), F32),
            pltpu.VMEM((2, d // 2), F32), pltpu.VMEM((2, d // 2), F32),
            pltpu.VMEM((n, d), BF16), pltpu.VMEM((4, n, half), BF16),
            pltpu.VMEM((4, n, half), F32), pltpu.VMEM((n, d), BF16),
            pltpu.VMEM((4, 2 * n, half), BF16), pltpu.VMEM((4, 2 * n, half), BF16),
            pltpu.VMEM((2 * n, half), BF16),
            pltpu.VMEM((2, d, 2 * half), BF16), pltpu.VMEM((4, d, half), BF16),
            pltpu.VMEM((TOKEN_ROWS, d), F32), pltpu.VMEM((TOKEN_ROWS, d), F32),
            pltpu.VMEM((chunks, TOKEN_ROWS, d), BF16), pltpu.VMEM((chunks, TOKEN_ROWS, d), BF16),
            pltpu.VMEM((chunks, TOKEN_ROWS, d), F32), pltpu.VMEM((chunks, TOKEN_ROWS, d), BF16),
            pltpu.VMEM((chunks, d, TOKEN_ROWS), BF16),
            pltpu.SemaphoreType.DMA((24 + 5 * chunks,)),
            pltpu.SemaphoreType.DMA((40,)), pltpu.SemaphoreType.DMA((40,)),
        ],
        compiler_params=params_of(collective_id=5, has_side_effects=True),
        name="front_kernel",
    )(
        inputs, cot, counts, gains, log_dt, skip, log_a, freq, c_real, c_imag, fwd, inv,
        w_value, w_gate, w_in, w_out,
    )


def conv_back_block(ga, mixed, x, xs, ks, skip, fwd, inv, gm, gy, ax, ak, put_gn, put_gk):
    n = x.shape[0]
    total = jnp.zeros((1, x.shape[1]), F32)
    for i in range(n // TOKEN_ROWS):
        at = pl.ds(i * TOKEN_ROWS, TOKEN_ROWS)
        v = ga[at, :] * gelu_slope(mixed[at, :])
        gm[at, :] = v
        gy[at, :] = v.astype(BF16)
        total += jnp.sum(v * x[at, :].astype(F32), axis=0, keepdims=True)
    g = gy[...]
    for i in range(n // DFT_ROWS):
        re = pl.ds(i * DFT_ROWS, DFT_ROWS)
        im = pl.ds(n + i * DFT_ROWS, DFT_ROWS)
        gr, gi = dot(fwd[re, :], g), dot(fwd[im, :], g)
        for src, dst in ((ks, ax), (xs, ak)):
            a, b = src[re, :].astype(F32), src[im, :].astype(F32)
            dst[re, :] = (a * gr + b * gi).astype(BF16)
            dst[im, :] = (a * gi - b * gr).astype(BF16)
    yx = ax[...]
    yk = ak[...]
    for i in range(n // TOKEN_ROWS):
        at = pl.ds(i * TOKEN_ROWS, TOKEN_ROWS)
        put_gk(at, dot(inv[at, :], yk))
        put_gn(at, dot(inv[at, :], yx) + skip * gm[at, :])
    return total


def project_all(left, own, direct, via, out):
    core, side = lax.axis_index("core"), lax.axis_index("tensor")
    width = direct.shape[1]
    far = (1 - side) * 2 * width
    for ref, first, count in (
        (own, side * 2 * width, 2 * width), (direct, far + core * width, width),
        (via, far + (1 - core) * width, width),
    ):
        out[:, pl.ds(pl.multiple_of(first, width), count)] = dot(left, ref[...])


def glu_back_body(
    g_far, g_own, residual, cot, value, sig, act, value_own, value_direct, value_via,
    gate_own, gate_direct, gate_via, gains,
    there_keep, there_come, in_box, here_out, out_come,
    resid_ref, ga_ref, gain_ref, bias_ref, there_ref, here_ref, in_x, in_y, out_z,
    gv, gt, mine, theirs, in_a, in_b, out_a, out_b, out_box, local, send, recv, *, bits
):
    step = pl.program_id(0)
    posts = Posts(bits, send, recv)
    links = [0, 1, "core", "tensor"]
    slots = {name: posts.slot() for name in ("x", "y", "z")}
    swap = [posts.slot(), posts.slot()]

    def transfers():
        return [
            posts.copy(in_box, in_x, slots["x"], 0),
            posts.copy(in_a, in_y, slots["y"], "tensor"),
            posts.copy(out_box, out_z, slots["z"], 1),
        ]

    @pl.when(step == 0)
    def _():
        posts.greet(links)
        other = 1 - posts.bit(1)
        loads = [
            pltpu.make_async_copy(src, dst, local.at[i])
            for i, (src, dst) in enumerate((
                (there_keep, in_a), (there_come, in_b),
                (here_out.at[:, other], out_a), (out_come.at[:, other], out_b),
            ))
        ]
        for copy in loads:
            copy.start()
        posts.meet(len(links))
        sends = transfers()
        sends[0].start()
        for copy in loads[:2]:
            copy.wait()
        in_a[...] = (in_a[...].astype(F32) + in_b[...].astype(F32)).astype(BF16)
        sends[1].start()
        for copy in loads[2:]:
            copy.wait()
        out_box[...] = (out_a[...] + out_b[...].astype(F32)).astype(BF16)
        sends[2].start()

    chunks = act.shape[0] // TOKEN_ROWS
    width = gv.shape[2]

    @pl.when(step < chunks)
    def _():
        standard, inv_std = norm_forward(residual[...], 1.0, 0.0)[1:]
        part, gain_grad, bias_grad = norm_backward(
            g_far[...] + g_own[...], standard, inv_std, gains[2:3, :]
        )
        new = step == 0
        gain_ref[...] = jnp.where(new, 0.0, gain_ref[...]) + gain_grad[None]
        bias_ref[...] = jnp.where(new, 0.0, bias_ref[...]) + bias_grad[None]
        resid = cot[...].astype(F32) + part
        resid_ref[...] = resid
        grad = resid.astype(BF16).astype(F32)
        gate = sig[...].astype(F32)
        grad_value = (grad * gate).astype(BF16)
        grad_gate = (grad * value[...].astype(F32) * gate * (1.0 - gate)).astype(BF16)
        at = pl.ds(pl.multiple_of(step * TOKEN_ROWS, TOKEN_ROWS), TOKEN_ROWS)
        for i in range(gv.shape[0]):
            gv[i, at, :] = grad_value[:, i * width : (i + 1) * width]
            gt[i, at, :] = grad_gate[:, i * width : (i + 1) * width]
        core, side = lax.axis_index("core"), lax.axis_index("tensor")
        far = 2 * (1 - side)
        total = 0.0
        for grads, own, direct, via in (
            (gv, value_own, value_direct, value_via), (gt, gate_own, gate_direct, gate_via)
        ):
            ours = jnp.concatenate([grads[2 * side, at, :], grads[2 * side + 1, at, :]], axis=1)
            total += contract_cols(ours, own[...])
            total += contract_cols(grads[far + core, at, :], direct[...])
            total += contract_cols(grads[far + 1 - core, at, :], via[...])
        ga_ref[...] = total

    @pl.when(step >= chunks)
    def _():
        j = step - chunks
        side = lax.rem(lax.axis_index("tensor") + 1 + j, 2)
        half = lax.rem(lax.axis_index("core") + 1 + j // 2, 2)
        block = 2 * side + half
        grads = [contract_rows(act[...], gv[block]), contract_rows(act[...], gt[block])]
        for slot in range(2):
            @pl.when(j == slot)
            def _():
                for i, g in enumerate(grads):
                    mine[slot, :, i * width : (i + 1) * width] = g.astype(BF16)
                posts.copy(mine.at[slot], theirs.at[slot], swap[slot], "core").start()

        @pl.when(j == 2)
        def _():
            posts.await_(theirs.at[0], swap[0], "core")
            for i, g in enumerate(grads):
                at = pl.ds(i * width, width)
                there_ref[:, at] = (g + theirs[0, :, at].astype(F32)).astype(BF16)

        @pl.when(j == 3)
        def _():
            posts.await_(theirs.at[1], swap[1], "core")
            for i, g in enumerate(grads):
                at = pl.ds(i * width, width)
                here_ref[:, at] = g + theirs[1, :, at].astype(F32)
            for slot in range(2):
                posts.copy(mine.at[slot], theirs.at[slot], swap[slot], "core").wait_send()
            for copy in transfers():
                copy.wait()


def glu_back_kernel(
    g_far, g_own, residual, cot, value, sig, act, weights, gains,
    there_keep, there_come, in_box, here_out, out_come,
):
    bits = log2_of(lax.axis_size("pair"))
    n, d = act.shape
    chunks = n // TOKEN_ROWS
    width = d // 4
    hbm = pl.BlockSpec(memory_space=pl.ANY)
    extra = (there_keep, there_come, in_box, here_out, out_come)
    split = (here_out.shape[0],) + here_out.shape[2:]

    def whole(a):
        return pl.BlockSpec(a.shape, lambda i: (0, 0), pipeline_mode=pl.Buffered(1))

    rows = pl.BlockSpec((TOKEN_ROWS, d), lambda i: (jnp.minimum(i, chunks - 1), 0))
    vector = pl.BlockSpec((1, d), lambda i: (0, 0))
    weight = pl.BlockSpec((d, 2 * width), lambda i: (0, 0))
    return pl.pallas_call(
        functools.partial(glu_back_body, bits=bits),
        grid=(chunks + 4,),
        in_specs=[rows] * 6 + [whole(act)] + [whole(w) for w in weights] + [whole(gains)] + [hbm] * 5,
        out_specs=[rows, rows, vector, vector, weight, weight] + [hbm] * 3,
        scratch_shapes=[pltpu.VMEM((4, n, width), BF16)] * 2
        + [pltpu.VMEM((2, d, 2 * width), BF16)] * 2
        + [pltpu.VMEM(there_keep.shape, BF16)] * 2
        + [pltpu.VMEM(split, F32), pltpu.VMEM(split, BF16), pltpu.VMEM(split, BF16)]
        + [pltpu.SemaphoreType.DMA((4,))]
        + [pltpu.SemaphoreType.DMA((5,))] * 2,
        out_shape=[
            jax.ShapeDtypeStruct((n, d), F32), jax.ShapeDtypeStruct((n, d), F32),
            jax.ShapeDtypeStruct((1, d), F32), jax.ShapeDtypeStruct((1, d), F32),
            jax.ShapeDtypeStruct((d, 2 * width), BF16), jax.ShapeDtypeStruct((d, 2 * width), F32),
            jax.ShapeDtypeStruct(in_box.shape, BF16), jax.ShapeDtypeStruct(in_box.shape, BF16),
            jax.ShapeDtypeStruct(split, BF16),
        ],
        compiler_params=params_of(collective_id=2, has_side_effects=True),
        name="glu_back_kernel",
    )(g_far, g_own, residual, cot, value, sig, act, *weights, gains, *extra)


def ffn_body(
    n2, n2t, gl, ia, ib, oa, ob, ffn, gn2, box_ref, keep_ref, out_ref,
    wi, wo, h, gp, total, in_mine, out_mine, in_theirs, out_theirs, send, recv,
):
    step, half = pl.program_id(0), in_mine.shape[0]
    first = step < half
    cores = CoreExchange([(in_mine, in_theirs), (out_mine, out_theirs)], send, recv)
    pl.when(step == 0)(cores.greet)

    @pl.when(first)
    def _():
        wi[...] = ia[...]
        wo[...] = oa[...]

    @pl.when(jnp.logical_not(first))
    def _():
        wi[...] = ib[...]
        wo[...] = ob[...]

    @pl.when(step == 0)
    def _():
        ffn[...] = jnp.zeros_like(ffn)
        gn2[...] = jnp.zeros_like(gn2)

    w1, w2 = wi[...], wo[...]
    for r in range(n2.shape[0] // TOKEN_ROWS):
        at = pl.ds(r * TOKEN_ROWS, TOKEN_ROWS)
        act, slope = gelu_both(dot(n2[at, :], w1))
        hidden = act.astype(BF16)
        grad_pre = (contract_cols(gl[at, :], w2) * slope).astype(BF16)
        h[at, :] = hidden
        gp[at, :] = grad_pre
        ffn[at, :] += dot(hidden, w2)
        gn2[at, :] += contract_cols(grad_pre, w1)
    out_grad = contract_rows(h[...], gl[...])
    in_grad = dot(n2t[...], gp[...])

    pl.when(step == 0)(cores.meet)

    @pl.when(first)
    def _():
        in_mine[step] = in_grad.astype(BF16)
        out_mine[step] = out_grad.astype(BF16)
        cores.start(step)

    @pl.when(jnp.logical_not(first))
    def _():
        cores.arrived(step - half)
        total[...] = in_grad + in_theirs[step - half].astype(F32)
        near, rows = lax.rem(lax.axis_index("pair"), 2), keep_ref.shape[0]
        for ref, at in ((keep_ref, near), (box_ref, 1 - near)):
            part = pl.ds(pl.multiple_of(at * rows, rows), rows)
            ref[...] = total[part, :].astype(ref.dtype)
        out_ref[...] = (out_grad + out_theirs[step - half].astype(F32)).astype(out_ref.dtype)

    @pl.when(step == 2 * half - 1)
    def _():
        cores.sent(half)


def ffn_kernel(n2, n2t, gl, ins, outs, units, own):
    n, d = n2.shape
    half = units // FFN_TILE

    def whole(a):
        return pl.BlockSpec(a.shape, lambda s: (0, 0), pipeline_mode=pl.Buffered(1))

    def fst(s):
        at = jnp.minimum(s, half - 1)
        return at + (1 - lax.axis_index("core")) * half if own else at

    def snd(s):
        at = jnp.maximum(s - half, 0)
        return at + lax.axis_index("core") * half if own else at

    total = pl.BlockSpec((n, d), lambda s: (0, 0))
    dtype = F32 if own else BF16
    return pl.pallas_call(
        ffn_body,
        grid=(2 * half,),
        in_specs=[
            whole(n2), whole(n2t), whole(gl),
            pl.BlockSpec((d, FFN_TILE), lambda s: (0, fst(s))),
            pl.BlockSpec((d, FFN_TILE), lambda s: (0, snd(s))),
            pl.BlockSpec((FFN_TILE, d), lambda s: (fst(s), 0)),
            pl.BlockSpec((FFN_TILE, d), lambda s: (snd(s), 0)),
        ],
        out_specs=[
            total, total,
            pl.BlockSpec((d // 2, FFN_TILE), lambda s: (0, jnp.maximum(s - half, 0))),
            pl.BlockSpec((d // 2, FFN_TILE), lambda s: (0, jnp.maximum(s - half, 0))),
            pl.BlockSpec((FFN_TILE, d), lambda s: (jnp.maximum(s - half, 0), 0)),
        ],
        scratch_shapes=[
            pltpu.VMEM((d, FFN_TILE), BF16), pltpu.VMEM((FFN_TILE, d), BF16),
            pltpu.VMEM((n, FFN_TILE), BF16), pltpu.VMEM((n, FFN_TILE), BF16),
            pltpu.VMEM((d, FFN_TILE), F32),
        ]
        + [pltpu.VMEM((half, d, FFN_TILE), BF16), pltpu.VMEM((half, FFN_TILE, d), BF16)] * 2
        + exchange_sems(2, half),
        out_shape=[
            jax.ShapeDtypeStruct((n, d), F32), jax.ShapeDtypeStruct((n, d), F32),
            jax.ShapeDtypeStruct((d // 2, units), BF16), jax.ShapeDtypeStruct((d // 2, units), dtype),
            jax.ShapeDtypeStruct((units, d), dtype),
        ],
        compiler_params=params_of(collective_id=int(own), has_side_effects=True),
        name="ffn_kernel",
    )(n2, n2t, gl, *ins, *outs)


def norm_forward(values, norm_gain, norm_bias):
    center = values - jnp.mean(values, axis=-1, keepdims=True)
    inv_std = lax.rsqrt(jnp.mean(center * center, axis=-1, keepdims=True) + norm_eps)
    standard = center * inv_std
    return (standard * norm_gain + norm_bias, standard, inv_std)


def norm_backward(incoming, standard, inv_std, norm_gain):
    scaled = incoming * norm_gain
    value_grad = inv_std * (
        scaled
        - jnp.mean(scaled, axis=-1, keepdims=True)
        - standard * jnp.mean(scaled * standard, axis=-1, keepdims=True)
    )
    return (value_grad, jnp.sum(incoming * standard, axis=0), jnp.sum(incoming, axis=0))


def contract_rows(left, right):
    return lax.dot_general(left, right, (((0,), (0,)), ((), ())), preferred_element_type=F32)


def contract_cols(left, right):
    return lax.dot_general(left, right, (((1,), (1,)), ((), ())), preferred_element_type=F32)


def scatter_steps(posts, acc, bits, order, boxes, come):
    def at(known, flipped):
        place = 0
        for i, b in enumerate(bits):
            here = posts.bit(b)
            if b in known:
                bit = 1 - here if known[b] else here
            else:
                bit = flipped >> i & 1
            place = place + bit * (1 << i)
        return place

    done = {}
    used = 0
    for n, b in enumerate(order):
        rest = [bits.index(i) for i in order[n + 1 :]]
        combos = [sum((c >> k & 1) << i for k, i in enumerate(rest)) for c in range(1 << len(rest))]
        slots = []
        for c, combo in enumerate(combos):
            slot = posts.slot()
            boxes[used + c] = acc[at({**done, b: True}, combo)].astype(BF16)
            posts.post(boxes.at[used + c], come.at[used + c], slot, b)
            slots.append(slot)
        yield
        done[b] = False
        for c, combo in enumerate(combos):
            posts.await_(come.at[used + c], slots[c], b)
            keep = at(done, combo)
            acc[keep] = acc[keep] + come[used + c].astype(F32)
        used += len(combos)
    posts.result = at(done, 0)


def gather_steps(posts, own, whole, local, order):
    core = lax.axis_index("core")
    count = 1 << posts.bits
    slots = {(rel, link): posts.slot() for rel in range(count) for link in ("bit", "core")}
    first = pltpu.make_async_copy(own, whole.at[core, posts.block(0)], local)
    first.start()

    def pass_on(src, rel, bits):
        dst = whole.at[core, posts.block(rel)]
        for b in bits:
            posts.post(src, dst, slots[rel ^ (1 << b), "bit"], b)
        posts.post(src, dst, slots[rel, "core"], "core")

    pass_on(own, 0, order)
    for n, b in enumerate(order):
        for c in range(1 << n):
            yield
            rel = sum((c >> k & 1) << order[k] for k in range(n)) | 1 << b
            block = whole.at[core, posts.block(rel)]
            posts.await_(block, slots[rel, "bit"], b)
            pass_on(block, rel, order[n + 1 :])
    yield
    first.wait()
    for rel in range(count):
        posts.await_(whole.at[1 - core, posts.block(rel)], slots[rel, "core"], "core")


def back_body(
    ga_hbm, mixed_hbm, x_hbm, xs_hbm, ks_hbm, fwd_hbm, inv_hbm, source_hbm, resid_hbm,
    in_keep, in_x, in_y, out_keep, out_come, out_z, glu_keep, glu_box,
    skip, gains, gain2, bias2, packed, log_dt,
    input_ref, in_all, out_all, glu_all, small_all,
    ga, fwd, inv, mixed, x, xs, ks, gm, gy, ax, ak, gk, gk_mine, gk_theirs, source, resid, staged,
    zr, zi, wr, wi, tmp, sums, moments, rows, rows_mine, rows_other, rows_come,
    in_acc, in_a, in_b, out_acc, out_a, out_b, glu_acc, glu_come, in_own, out_own, glu_own,
    in_boxes, in_got, out_boxes, out_got, glu_boxes, glu_got, small, small_far, small_got,
    local, send, recv, *, bits
):
    posts = Posts(bits, send, recv)
    links = list(range(bits)) + ["core", "tensor"]
    posts.greet(links)
    core, side = lax.axis_index("core"), lax.axis_index("tensor")
    n, width = mixed.shape[1:]
    used = [3]

    def load(src, dst):
        copy = pltpu.make_async_copy(src, dst, local.at[used[0]])
        used[0] += 1
        copy.start()
        return copy

    def columns(i):
        there = lax.rem(side + 1 + i, 2)
        which = lax.rem(core + 1 + i // 2, 2)
        return pl.ds(pl.multiple_of((2 * there + which) * width, width), width)

    def load_block(i):
        j, slot = 2 * ((i + 1) % 2) + 1 - i // 2, i % 2
        return [
            load(mixed_hbm.at[j], mixed.at[slot]), load(x_hbm.at[:, columns(i)], x.at[slot]),
            load(xs_hbm.at[j], xs.at[slot]), load(ks_hbm.at[j], ks.at[slot]),
        ]

    mine = posts.bit(1)
    in_loads = [load(in_keep, in_acc), load(in_x, in_a), load(in_y, in_b)]
    out_loads = [
        load(out_keep.at[:, mine], out_acc), load(out_come.at[:, mine], out_a), load(out_z, out_b)
    ]
    ga_load = load(ga_hbm, ga)
    block_loads = load_block(0)
    tables = [load(fwd_hbm, fwd), load(inv_hbm, inv)]
    glu_load = load(glu_keep, glu_acc)
    posts.meet(len(links))
    near, far = list(range(1, bits)), list(range(2, bits))

    def in_steps():
        for copy in in_loads:
            copy.wait()
        in_acc[...] = in_acc[...] + in_a[...].astype(F32) + in_b[...].astype(F32)
        yield from scatter_steps(posts, in_acc, near, near, in_boxes, in_got)
        in_own[...] = in_acc[posts.result].astype(BF16)
        yield from gather_steps(posts, in_own, in_all, local.at[0], list(reversed(range(bits))))

    def out_steps():
        for copy in out_loads:
            copy.wait()
        out_acc[...] = out_acc[...] + out_a[...].astype(F32) + out_b[...].astype(F32)
        yield from scatter_steps(posts, out_acc, far + [0], [0] + far, out_boxes, out_got)
        out_own[...] = out_acc[posts.result].astype(BF16)
        yield from gather_steps(posts, out_own, out_all, local.at[1], list(reversed(range(bits))))

    def glu_steps():
        slot = posts.slot()
        posts.post(glu_box, glu_come, slot, "tensor")
        yield
        posts.await_(glu_come, slot, "tensor")
        glu_load.wait()
        glu_acc[...] = glu_acc[...] + glu_come[...].astype(F32)
        yield from scatter_steps(posts, glu_acc, near + [0], [0] + near, glu_boxes, glu_got)
        glu_own[...] = glu_acc[posts.result].astype(BF16)
        yield from gather_steps(posts, glu_own, glu_all, local.at[2], GLU_ORDER(bits))

    def small_steps():
        for j in range(2):
            for half, ref in ((core, rows_mine), (1 - core, rows_other)):
                there = lax.rem(side + 1 + j, 2)
                at = pl.multiple_of((2 * there + half) * width, width)
                ref[j] = rows[:, pl.ds(at, width)]
        slot = posts.slot()
        posts.post(rows_other, rows_come, slot, "core")
        yield
        posts.await_(rows_come, slot, "core")
        top = moments.shape[1]
        for j, ref in ((0, small_far), (1, small)):
            ref[:top, :] = moments[j]
            ref[top:, :] = rows_mine[j] + rows_come[j]
        slot = posts.slot()
        posts.post(small_far, small_got.at[0], slot, "tensor")
        yield
        posts.await_(small_got.at[0], slot, "tensor")
        small[...] = small[...] + small_got[0]
        for b in range(bits):
            slot = posts.slot()
            small_all[b] = small[...]
            posts.post(small_all.at[b], small_got.at[1 + b], slot, b)
            yield
            posts.await_(small_got.at[1 + b], slot, b)
            small[...] = small[...] + small_got[1 + b]
        slot = posts.slot()
        small_all[bits] = small[...]
        posts.post(small_all.at[bits], small_got.at[1 + bits], slot, "core")
        yield
        posts.await_(small_got.at[1 + bits], slot, "core")
        small_all[bits + 1] = small_got[1 + bits]

    flows = {"in": in_steps(), "out": out_steps(), "glu": glu_steps()}
    done = object()

    def advance(*names):
        for name in names:
            if name in flows and next(flows[name], done) is done:
                del flows[name]

    advance("glu", "in", "out")
    rows[...] = jnp.zeros_like(rows)
    rows[3:4, :] = gain2[...]
    rows[4:5, :] = bias2[...]
    ga_load.wait()
    slots = [posts.slot(), posts.slot()]
    for i in range(4):
        slot = i % 2
        for copy in block_loads:
            copy.wait()
        if i < 3:
            block_loads = load_block(i + 1)
        if i == 0:
            for copy in tables:
                copy.wait()
        at = columns(i)

        def put_gn(tokens, value, at=at):
            ga[tokens, at] = value

        def put_gk(tokens, value, i=i):
            if i < 2:
                gk_mine[i, tokens, :] = value.astype(BF16)
            else:
                gk[i - 2, tokens, :] = value

        rows[0:1, at] = conv_back_block(
            ga.at[:, at], mixed.at[slot], x.at[slot], xs.at[slot], ks.at[slot], skip[:, at],
            fwd, inv, gm, gy, ax, ak, put_gn, put_gk,
        )
        if i < 2:
            posts.post(gk_mine.at[i], gk_theirs.at[i], slots[i], "core")
        else:
            posts.await_(gk_theirs.at[i - 2], slots[i - 2], "core")
            gk[i - 2] = gk[i - 2] + gk_theirs[i - 2].astype(F32)
        if i in BACK_ROUNDS:
            advance(*BACK_ROUNDS[i])

    chunks = n // TOKEN_ROWS

    def load_rows(r):
        at = pl.ds(r * TOKEN_ROWS, TOKEN_ROWS)
        return [load(source_hbm.at[at], source.at[r % 2]), load(resid_hbm.at[at], resid.at[r % 2])]

    row_loads = load_rows(0)
    stores = []
    for r in range(chunks):
        for copy in row_loads:
            copy.wait()
        if r + 1 < chunks:
            row_loads = load_rows(r + 1)
        at = pl.ds(r * TOKEN_ROWS, TOKEN_ROWS)
        standard, inv_std = norm_forward(source[r % 2].astype(F32), 1.0, 0.0)[1:]
        part, gain_grad, bias_grad = norm_backward(ga[at, :], standard, inv_std, gains[0:1, :])
        rows[1:2, :] = rows[1:2, :] + gain_grad[None]
        rows[2:3, :] = rows[2:3, :] + bias_grad[None]
        staged[r] = (resid[r % 2] + part).astype(BF16)
        stores.append(load(staged.at[r], input_ref.at[at]))
    advance(*BACK_ROUNDS["norm"])

    def block(j, i):
        at = pl.ds(i * LANES, LANES)
        moments_block(
            packed.at[j, :, at], log_dt.at[j, :, at], gk.at[j, :, at], moments.at[j, :, at],
            zr, zi, wr, wi, tmp, sums,
        )

    for j in range(2):
        for i in range(width // LANES):
            block(j, i)
            advance("in", "out", "glu")
    flows["small"] = small_steps()
    while flows:
        advance("small", "in", "out", "glu")
    for copy in stores:
        copy.wait()
    posts.finish()


def back_kernel(
    ga, mixed, x, xs, ks, fwd, inv, source, resid, in_keep, in_x, in_y, out_keep, out_come, out_z,
    glu_keep, glu_box, skip, gains, gain2, bias2, packed, log_dt,
):
    bits = log2_of(lax.axis_size("pair"))
    blocks = 1 << bits
    width, modes = packed.shape[2], packed.shape[1] // 4
    n, d = ga.shape
    block_rows, cols = glu_keep.shape[1:]
    kept = in_keep.shape[0]
    small_rows = 4 * modes + 8 + 8
    vmem = pl.BlockSpec(memory_space=pltpu.VMEM)
    hbm = pl.BlockSpec(memory_space=pl.ANY)
    big = pltpu.VMEM((block_rows, d), BF16)
    small = pltpu.VMEM((small_rows, width), F32)
    rows = pltpu.VMEM((2, 8, width), F32)
    copies = 3 * 2 * blocks + 2 * kept + blocks + bits + 12
    shape = jax.ShapeDtypeStruct
    return pl.pallas_call(
        functools.partial(back_body, bits=bits),
        in_specs=[hbm] * 17 + [vmem] * 6,
        out_specs=[hbm] * 4 + [vmem],
        out_shape=[
            shape((n, d), BF16), shape((2, blocks, block_rows, d), BF16),
            shape((2, blocks, block_rows, d), BF16), shape((2, blocks, block_rows, cols), BF16),
            shape((bits + 2, small_rows, width), F32),
        ],
        scratch_shapes=[
            pltpu.VMEM((n, d), F32), pltpu.VMEM(fwd.shape, BF16), pltpu.VMEM(inv.shape, BF16),
            pltpu.VMEM((2, n, width), F32), pltpu.VMEM((2, n, width), BF16),
            pltpu.VMEM((2, 2 * n, width), BF16), pltpu.VMEM((2, 2 * n, width), BF16),
            pltpu.VMEM((n, width), F32), pltpu.VMEM((n, width), BF16),
            pltpu.VMEM((2 * n, width), BF16), pltpu.VMEM((2 * n, width), BF16),
            pltpu.VMEM((2, n, width), F32), pltpu.VMEM((2, n, width), BF16),
            pltpu.VMEM((2, n, width), BF16),
            pltpu.VMEM((2, TOKEN_ROWS, d), BF16), pltpu.VMEM((2, TOKEN_ROWS, d), F32),
            pltpu.VMEM((n // TOKEN_ROWS, TOKEN_ROWS, d), BF16),
        ]
        + power_scratch(modes, MOMENT_INNER, n // MOMENT_INNER)
        + [
            pltpu.VMEM((4, modes, LANES), F32), pltpu.VMEM((2, 4 * modes + 8, width), F32),
            pltpu.VMEM((8, d), F32), rows, rows, rows,
            pltpu.VMEM(in_keep.shape, F32), pltpu.VMEM(in_keep.shape, BF16),
            pltpu.VMEM(in_keep.shape, BF16),
            pltpu.VMEM(in_keep.shape, F32), pltpu.VMEM(in_keep.shape, BF16),
            pltpu.VMEM(in_keep.shape, BF16),
            pltpu.VMEM(glu_keep.shape, F32), pltpu.VMEM(glu_keep.shape, BF16),
            big, big, pltpu.VMEM((block_rows, cols), BF16),
        ]
        + [pltpu.VMEM((kept - 1, block_rows, d), BF16)] * 4
        + [pltpu.VMEM((blocks - 1, block_rows, cols), BF16)] * 2
        + [small, small, pltpu.VMEM((bits + 2, small_rows, width), F32)]
        + [pltpu.SemaphoreType.DMA((48,))]
        + [pltpu.SemaphoreType.DMA((copies,))] * 2,
        compiler_params=params_of(collective_id=4, has_side_effects=True),
        name="back_kernel",
    )(
        ga, mixed, x, xs, ks, fwd, inv, source, resid, in_keep, in_x, in_y, out_keep, out_come, out_z,
        glu_keep, glu_box, skip, gains, gain2, bias2, packed, log_dt,
    )


def GLU_ORDER(bits):
    return list(reversed(range(bits)))


BACK_ROUNDS = {1: ("in", "out"), 3: ("glu", "in"), "norm": ("out", "in", "glu")}


def last_body(
    counts, residual, far, own, in_all, out_all, glu_all, small,
    output, in_total, out_total, value_total, gate_total, *rest, modes
):
    core, side = lax.axis_index("core"), lax.axis_index("tensor")
    used = (side < counts[0]).astype(F32)
    output[...] = (used * (residual[...] + (far[...] + own[...]))).astype(BF16)
    out_total[...] = out_all[...].astype(F32)
    width = in_all.shape[2]
    half = glu_all.shape[2] // 2
    for i in range(2):
        in_total[:, i * width : (i + 1) * width] = in_all[i].astype(F32)
        value_total[:, i * half : (i + 1) * half] = glu_all[i, :, :half].astype(F32)
        gate_total[:, i * half : (i + 1) * half] = glu_all[i, :, half:].astype(F32)

    @pl.when(pl.program_id(0) == 0)
    def _():
        count = small.shape[2]
        top = 4 * modes
        spans = [(i * modes, modes) for i in range(4)] + [(top + i, 1) for i in (0, 8, 9, 10, 11, 12)]
        for ref, (first, rows) in zip(rest, spans):
            for i, which in ((-2, core), (-1, 1 - core)):
                at = pl.ds(pl.multiple_of(which * count, count), count)
                ref[:, at] = small[small.shape[0] + i, first : first + rows, :]


def last_kernel(counts, residual, far, own, in_all, out_all, glu_all, small):
    n, d = residual.shape
    steps = 8
    modes = (small.shape[1] - 16) // 4
    units, cols, count = in_all.shape[2], glu_all.shape[2], 2 * small.shape[2]
    shape = jax.ShapeDtypeStruct

    def rows(count, width):
        return pl.BlockSpec((count // steps, width), lambda i: (i, 0))

    def pair(width):
        return pl.BlockSpec((2, d // steps, width), lambda i: (0, i, 0))

    def whole(shape):
        return pl.BlockSpec(shape, lambda i: (0,) * len(shape))

    sizes = [(modes, count)] * 4 + [(1, count)] * 6
    return pl.pallas_call(
        functools.partial(last_body, modes=modes),
        grid=(steps,),
        in_specs=[
            pl.BlockSpec(memory_space=pltpu.SMEM), rows(n, d), rows(n, d), rows(n, d),
            pair(units), rows(2 * units, d), pair(cols), whole(small.shape),
        ],
        out_specs=[rows(n, d), rows(d, 2 * units), rows(2 * units, d), rows(d, cols), rows(d, cols)]
        + [whole(size) for size in sizes],
        out_shape=[
            shape((n, d), BF16), shape((d, 2 * units), F32), shape((2 * units, d), F32),
            shape((d, cols), F32), shape((d, cols), F32),
        ]
        + [shape(size, F32) for size in sizes],
        compiler_params=params_of(),
        name="last_kernel",
    )(counts, residual, far, own, in_all, out_all, glu_all, small)


SWAP = ((0, 1), (1, 0))


def over_tensor(values):
    return lax.ppermute(values, "tensor", SWAP)


def over_pair(values, flip):
    size = lax.axis_size("pair")
    return lax.ppermute(values, "pair", [(p, p ^ flip) for p in range(size)])


def together(*values):
    return lax.optimization_barrier(values)


def shards(
    inputs, counts, ln1_gain, ln1_bias, log_dt, log_a, freq, c_real, c_imag, skip_gain,
    w_value, w_gate, ln2_gain, ln2_bias, w_in, w_out, cotangent,
):
    _, length, width = inputs.shape
    source = inputs.reshape(length, width)
    gains = jnp.stack([ln1_gain, ln1_bias, ln2_gain, ln2_bias]).astype(F32)
    table = transform_table(length)
    fwd = jnp.asarray(table.astype(ml_dtypes.bfloat16))
    inv = jnp.asarray(np.ascontiguousarray((table.T / length).astype(ml_dtypes.bfloat16)))
    (
        packed, log_dts, skip, grad_low, normed1, mixed, act, spectrum, kernel_spectrum,
        value_proj, gate_sig, residual, normed2, normed2_t,
        value_direct, value_via, gate_direct, gate_via, in_direct, in_via, out_direct, out_via,
    ) = front_kernel(
        source, cotangent.reshape(length, width), counts, gains, log_dt[None], skip_gain[None],
        log_a.T, freq.T, c_real.T, c_imag.T, fwd, inv, w_value, w_gate, w_in, w_out,
    )
    glu_weights = (w_value, value_direct, value_via, w_gate, gate_direct, gate_via)
    units = in_direct.shape[1]
    far_ffn, far_normed2, there_box, there_keep, there_out = ffn_kernel(
        normed2, normed2_t, grad_low, (in_via, in_direct), (out_via, out_direct), units, False
    )
    normed2, there_out, there_box = together(normed2, there_out, there_box)
    out_come, there_come = over_tensor(there_out), over_pair(there_box, 1)
    own_sums = ffn_kernel(normed2, normed2_t, grad_low, (w_in, w_in), (w_out, w_out), units, True)
    own_sums, out_come, there_come = together(own_sums, out_come, there_come)
    own_ffn, own_normed2, in_box, in_keep, here_out = own_sums
    blocks = lax.axis_size("pair")
    split = (blocks // 2, 2, width // blocks, width)
    here_out, out_come = here_out.reshape(split), out_come.reshape(split)
    (
        grad_residual, grad_act, gain_second_grad, bias_second_grad, there_glu, here_glu,
        in_x, in_y, out_z,
    ) = glu_back_kernel(
        far_normed2, own_normed2, residual, grad_low, value_proj, gate_sig, act, glu_weights, gains,
        there_keep, there_come, in_box, here_out, out_come,
    )
    halved = (blocks // 2, width // blocks, width)
    by_block = (blocks, width // blocks, -1)
    input_grad, in_all, out_all, glu_all, small = back_kernel(
        grad_act, mixed, normed1, spectrum, kernel_spectrum, fwd, inv, source, grad_residual,
        in_keep.reshape(halved), in_x.reshape(halved), in_y.reshape(halved),
        here_out, out_come, out_z, here_glu.reshape(by_block), there_glu.reshape(by_block),
        skip, gains, gain_second_grad, bias_second_grad, packed, log_dts,
    )
    (
        output, in_total, out_total, value_total, gate_total,
        log_a_grad, freq_grad, real_grad, imag_grad, *vectors,
    ) = last_kernel(
        counts, residual, far_ffn, own_ffn, in_all.reshape(2, width, -1), out_all.reshape(-1, width),
        glu_all.reshape(2, width, -1), small,
    )
    log_dt_grad, skip_grad, gain1, bias1, gain2, bias2 = (v.reshape(-1) for v in vectors)
    return (
        output.reshape(inputs.shape),
        input_grad.reshape(inputs.shape),
        gain1,
        bias1,
        log_dt_grad,
        log_a_grad.T,
        freq_grad.T,
        real_grad.T,
        imag_grad.T,
        skip_grad,
        value_total,
        gate_total,
        gain2,
        bias2,
        in_total,
        out_total,
    )


def solution(mesh):
    devices = mesh.devices
    cores = jax.sharding.Mesh(
        devices.reshape(devices.shape[0] // 2, 2, devices.shape[1]), ("pair", "core", "tensor")
    )
    batch, every = ("pair", "core"), ("pair", "core", "tensor")
    in_specs = (
        P(every, None, None), P(batch), P(), P(), P("tensor"), P("tensor", None), P("tensor", None),
        P("tensor", None), P("tensor", None), P("tensor"), P(None, "tensor"), P(None, "tensor"),
        P(), P(), P(None, "tensor"), P("tensor", None), P(every, None, None),
    )
    out_specs = (
        P(every, None, None), P(every, None, None), P("tensor"), P("tensor"), P("tensor"),
        P("tensor", None), P("tensor", None), P("tensor", None), P("tensor", None), P("tensor"),
        P(None, "tensor"), P(None, "tensor"), P("tensor"), P("tensor"), P(None, "tensor"),
        P("tensor", None),
    )
    return jax.shard_map(shards, mesh=cores, in_specs=in_specs, out_specs=out_specs, check_vma=False)
```

```python
import functools

import ml_dtypes
import numpy as np

import jax
import jax.numpy as jnp
from jax import lax
from jax.experimental import pallas as pl
from jax.experimental.pallas import tpu as pltpu
from jax.sharding import PartitionSpec as P

VMEM_LIMIT = 60 * 1024 * 1024
F32, BF16 = jnp.float32, jnp.bfloat16
LANES = 128
MESH = pl.DeviceIdType.MESH
KERNEL_INNER = 64
MOMENT_INNER = 32
CB = 256
DFT_ROWS = 512
TOKEN_ROWS = 256
FFN_TILE = 512
GELU_A = 0.7978845608028654
GELU_B = 0.044715
norm_eps = 1e-05


def params_of(**extra):
    return pltpu.CompilerParams(vmem_limit_bytes=VMEM_LIMIT, **extra)


class CoreExchange:
    def __init__(self, pairs, send, recv):
        self.pairs, self.send, self.recv = pairs, send, recv
        self.other = {"core": 1 - lax.axis_index("core")}

    def copies(self, slot):
        return [
            pltpu.make_async_remote_copy(
                src_ref=mine.at[slot], dst_ref=theirs.at[slot],
                send_sem=self.send.at[i, slot], recv_sem=self.recv.at[i, slot],
                device_id=self.other, device_id_type=MESH,
            )
            for i, (mine, theirs) in enumerate(self.pairs)
        ]

    def start(self, slot):
        for copy in self.copies(slot):
            copy.start()

    def arrived(self, slot):
        for copy in self.copies(slot):
            copy.wait_recv()

    def sent(self, slots):
        for slot in range(slots):
            for copy in self.copies(slot):
                copy.wait_send()


class Posts:
    def __init__(self, bits, send, recv):
        self.bits, self.send, self.recv, self.used = bits, send, recv, 0
        self.place = lax.axis_index("pair")
        self.started = []

    def bit(self, b):
        return lax.rem(lax.div(self.place, 1 << b), 2)

    def device(self, link):
        if isinstance(link, str):
            return {link: 1 - lax.axis_index(link)}
        return {"pair": self.place + (1 - 2 * self.bit(link)) * (1 << link)}

    def block(self, flipped):
        at = 0
        for b in range(self.bits):
            here = 1 - self.bit(b) if flipped >> b & 1 else self.bit(b)
            at = at + here * (1 << (self.bits - 1 if b == 0 else b - 1))
        return at

    def slot(self):
        self.used += 1
        return self.used - 1

    def copy(self, src, dst, slot, link):
        return pltpu.make_async_remote_copy(
            src_ref=src, dst_ref=dst, send_sem=self.send.at[slot], recv_sem=self.recv.at[slot],
            device_id=self.device(link), device_id_type=MESH,
        )

    def post(self, src, dst, slot, link):
        copy = self.copy(src, dst, slot, link)
        copy.start()
        self.started.append(copy)

    def await_(self, dst, slot, link):
        self.copy(dst, dst, slot, link).wait_recv()

    def greet(self, links):
        for link in links:
            pl.semaphore_signal(
                pltpu.get_barrier_semaphore(), inc=1, device_id=self.device(link),
                device_id_type=MESH,
            )

    def meet(self, count):
        pl.semaphore_wait(pltpu.get_barrier_semaphore(), count)

    def finish(self):
        for copy in self.started:
            copy.wait_send()


def exchange_sems(pairs, slots):
    return [pltpu.SemaphoreType.DMA((pairs, slots))] * 2


def transform_table(length):
    f = np.arange(length, dtype=np.int64)[:, None]
    t = np.arange(length, dtype=np.int64)[None, :]
    turn = ((4 * f + 1) * t) % (4 * length)
    angle = turn * (2.0 * np.pi / (4 * length))
    return np.concatenate([np.cos(angle), -np.sin(angle)], axis=0)


def cmul(a, b):
    return a[0] * b[0] - a[1] * b[1], a[0] * b[1] + a[1] * b[0]


def log2_of(count):
    bits = count.bit_length() - 1
    assert 1 << bits == count
    return bits


def fill_powers(base, count, out_r, out_i, tmp, scale=None):
    bits = log2_of(count)
    p = base
    for i in range(bits):
        tmp[2 * i] = p[0]
        tmp[2 * i + 1] = p[1]
        p = cmul(p, p)
    if scale is not None:
        tmp[2 * bits] = scale[0]
        tmp[2 * bits + 1] = scale[1]
    row = lax.broadcasted_iota(jnp.int32, (8, LANES), 0)

    def mode(n, carry):
        def at(i):
            return tuple(
                jnp.broadcast_to(tmp[2 * i + j, pl.ds(n, 1), :], (8, LANES)) for j in range(2)
            )

        if scale is None:
            p = (jnp.ones((8, LANES), F32), jnp.zeros((8, LANES), F32))
        else:
            p = at(bits)
        for bit in range(3):
            q = cmul(p, at(bit))
            on = (row & (1 << bit)) != 0
            p = (jnp.where(on, q[0], p[0]), jnp.where(on, q[1], p[1]))
        parts = [p]
        for bit in range(3, bits):
            w = at(bit)
            parts += [cmul(x, w) for x in parts]
        for j, part in enumerate(parts):
            out_r[n, 8 * j : 8 * j + 8, :] = part[0]
            out_i[n, 8 * j : 8 * j + 8, :] = part[1]
        return carry

    lax.fori_loop(0, base[0].shape[0], mode, 0)
    return p


def split_params(packed_ref, log_dt_ref):
    rows = packed_ref[...]
    modes = rows.shape[0] // 4
    log_a, freq, c_real, c_imag = (rows[i * modes : (i + 1) * modes] for i in range(4))
    step = jnp.exp(log_dt_ref[...])
    rate = jnp.exp(log_a)
    decay = jnp.exp(-(step * rate))
    turn = step * freq
    return step, rate, freq, c_real, c_imag, (decay * jnp.cos(turn), decay * jnp.sin(turn))


def kernel_block(packed_ref, log_dt_ref, k_ref, zr, zi, wr, wi, tmp):
    step, _, _, c_real, c_imag, z = split_params(packed_ref, log_dt_ref)
    inner = KERNEL_INNER
    outer = k_ref.shape[0] // inner
    modes = c_real.shape[0]
    z_inner = fill_powers(z, inner, zr, zi, tmp)
    fill_powers(z_inner, outer, wr, wi, tmp, (2.0 * step * c_real, 2.0 * step * c_imag))
    group = 2

    def rows(i, carry):
        d = i * group
        acc = [jnp.zeros((inner, LANES), F32) for _ in range(group)]
        for n in range(modes):
            a, b = zr[n], zi[n]
            for u in range(group):
                acc[u] = acc[u] + (
                    wr[n, pl.ds(d + u, 1), :] * a - wi[n, pl.ds(d + u, 1), :] * b
                )
        for u in range(group):
            at = pl.ds(pl.multiple_of((d + u) * inner, inner), inner)
            k_ref[at, :] = acc[u].astype(BF16)
        return carry

    lax.fori_loop(0, outer // group, rows, 0)


def power_scratch(modes, inner, outer):
    return (
        [pltpu.VMEM((modes, inner, LANES), F32)] * 2
        + [pltpu.VMEM((modes, outer, LANES), F32)] * 2
        + [pltpu.VMEM((20, modes, LANES), F32)]
    )


def moments_block(packed_ref, log_dt_ref, g_ref, out_ref, zr, zi, wr, wi, tmp, sums):
    step, rate, freq, c_real, c_imag, z = split_params(packed_ref, log_dt_ref)
    inner, outer = zr.shape[1], wr.shape[1]
    z_inner = fill_powers(z, inner, zr, zi, tmp)
    fill_powers(z_inner, outer, wr, wi, tmp)
    modes = c_real.shape[0]
    pos = lax.broadcasted_iota(jnp.int32, (inner, LANES), 0).astype(F32)

    def mode(n, carry):
        zero = jnp.zeros((inner, LANES), F32)
        sr, si, tr, ti = zero, zero, zero, zero
        for d in reversed(range(outer)):
            v = g_ref[d * inner : (d + 1) * inner, :]
            sr = sr + v * wr[n, d : d + 1, :]
            si = si + v * wi[n, d : d + 1, :]
            if d > 0:
                tr = tr + sr
                ti = ti + si
        zn = (zr[n], zi[n])
        first = cmul(zn, (sr, si))
        second = cmul(zn, (pos * sr + float(inner) * tr, pos * si + float(inner) * ti))
        for j, v in enumerate(first + second):
            sums[j, pl.ds(n, 1), :] = jnp.sum(v, axis=0, keepdims=True)
        return carry

    lax.fori_loop(0, modes, mode, 0)
    scale = 2.0 * step
    real_grad, imag_grad = scale * sums[0], -scale * sums[1]
    slope_r = scale * (c_real * sums[2] - c_imag * sums[3])
    slope_i = scale * (c_real * sums[3] + c_imag * sums[2])
    log_a_grad = -step * rate * slope_r
    freq_grad = -step * slope_i
    log_dt_grad = jnp.sum(
        c_real * real_grad + c_imag * imag_grad + log_a_grad + freq * freq_grad,
        axis=0, keepdims=True,
    )
    for i, part in enumerate((log_a_grad, freq_grad, real_grad, imag_grad)):
        out_ref[i * modes : (i + 1) * modes, :] = part
    top = 4 * modes
    row = lax.broadcasted_iota(jnp.int32, (8, LANES), 0)
    out_ref[top : top + 8, :] = jnp.where(row == 0, log_dt_grad, 0.0)


def gelu_both(v):
    sq = v * v
    th = jnp.tanh(v * (GELU_A + (GELU_A * GELU_B) * sq))
    rise = 0.5 + 0.5 * th
    slope = rise + v * (0.5 - 0.5 * th * th) * (GELU_A + (3.0 * GELU_A * GELU_B) * sq)
    return v * rise, slope


def gelu(v):
    return gelu_both(v)[0]


def gelu_slope(v):
    return gelu_both(v)[1]


def dot(a, b):
    return jnp.dot(a, b, preferred_element_type=F32)


def conv_block(x, k, skip, fwd_ref, inv_ref, mixed_ref, act_ref, xs_ref, ks_ref, ys):
    n = x.shape[0]
    for i in range(n // DFT_ROWS):
        re = pl.ds(i * DFT_ROWS, DFT_ROWS)
        im = pl.ds(n + i * DFT_ROWS, DFT_ROWS)
        xr, xi = dot(fwd_ref[re, :], x), dot(fwd_ref[im, :], x)
        kr, ki = dot(fwd_ref[re, :], k), dot(fwd_ref[im, :], k)
        xs_ref[re, :] = xr.astype(BF16)
        xs_ref[im, :] = xi.astype(BF16)
        ks_ref[re, :] = kr.astype(BF16)
        ks_ref[im, :] = ki.astype(BF16)
        ys[re, :] = (xr * kr - xi * ki).astype(BF16)
        ys[im, :] = (xr * ki + xi * kr).astype(BF16)
    y = ys[...]
    for i in range(n // TOKEN_ROWS):
        at = pl.ds(i * TOKEN_ROWS, TOKEN_ROWS)
        mixed = dot(inv_ref[at, :], y) + skip * x[i * TOKEN_ROWS : (i + 1) * TOKEN_ROWS].astype(F32)
        mixed_ref[at, :] = mixed
        act_ref[at, :] = gelu(mixed).astype(BF16)


def front_body(
    inputs, cot, counts, gains, log_dt, skip, log_a, freq, c_real, c_imag, fwd_hbm, inv_hbm,
    w_value, w_gate, w_in, w_out,
    packed_ref, vec_ref, skip_ref, grad_ref, x_out, mixed_out, act_out, xs_out, ks_out,
    value_out, sig_out, residual_out, n2_out, n2t_out,
    value_direct, value_via, gate_direct, gate_via, in_direct, in_via, out_direct, out_via,
    zr, zi, wr, wi, tmp, fwd, inv, packed, vec, got_vec, nx, k, mixed, act, xs, ks, ys,
    owns, fars, values, gates, value_s, sig_s, residual_s, n2_s, n2t_s,
    local, send, recv, *, bits
):
    posts = Posts(bits, send, recv)
    core, side = lax.axis_index("core"), lax.axis_index("tensor")
    half = packed.shape[2]
    modes = log_a.shape[0]
    posts.greet([0, 1, "core", "tensor"])
    tables = [
        pltpu.make_async_copy(src, dst, local.at[i])
        for i, (src, dst) in enumerate(
            ((fwd_hbm, fwd), (inv_hbm, inv), (w_value, owns.at[0]), (w_gate, owns.at[1]))
        )
    ]
    for copy in tables:
        copy.start()
    mine = pl.ds(pl.multiple_of(core * half, half), half)
    for i, ref in enumerate((log_a, freq, c_real, c_imag)):
        packed[1, i * modes : (i + 1) * modes, :] = ref[:, mine]
    vec[0:1, :] = log_dt[...]
    vec[1:2, :] = skip[...]
    posts.meet(4)

    def exchange(src, dst, link):
        slot = posts.slot()
        posts.post(src, dst, slot, link)
        return lambda: posts.await_(dst, slot, link)

    params_come = [
        exchange(packed.at[1], packed.at[0], "tensor"), exchange(vec, got_vec, "tensor")
    ]
    rows = value_direct.shape[0] // 4
    place = 2 * posts.bit(1) + posts.bit(0)

    def quarter(at, part=None):
        first, count = (0, rows) if part is None else (part * (rows // 2), rows // 2)
        return pl.ds(pl.multiple_of(at * rows + first, rows // 2), count)

    def cols(count):
        return pl.ds(pl.multiple_of(core * count, count), count)

    near, up, across = (place + 1 - 2 * posts.bit(0)), (place + 2 - 4 * posts.bit(1)), 3 - place
    out_row = pl.multiple_of(core * (4 * rows) + place * rows, rows)
    sources = [
        [(w_value.at[quarter(place), cols(half)], value_direct, value_via),
         (w_gate.at[quarter(place), cols(half)], gate_direct, gate_via)],
        [(w_in.at[quarter(place), cols(in_direct.shape[1])], in_direct, in_via)],
        [(w_out.at[pl.ds(out_row, rows), :], out_direct, out_via)],
    ]

    def fetch_steps(items):
        slots = []
        for src, direct, via in items:
            took = [posts.slot() for _ in range(9)]
            slots.append(took)
            posts.post(src, direct.at[quarter(place)], took[0], "tensor")
        yield
        for (src, direct, via), took in zip(items, slots):
            own = direct.at[quarter(place)]
            posts.await_(own, took[0], "tensor")
            posts.post(own, own, took[1], 0)
            posts.post(own, own, took[2], 1)
            posts.post(own, via.at[quarter(place)], took[5], "core")
        yield
        for (src, direct, via), took in zip(items, slots):
            for link, at, slot, on, over, piece in (
                (0, near, 1, 3, 1, 0), (1, up, 2, 4, 0, 1)
            ):
                come = direct.at[quarter(at)]
                posts.await_(come, took[slot], link)
                passed = direct.at[quarter(at, piece)]
                posts.post(passed, passed, took[on], over)
                posts.post(come, via.at[quarter(at)], took[5 + slot], "core")
        yield
        for (src, direct, via), took in zip(items, slots):
            for slot, link, piece in ((3, 1, 0), (4, 0, 1)):
                posts.await_(direct.at[quarter(across, piece)], took[slot], link)
            come = direct.at[quarter(across)]
            posts.post(come, via.at[quarter(across)], took[8], "core")
        yield
        for (src, direct, via), took in zip(items, slots):
            for at, slot in ((place, 5), (near, 6), (up, 7), (across, 8)):
                posts.await_(via.at[quarter(at)], took[slot], "core")

    flows = [fetch_steps(items) for items in sources]
    for flow in flows:
        next(flow)

    def kernel_of(j, log_dt, between=lambda: None):
        for i in range(half // LANES):
            if i:
                between()
            at = pl.ds(i * LANES, LANES)
            kernel_block(packed.at[1 - j, :, at], log_dt.at[:, at], k.at[2 * j, :, at], zr, zi, wr, wi, tmp)

    vec_ref[1] = vec[0:1, mine]
    kernel_of(0, vec_ref.at[1])
    kernels_come = [exchange(k.at[0], k.at[1], "core")]
    for come in params_come:
        come()
    vec_ref[0] = got_vec[0:1, mine]
    kernel_of(1, vec_ref.at[0], lambda: next(flows[0]))
    kernels_come.append(exchange(k.at[2], k.at[3], "core"))
    for i in range(nx.shape[0] // TOKEN_ROWS):
        at = pl.ds(i * TOKEN_ROWS, TOKEN_ROWS)
        source = inputs[at, :].astype(F32)
        nx[at, :] = norm_forward(source, gains[0:1, :], gains[1:2, :])[0].astype(BF16)
    used = (side < counts[0]).astype(F32)
    grad_ref[...] = (used * cot[...].astype(F32)).astype(BF16)
    width = vec.shape[1]
    for ref, at in ((vec, side), (got_vec, 1 - side)):
        skip_ref[:, pl.ds(pl.multiple_of(at * width, width), width)] = ref[1:2, :]
    stores = [
        pltpu.make_async_copy(nx, x_out, local.at[4]),
        pltpu.make_async_copy(packed, packed_ref, local.at[5]),
    ]
    for copy in stores:
        copy.start()
    for copy in tables:
        copy.wait()
    next(flows[0])
    next(flows[1])
    plan = ((0, None), (2, flows[2]), (1, flows[1]), (3, flows[0]))
    for n, (j, flow) in enumerate(plan):
        there = lax.rem(side + j // 2, 2)
        which = lax.rem(core + j % 2, 2)
        at = pl.ds(pl.multiple_of((2 * there + which) * half, half), half)
        if j % 2:
            kernels_come[j // 2]()
        params = vec if j < 2 else got_vec
        skip = params[1:2, pl.ds(pl.multiple_of(which * half, half), half)]
        conv_block(
            nx[:, at], k[j], skip, fwd, inv, mixed.at[j], act.at[:, at], xs.at[j], ks.at[j], ys
        )
        for i, (src, dst) in enumerate(
            ((mixed.at[j], mixed_out.at[j]), (xs.at[j], xs_out.at[j]), (ks.at[j], ks_out.at[j]))
        ):
            copy = pltpu.make_async_copy(src, dst, local.at[6 + 3 * j + i])
            copy.start()
            stores.append(copy)
        if flow is not None:
            next(flow)
    next(flows[0], None)
    loads = [
        pltpu.make_async_copy(src, fars.at[i], local.at[18 + i])
        for i, src in enumerate((value_direct, value_via, gate_direct, gate_via))
    ]
    for copy in loads:
        copy.start()
    stores.append(pltpu.make_async_copy(act, act_out, local.at[22]))
    stores[-1].start()
    for copy in loads:
        copy.wait()
    services = {0: [flows[2]], 1: [flows[1]], 2: [], 3: []}
    for r in range(nx.shape[0] // TOKEN_ROWS):
        at = pl.ds(r * TOKEN_ROWS, TOKEN_ROWS)
        left = act[at, :]
        project_all(left, owns.at[0], fars.at[0], fars.at[1], values)
        project_all(left, owns.at[1], fars.at[2], fars.at[3], gates)
        value = values[...]
        sig = 1.0 / (1.0 + jnp.exp(-gates[...]))
        value_s[r] = value.astype(BF16)
        sig_s[r] = sig.astype(BF16)
        residual = inputs[at, :].astype(F32) + (value * sig).astype(BF16).astype(F32)
        residual_s[r] = residual
        n2 = norm_forward(residual, gains[2:3, :], gains[3:4, :])[0].astype(BF16)
        n2_s[r] = n2
        n2t_s[r] = n2.T
        for i, (src, dst) in enumerate((
            (value_s, value_out.at[at]), (sig_s, sig_out.at[at]), (residual_s, residual_out.at[at]),
            (n2_s, n2_out.at[at]), (n2t_s, n2t_out.at[:, at]),
        )):
            copy = pltpu.make_async_copy(src.at[r], dst, local.at[23 + 5 * r + i])
            copy.start()
            stores.append(copy)
        for flow in services[r]:
            next(flow)
    for flow in (flows[1], flows[2], flows[2]):
        next(flow, None)
    for copy in stores:
        copy.wait()
    posts.finish()


def front_kernel(
    inputs, cot, counts, gains, log_dt, skip, log_a, freq, c_real, c_imag, fwd, inv,
    w_value, w_gate, w_in, w_out,
):
    bits = log2_of(lax.axis_size("pair"))
    n, d = inputs.shape
    modes = log_a.shape[0]
    half = d // 4
    units = w_in.shape[1] // 2
    chunks = n // TOKEN_ROWS
    vmem = pl.BlockSpec(memory_space=pltpu.VMEM)
    hbm = pl.BlockSpec(memory_space=pl.ANY)
    shape = jax.ShapeDtypeStruct
    return pl.pallas_call(
        functools.partial(front_body, bits=bits),
        in_specs=[vmem] * 2 + [pl.BlockSpec(memory_space=pltpu.SMEM)] + [vmem] * 7 + [hbm] * 6,
        out_specs=[hbm, vmem, vmem, vmem] + [hbm] * 18,
        out_shape=[
            shape((2, 4 * modes, half), F32), shape((2, 1, half), F32), shape((1, d), F32),
            shape((n, d), BF16), shape((n, d), BF16), shape((4, n, half), F32), shape((n, d), BF16),
            shape((4, 2 * n, half), BF16), shape((4, 2 * n, half), BF16),
            shape((n, d), BF16), shape((n, d), BF16), shape((n, d), F32), shape((n, d), BF16),
            shape((d, n), BF16),
        ]
        + [shape((d, half), BF16)] * 4
        + [shape((d, units), BF16)] * 2
        + [shape((units, d), BF16)] * 2,
        scratch_shapes=power_scratch(modes, KERNEL_INNER, n // KERNEL_INNER)
        + [
            pltpu.VMEM(fwd.shape, BF16), pltpu.VMEM(inv.shape, BF16),
            pltpu.VMEM((2, 4 * modes, half), F32),
            pltpu.VMEM((2, d // 2), F32), pltpu.VMEM((2, d // 2), F32),
            pltpu.VMEM((n, d), BF16), pltpu.VMEM((4, n, half), BF16),
            pltpu.VMEM((4, n, half), F32), pltpu.VMEM((n, d), BF16),
            pltpu.VMEM((4, 2 * n, half), BF16), pltpu.VMEM((4, 2 * n, half), BF16),
            pltpu.VMEM((2 * n, half), BF16),
            pltpu.VMEM((2, d, 2 * half), BF16), pltpu.VMEM((4, d, half), BF16),
            pltpu.VMEM((TOKEN_ROWS, d), F32), pltpu.VMEM((TOKEN_ROWS, d), F32),
            pltpu.VMEM((chunks, TOKEN_ROWS, d), BF16), pltpu.VMEM((chunks, TOKEN_ROWS, d), BF16),
            pltpu.VMEM((chunks, TOKEN_ROWS, d), F32), pltpu.VMEM((chunks, TOKEN_ROWS, d), BF16),
            pltpu.VMEM((chunks, d, TOKEN_ROWS), BF16),
            pltpu.SemaphoreType.DMA((24 + 5 * chunks,)),
            pltpu.SemaphoreType.DMA((40,)), pltpu.SemaphoreType.DMA((40,)),
        ],
        compiler_params=params_of(collective_id=5, has_side_effects=True),
        name="front_kernel",
    )(
        inputs, cot, counts, gains, log_dt, skip, log_a, freq, c_real, c_imag, fwd, inv,
        w_value, w_gate, w_in, w_out,
    )


def conv_back_block(ga, mixed, x, xs, ks, skip, fwd, inv, gm, gy, ax, ak, put_gn, put_gk):
    n = x.shape[0]
    total = jnp.zeros((1, x.shape[1]), F32)
    for i in range(n // TOKEN_ROWS):
        at = pl.ds(i * TOKEN_ROWS, TOKEN_ROWS)
        v = ga[at, :] * gelu_slope(mixed[at, :])
        gm[at, :] = v
        gy[at, :] = v.astype(BF16)
        total += jnp.sum(v * x[at, :].astype(F32), axis=0, keepdims=True)
    g = gy[...]
    for i in range(n // DFT_ROWS):
        re = pl.ds(i * DFT_ROWS, DFT_ROWS)
        im = pl.ds(n + i * DFT_ROWS, DFT_ROWS)
        gr, gi = dot(fwd[re, :], g), dot(fwd[im, :], g)
        for src, dst in ((ks, ax), (xs, ak)):
            a, b = src[re, :].astype(F32), src[im, :].astype(F32)
            dst[re, :] = (a * gr + b * gi).astype(BF16)
            dst[im, :] = (a * gi - b * gr).astype(BF16)
    yx = ax[...]
    yk = ak[...]
    for i in range(n // TOKEN_ROWS):
        at = pl.ds(i * TOKEN_ROWS, TOKEN_ROWS)
        put_gk(at, dot(inv[at, :], yk))
        put_gn(at, dot(inv[at, :], yx) + skip * gm[at, :])
    return total


def project_all(left, own, direct, via, out):
    core, side = lax.axis_index("core"), lax.axis_index("tensor")
    width = direct.shape[1]
    far = (1 - side) * 2 * width
    for ref, first, count in (
        (own, side * 2 * width, 2 * width), (direct, far + core * width, width),
        (via, far + (1 - core) * width, width),
    ):
        out[:, pl.ds(pl.multiple_of(first, width), count)] = dot(left, ref[...])


def glu_back_body(
    g_sum, residual, cot, value, sig, act, value_own, value_direct, value_via,
    gate_own, gate_direct, gate_via, gains,
    there_keep, there_come, in_box, here_out, out_come,
    resid_ref, ga_ref, gain_ref, bias_ref, there_ref, here_ref, in_x, in_y, out_z,
    gv, gt, mine, theirs, in_a, in_b, out_a, out_b, out_box, local, send, recv, *, bits
):
    step = pl.program_id(0)
    posts = Posts(bits, send, recv)
    links = [0, 1, "core", "tensor"]
    slots = {name: posts.slot() for name in ("x", "y", "z")}
    swap = [posts.slot(), posts.slot()]

    def transfers():
        return [
            posts.copy(in_box, in_x, slots["x"], 0),
            posts.copy(in_a, in_y, slots["y"], "tensor"),
            posts.copy(out_box, out_z, slots["z"], 1),
        ]

    @pl.when(step == 0)
    def _():
        posts.greet(links)
        other = 1 - posts.bit(1)
        loads = [
            pltpu.make_async_copy(src, dst, local.at[i])
            for i, (src, dst) in enumerate((
                (there_keep, in_a), (there_come, in_b),
                (here_out.at[:, other], out_a), (out_come.at[:, other], out_b),
            ))
        ]
        for copy in loads:
            copy.start()
        posts.meet(len(links))
        sends = transfers()
        sends[0].start()
        for copy in loads[:2]:
            copy.wait()
        in_a[...] = (in_a[...].astype(F32) + in_b[...].astype(F32)).astype(BF16)
        sends[1].start()
        for copy in loads[2:]:
            copy.wait()
        out_box[...] = (out_a[...] + out_b[...].astype(F32)).astype(BF16)
        sends[2].start()

    chunks = act.shape[0] // TOKEN_ROWS
    width = gv.shape[2]

    @pl.when(step < chunks)
    def _():
        standard, inv_std = norm_forward(residual[...], 1.0, 0.0)[1:]
        part, gain_grad, bias_grad = norm_backward(
            g_sum[...], standard, inv_std, gains[2:3, :]
        )
        new = step == 0
        gain_ref[...] = jnp.where(new, 0.0, gain_ref[...]) + gain_grad[None]
        bias_ref[...] = jnp.where(new, 0.0, bias_ref[...]) + bias_grad[None]
        resid = cot[...].astype(F32) + part
        resid_ref[...] = resid
        grad = resid.astype(BF16).astype(F32)
        gate = sig[...].astype(F32)
        grad_value = (grad * gate).astype(BF16)
        grad_gate = (grad * value[...].astype(F32) * gate * (1.0 - gate)).astype(BF16)
        at = pl.ds(pl.multiple_of(step * TOKEN_ROWS, TOKEN_ROWS), TOKEN_ROWS)
        for i in range(gv.shape[0]):
            gv[i, at, :] = grad_value[:, i * width : (i + 1) * width]
            gt[i, at, :] = grad_gate[:, i * width : (i + 1) * width]
        core, side = lax.axis_index("core"), lax.axis_index("tensor")
        far = 2 * (1 - side)
        total = 0.0
        for grads, own, direct, via in (
            (gv, value_own, value_direct, value_via), (gt, gate_own, gate_direct, gate_via)
        ):
            ours = jnp.concatenate([grads[2 * side, at, :], grads[2 * side + 1, at, :]], axis=1)
            total += contract_cols(ours, own[...])
            total += contract_cols(grads[far + core, at, :], direct[...])
            total += contract_cols(grads[far + 1 - core, at, :], via[...])
        ga_ref[...] = total

    @pl.when(step >= chunks)
    def _():
        j = step - chunks
        side = lax.rem(lax.axis_index("tensor") + 1 + j, 2)
        half = lax.rem(lax.axis_index("core") + 1 + j // 2, 2)
        block = 2 * side + half
        grads = [contract_rows(act[...], gv[block]), contract_rows(act[...], gt[block])]
        for slot in range(2):
            @pl.when(j == slot)
            def _():
                for i, g in enumerate(grads):
                    mine[slot, :, i * width : (i + 1) * width] = g.astype(BF16)
                posts.copy(mine.at[slot], theirs.at[slot], swap[slot], "core").start()

        @pl.when(j == 2)
        def _():
            posts.await_(theirs.at[0], swap[0], "core")
            for i, g in enumerate(grads):
                at = pl.ds(i * width, width)
                there_ref[:, at] = (g + theirs[0, :, at].astype(F32)).astype(BF16)

        @pl.when(j == 3)
        def _():
            posts.await_(theirs.at[1], swap[1], "core")
            for i, g in enumerate(grads):
                at = pl.ds(i * width, width)
                here_ref[:, at] = g + theirs[1, :, at].astype(F32)
            for slot in range(2):
                posts.copy(mine.at[slot], theirs.at[slot], swap[slot], "core").wait_send()
            for copy in transfers():
                copy.wait()


def glu_back_kernel(
    g_sum, residual, cot, value, sig, act, weights, gains,
    there_keep, there_come, in_box, here_out, out_come,
):
    bits = log2_of(lax.axis_size("pair"))
    n, d = act.shape
    chunks = n // TOKEN_ROWS
    width = d // 4
    hbm = pl.BlockSpec(memory_space=pl.ANY)
    extra = (there_keep, there_come, in_box, here_out, out_come)
    split = (here_out.shape[0],) + here_out.shape[2:]

    def whole(a):
        return pl.BlockSpec(a.shape, lambda i: (0, 0), pipeline_mode=pl.Buffered(1))

    rows = pl.BlockSpec((TOKEN_ROWS, d), lambda i: (jnp.minimum(i, chunks - 1), 0))
    vector = pl.BlockSpec((1, d), lambda i: (0, 0))
    weight = pl.BlockSpec((d, 2 * width), lambda i: (0, 0))
    return pl.pallas_call(
        functools.partial(glu_back_body, bits=bits),
        grid=(chunks + 4,),
        in_specs=[rows] * 5 + [whole(act)] + [whole(w) for w in weights] + [whole(gains)] + [hbm] * 5,
        out_specs=[rows, rows, vector, vector, weight, weight] + [hbm] * 3,
        scratch_shapes=[pltpu.VMEM((4, n, width), BF16)] * 2
        + [pltpu.VMEM((2, d, 2 * width), BF16)] * 2
        + [pltpu.VMEM(there_keep.shape, BF16)] * 2
        + [pltpu.VMEM(split, F32), pltpu.VMEM(split, BF16), pltpu.VMEM(split, BF16)]
        + [pltpu.SemaphoreType.DMA((4,))]
        + [pltpu.SemaphoreType.DMA((5,))] * 2,
        out_shape=[
            jax.ShapeDtypeStruct((n, d), F32), jax.ShapeDtypeStruct((n, d), F32),
            jax.ShapeDtypeStruct((1, d), F32), jax.ShapeDtypeStruct((1, d), F32),
            jax.ShapeDtypeStruct((d, 2 * width), BF16), jax.ShapeDtypeStruct((d, 2 * width), F32),
            jax.ShapeDtypeStruct(in_box.shape, BF16), jax.ShapeDtypeStruct(in_box.shape, BF16),
            jax.ShapeDtypeStruct(split, BF16),
        ],
        compiler_params=params_of(collective_id=2, has_side_effects=True),
        name="glu_back_kernel",
    )(g_sum, residual, cot, value, sig, act, *weights, gains, *extra)


def ffn_body(*refs, own):
    n2, n2t, gl, ia, ib, oa, ob, before, *refs = refs
    if own:
        counts, gn2_before, *refs = refs
    first_out, gn2, box_ref, keep_ref, out_ref, *refs = refs
    if own:
        ffn, *refs = refs
    else:
        ffn = first_out
    wi, wo, h, gp, total, in_mine, out_mine, in_theirs, out_theirs, local, send, recv = refs
    step, half = pl.program_id(0), in_mine.shape[0]
    first = step < half
    cores = CoreExchange([(in_mine, in_theirs), (out_mine, out_theirs)], send, recv)
    barrier = pltpu.get_barrier_semaphore()

    def before_loads():
        pairs = [(before, ffn)] + ([(gn2_before, gn2)] if own else [])
        return [pltpu.make_async_copy(src, dst, local.at[i]) for i, (src, dst) in enumerate(pairs)]

    @pl.when(step == 0)
    def _():
        pl.semaphore_signal(barrier, inc=1, device_id=cores.other, device_id_type=MESH)
        for copy in before_loads():
            copy.start()
        if not own:
            gn2[...] = jnp.zeros_like(gn2)

    @pl.when(first)
    def _():
        wi[...] = ia[...]
        wo[...] = oa[...]

    @pl.when(jnp.logical_not(first))
    def _():
        wi[...] = ib[...]
        wo[...] = ob[...]

    w1, w2 = wi[...], wo[...]
    for r in range(n2.shape[0] // TOKEN_ROWS):
        at = pl.ds(r * TOKEN_ROWS, TOKEN_ROWS)
        act, slope = gelu_both(dot(n2[at, :], w1))
        h[at, :] = act.astype(BF16)
        gp[at, :] = (contract_cols(gl[at, :], w2) * slope).astype(BF16)

    @pl.when(step == 0)
    def _():
        for copy in before_loads():
            copy.wait()

    for r in range(n2.shape[0] // TOKEN_ROWS):
        at = pl.ds(r * TOKEN_ROWS, TOKEN_ROWS)
        ffn[at, :] += dot(h[at, :], w2)
        gn2[at, :] += contract_cols(gp[at, :], w1)
    out_grad = contract_rows(h[...], gl[...])
    in_grad = dot(n2t[...], gp[...])

    @pl.when(step == 0)
    def _():
        pl.semaphore_wait(barrier, 1)

    @pl.when(first)
    def _():
        in_mine[step] = in_grad.astype(BF16)
        out_mine[step] = out_grad.astype(BF16)
        cores.start(step)

    @pl.when(jnp.logical_not(first))
    def _():
        cores.arrived(step - half)
        total[...] = in_grad + in_theirs[step - half].astype(F32)
        near, rows = lax.rem(lax.axis_index("pair"), 2), keep_ref.shape[0]
        for ref, at in ((keep_ref, near), (box_ref, 1 - near)):
            part = pl.ds(pl.multiple_of(at * rows, rows), rows)
            ref[...] = total[part, :].astype(ref.dtype)
        out_ref[...] = (out_grad + out_theirs[step - half].astype(F32)).astype(out_ref.dtype)

    @pl.when(step == 2 * half - 1)
    def _():
        if own:
            used = (lax.axis_index("tensor") < counts[0]).astype(F32)
            first_out[...] = (used * ffn[...]).astype(BF16)
        cores.sent(half)


def ffn_kernel(n2, n2t, gl, ins, outs, units, before, own=()):
    n, d = n2.shape
    half = units // FFN_TILE
    owned = bool(own)
    hbm = pl.BlockSpec(memory_space=pl.ANY)

    def whole(a):
        return pl.BlockSpec(a.shape, lambda s: (0, 0), pipeline_mode=pl.Buffered(1))

    def fst(s):
        at = jnp.minimum(s, half - 1)
        return at + (1 - lax.axis_index("core")) * half if owned else at

    def snd(s):
        at = jnp.maximum(s - half, 0)
        return at + lax.axis_index("core") * half if owned else at

    def late(s):
        return jnp.maximum(s - half, 0)

    total = pl.BlockSpec((n, d), lambda s: (0, 0))
    dtype = F32 if owned else BF16
    shape = jax.ShapeDtypeStruct
    return pl.pallas_call(
        functools.partial(ffn_body, own=owned),
        grid=(2 * half,),
        in_specs=[
            whole(n2), whole(n2t), whole(gl),
            pl.BlockSpec((d, FFN_TILE), lambda s: (0, fst(s))),
            pl.BlockSpec((d, FFN_TILE), lambda s: (0, snd(s))),
            pl.BlockSpec((FFN_TILE, d), lambda s: (fst(s), 0)),
            pl.BlockSpec((FFN_TILE, d), lambda s: (snd(s), 0)),
            hbm,
        ]
        + ([pl.BlockSpec(memory_space=pltpu.SMEM), hbm] if owned else []),
        out_specs=[
            total, total,
            pl.BlockSpec((d // 2, FFN_TILE), lambda s: (0, late(s))),
            pl.BlockSpec((d // 2, FFN_TILE), lambda s: (0, late(s))),
            pl.BlockSpec((FFN_TILE, d), lambda s: (late(s), 0)),
        ],
        scratch_shapes=([pltpu.VMEM((n, d), F32)] if owned else [])
        + [
            pltpu.VMEM((d, FFN_TILE), BF16), pltpu.VMEM((FFN_TILE, d), BF16),
            pltpu.VMEM((n, FFN_TILE), BF16), pltpu.VMEM((n, FFN_TILE), BF16),
            pltpu.VMEM((d, FFN_TILE), F32),
        ]
        + [pltpu.VMEM((half, d, FFN_TILE), BF16), pltpu.VMEM((half, FFN_TILE, d), BF16)] * 2
        + [pltpu.SemaphoreType.DMA((2,))]
        + exchange_sems(2, half),
        out_shape=[
            shape((n, d), BF16 if owned else F32), shape((n, d), F32),
            shape((d // 2, units), BF16), shape((d // 2, units), dtype), shape((units, d), dtype),
        ],
        compiler_params=params_of(collective_id=int(owned), has_side_effects=True),
        name="ffn_kernel",
    )(n2, n2t, gl, *ins, *outs, before, *own)


def norm_forward(values, norm_gain, norm_bias):
    center = values - jnp.mean(values, axis=-1, keepdims=True)
    inv_std = lax.rsqrt(jnp.mean(center * center, axis=-1, keepdims=True) + norm_eps)
    standard = center * inv_std
    return (standard * norm_gain + norm_bias, standard, inv_std)


def norm_backward(incoming, standard, inv_std, norm_gain):
    scaled = incoming * norm_gain
    value_grad = inv_std * (
        scaled
        - jnp.mean(scaled, axis=-1, keepdims=True)
        - standard * jnp.mean(scaled * standard, axis=-1, keepdims=True)
    )
    return (value_grad, jnp.sum(incoming * standard, axis=0), jnp.sum(incoming, axis=0))


def contract_rows(left, right):
    return lax.dot_general(left, right, (((0,), (0,)), ((), ())), preferred_element_type=F32)


def contract_cols(left, right):
    return lax.dot_general(left, right, (((1,), (1,)), ((), ())), preferred_element_type=F32)


def scatter_steps(posts, acc, bits, order, boxes, come):
    def at(known, flipped):
        place = 0
        for i, b in enumerate(bits):
            here = posts.bit(b)
            if b in known:
                bit = 1 - here if known[b] else here
            else:
                bit = flipped >> i & 1
            place = place + bit * (1 << i)
        return place

    done = {}
    used = 0
    for n, b in enumerate(order):
        rest = [bits.index(i) for i in order[n + 1 :]]
        combos = [sum((c >> k & 1) << i for k, i in enumerate(rest)) for c in range(1 << len(rest))]
        slots = []
        for c, combo in enumerate(combos):
            slot = posts.slot()
            boxes[used + c] = acc[at({**done, b: True}, combo)].astype(BF16)
            posts.post(boxes.at[used + c], come.at[used + c], slot, b)
            slots.append(slot)
        yield
        done[b] = False
        for c, combo in enumerate(combos):
            posts.await_(come.at[used + c], slots[c], b)
            keep = at(done, combo)
            acc[keep] = acc[keep] + come[used + c].astype(F32)
        used += len(combos)
    posts.result = at(done, 0)


def gather_steps(posts, own, whole, local, order):
    core = lax.axis_index("core")
    count = 1 << posts.bits
    slots = {(rel, link): posts.slot() for rel in range(count) for link in ("bit", "core")}
    first = pltpu.make_async_copy(own, whole.at[core, posts.block(0)], local)
    first.start()

    def pass_on(src, rel, bits):
        dst = whole.at[core, posts.block(rel)]
        for b in bits:
            posts.post(src, dst, slots[rel ^ (1 << b), "bit"], b)
        posts.post(src, dst, slots[rel, "core"], "core")

    pass_on(own, 0, order)
    for n, b in enumerate(order):
        for c in range(1 << n):
            yield
            rel = sum((c >> k & 1) << order[k] for k in range(n)) | 1 << b
            block = whole.at[core, posts.block(rel)]
            posts.await_(block, slots[rel, "bit"], b)
            pass_on(block, rel, order[n + 1 :])
    yield
    first.wait()
    for rel in range(count):
        posts.await_(whole.at[1 - core, posts.block(rel)], slots[rel, "core"], "core")


def back_body(
    ga_hbm, mixed_hbm, x_hbm, xs_hbm, ks_hbm, fwd_hbm, inv_hbm, source_hbm, resid_hbm,
    in_keep, in_x, in_y, out_keep, out_come, out_z, glu_keep, glu_box,
    skip, gains, gain2, bias2, packed, log_dt,
    input_ref, in_all, out_all, glu_all, small_all,
    ga, fwd, inv, mixed, x, xs, ks, gm, gy, ax, ak, gk, gk_mine, gk_theirs, source, resid, staged,
    zr, zi, wr, wi, tmp, sums, moments, rows, rows_mine, rows_other, rows_come,
    in_acc, in_a, in_b, out_acc, out_a, out_b, glu_acc, glu_come, in_own, out_own, glu_own,
    in_boxes, in_got, out_boxes, out_got, glu_boxes, glu_got, small, small_far, small_got,
    local, send, recv, *, bits
):
    posts = Posts(bits, send, recv)
    links = list(range(bits)) + ["core", "tensor"]
    posts.greet(links)
    core, side = lax.axis_index("core"), lax.axis_index("tensor")
    n, width = mixed.shape[1:]
    used = [3]

    def load(src, dst):
        copy = pltpu.make_async_copy(src, dst, local.at[used[0]])
        used[0] += 1
        copy.start()
        return copy

    def columns(i):
        there = lax.rem(side + 1 + i, 2)
        which = lax.rem(core + 1 + i // 2, 2)
        return pl.ds(pl.multiple_of((2 * there + which) * width, width), width)

    def load_block(i):
        j, slot = 2 * ((i + 1) % 2) + 1 - i // 2, i % 2
        return [
            load(mixed_hbm.at[j], mixed.at[slot]), load(x_hbm.at[:, columns(i)], x.at[slot]),
            load(xs_hbm.at[j], xs.at[slot]), load(ks_hbm.at[j], ks.at[slot]),
        ]

    mine = posts.bit(1)
    in_loads = [load(in_keep, in_acc), load(in_x, in_a), load(in_y, in_b)]
    out_loads = [
        load(out_keep.at[:, mine], out_acc), load(out_come.at[:, mine], out_a), load(out_z, out_b)
    ]
    ga_load = load(ga_hbm, ga)
    block_loads = load_block(0)
    tables = [load(fwd_hbm, fwd), load(inv_hbm, inv)]
    glu_load = load(glu_keep, glu_acc)
    posts.meet(len(links))
    near, far = list(range(1, bits)), list(range(2, bits))

    def in_steps():
        for copy in in_loads:
            copy.wait()
        in_acc[...] = in_acc[...] + in_a[...].astype(F32) + in_b[...].astype(F32)
        yield from scatter_steps(posts, in_acc, near, near, in_boxes, in_got)
        in_own[...] = in_acc[posts.result].astype(BF16)
        yield from gather_steps(posts, in_own, in_all, local.at[0], list(reversed(range(bits))))

    def out_steps():
        for copy in out_loads:
            copy.wait()
        out_acc[...] = out_acc[...] + out_a[...].astype(F32) + out_b[...].astype(F32)
        yield from scatter_steps(posts, out_acc, far + [0], [0] + far, out_boxes, out_got)
        out_own[...] = out_acc[posts.result].astype(BF16)
        yield from gather_steps(posts, out_own, out_all, local.at[1], list(reversed(range(bits))))

    def glu_steps():
        slot = posts.slot()
        posts.post(glu_box, glu_come, slot, "tensor")
        yield
        posts.await_(glu_come, slot, "tensor")
        glu_load.wait()
        glu_acc[...] = glu_acc[...] + glu_come[...].astype(F32)
        yield from scatter_steps(posts, glu_acc, near + [0], [0] + near, glu_boxes, glu_got)
        glu_own[...] = glu_acc[posts.result].astype(BF16)
        yield from gather_steps(posts, glu_own, glu_all, local.at[2], GLU_ORDER(bits))

    def small_steps():
        for j in range(2):
            for half, ref in ((core, rows_mine), (1 - core, rows_other)):
                there = lax.rem(side + 1 + j, 2)
                at = pl.multiple_of((2 * there + half) * width, width)
                ref[j] = rows[:, pl.ds(at, width)]
        slot = posts.slot()
        posts.post(rows_other, rows_come, slot, "core")
        yield
        posts.await_(rows_come, slot, "core")
        top = moments.shape[1]
        for j, ref in ((0, small_far), (1, small)):
            ref[:top, :] = moments[j]
            ref[top:, :] = rows_mine[j] + rows_come[j]
        slot = posts.slot()
        posts.post(small_far, small_got.at[0], slot, "tensor")
        yield
        posts.await_(small_got.at[0], slot, "tensor")
        small[...] = small[...] + small_got[0]
        for b in range(bits):
            slot = posts.slot()
            small_all[b] = small[...]
            posts.post(small_all.at[b], small_got.at[1 + b], slot, b)
            yield
            posts.await_(small_got.at[1 + b], slot, b)
            small[...] = small[...] + small_got[1 + b]
        slot = posts.slot()
        small_all[bits] = small[...]
        posts.post(small_all.at[bits], small_got.at[1 + bits], slot, "core")
        yield
        posts.await_(small_got.at[1 + bits], slot, "core")
        small_all[bits + 1] = small_got[1 + bits]

    flows = {"in": in_steps(), "out": out_steps(), "glu": glu_steps()}
    done = object()

    def advance(*names):
        for name in names:
            if name in flows and next(flows[name], done) is done:
                del flows[name]

    advance("glu", "in", "out")
    rows[...] = jnp.zeros_like(rows)
    rows[3:4, :] = gain2[...]
    rows[4:5, :] = bias2[...]
    ga_load.wait()
    slots = [posts.slot(), posts.slot()]
    for i in range(4):
        slot = i % 2
        for copy in block_loads:
            copy.wait()
        if i < 3:
            block_loads = load_block(i + 1)
        if i == 0:
            for copy in tables:
                copy.wait()
        at = columns(i)

        def put_gn(tokens, value, at=at):
            ga[tokens, at] = value

        def put_gk(tokens, value, i=i):
            if i < 2:
                gk_mine[i, tokens, :] = value.astype(BF16)
            else:
                gk[i - 2, tokens, :] = value

        rows[0:1, at] = conv_back_block(
            ga.at[:, at], mixed.at[slot], x.at[slot], xs.at[slot], ks.at[slot], skip[:, at],
            fwd, inv, gm, gy, ax, ak, put_gn, put_gk,
        )
        if i < 2:
            posts.post(gk_mine.at[i], gk_theirs.at[i], slots[i], "core")
        else:
            posts.await_(gk_theirs.at[i - 2], slots[i - 2], "core")
            gk[i - 2] = gk[i - 2] + gk_theirs[i - 2].astype(F32)
        if i in BACK_ROUNDS:
            advance(*BACK_ROUNDS[i])

    chunks = n // TOKEN_ROWS

    def load_rows(r):
        at = pl.ds(r * TOKEN_ROWS, TOKEN_ROWS)
        return [load(source_hbm.at[at], source.at[r % 2]), load(resid_hbm.at[at], resid.at[r % 2])]

    row_loads = load_rows(0)
    stores = []
    for r in range(chunks):
        for copy in row_loads:
            copy.wait()
        if r + 1 < chunks:
            row_loads = load_rows(r + 1)
        at = pl.ds(r * TOKEN_ROWS, TOKEN_ROWS)
        standard, inv_std = norm_forward(source[r % 2].astype(F32), 1.0, 0.0)[1:]
        part, gain_grad, bias_grad = norm_backward(ga[at, :], standard, inv_std, gains[0:1, :])
        rows[1:2, :] = rows[1:2, :] + gain_grad[None]
        rows[2:3, :] = rows[2:3, :] + bias_grad[None]
        staged[r] = (resid[r % 2] + part).astype(BF16)
        stores.append(load(staged.at[r], input_ref.at[at]))
    advance(*BACK_ROUNDS["norm"])

    def block(j, i):
        at = pl.ds(i * LANES, LANES)
        moments_block(
            packed.at[j, :, at], log_dt.at[j, :, at], gk.at[j, :, at], moments.at[j, :, at],
            zr, zi, wr, wi, tmp, sums,
        )

    for j in range(2):
        for i in range(width // LANES):
            block(j, i)
            advance("in", "out", "glu")
    flows["small"] = small_steps()
    while flows:
        advance("small", "in", "out", "glu")
    for copy in stores:
        copy.wait()
    posts.finish()


def back_kernel(
    ga, mixed, x, xs, ks, fwd, inv, source, resid, in_keep, in_x, in_y, out_keep, out_come, out_z,
    glu_keep, glu_box, skip, gains, gain2, bias2, packed, log_dt,
):
    bits = log2_of(lax.axis_size("pair"))
    blocks = 1 << bits
    width, modes = packed.shape[2], packed.shape[1] // 4
    n, d = ga.shape
    block_rows, cols = glu_keep.shape[1:]
    kept = in_keep.shape[0]
    small_rows = 4 * modes + 8 + 8
    vmem = pl.BlockSpec(memory_space=pltpu.VMEM)
    hbm = pl.BlockSpec(memory_space=pl.ANY)
    big = pltpu.VMEM((block_rows, d), BF16)
    small = pltpu.VMEM((small_rows, width), F32)
    rows = pltpu.VMEM((2, 8, width), F32)
    copies = 3 * 2 * blocks + 2 * kept + blocks + bits + 12
    shape = jax.ShapeDtypeStruct
    return pl.pallas_call(
        functools.partial(back_body, bits=bits),
        in_specs=[hbm] * 17 + [vmem] * 6,
        out_specs=[hbm] * 4 + [vmem],
        out_shape=[
            shape((n, d), BF16), shape((2, blocks, block_rows, d), BF16),
            shape((2, blocks, block_rows, d), BF16), shape((2, blocks, block_rows, cols), BF16),
            shape((bits + 2, small_rows, width), F32),
        ],
        scratch_shapes=[
            pltpu.VMEM((n, d), F32), pltpu.VMEM(fwd.shape, BF16), pltpu.VMEM(inv.shape, BF16),
            pltpu.VMEM((2, n, width), F32), pltpu.VMEM((2, n, width), BF16),
            pltpu.VMEM((2, 2 * n, width), BF16), pltpu.VMEM((2, 2 * n, width), BF16),
            pltpu.VMEM((n, width), F32), pltpu.VMEM((n, width), BF16),
            pltpu.VMEM((2 * n, width), BF16), pltpu.VMEM((2 * n, width), BF16),
            pltpu.VMEM((2, n, width), F32), pltpu.VMEM((2, n, width), BF16),
            pltpu.VMEM((2, n, width), BF16),
            pltpu.VMEM((2, TOKEN_ROWS, d), BF16), pltpu.VMEM((2, TOKEN_ROWS, d), F32),
            pltpu.VMEM((n // TOKEN_ROWS, TOKEN_ROWS, d), BF16),
        ]
        + power_scratch(modes, MOMENT_INNER, n // MOMENT_INNER)
        + [
            pltpu.VMEM((4, modes, LANES), F32), pltpu.VMEM((2, 4 * modes + 8, width), F32),
            pltpu.VMEM((8, d), F32), rows, rows, rows,
            pltpu.VMEM(in_keep.shape, F32), pltpu.VMEM(in_keep.shape, BF16),
            pltpu.VMEM(in_keep.shape, BF16),
            pltpu.VMEM(in_keep.shape, F32), pltpu.VMEM(in_keep.shape, BF16),
            pltpu.VMEM(in_keep.shape, BF16),
            pltpu.VMEM(glu_keep.shape, F32), pltpu.VMEM(glu_keep.shape, BF16),
            big, big, pltpu.VMEM((block_rows, cols), BF16),
        ]
        + [pltpu.VMEM((kept - 1, block_rows, d), BF16)] * 4
        + [pltpu.VMEM((blocks - 1, block_rows, cols), BF16)] * 2
        + [small, small, pltpu.VMEM((bits + 2, small_rows, width), F32)]
        + [pltpu.SemaphoreType.DMA((48,))]
        + [pltpu.SemaphoreType.DMA((copies,))] * 2,
        compiler_params=params_of(collective_id=4, has_side_effects=True),
        name="back_kernel",
    )(
        ga, mixed, x, xs, ks, fwd, inv, source, resid, in_keep, in_x, in_y, out_keep, out_come, out_z,
        glu_keep, glu_box, skip, gains, gain2, bias2, packed, log_dt,
    )


def GLU_ORDER(bits):
    return list(reversed(range(bits)))


BACK_ROUNDS = {1: ("in", "out"), 3: ("glu", "in"), "norm": ("out", "in", "glu")}


def last_body(
    in_all, out_all, glu_all, small, in_total, out_total, value_total, gate_total, *rest, modes
):
    core = lax.axis_index("core")
    out_total[...] = out_all[...].astype(F32)
    width = in_all.shape[2]
    half = glu_all.shape[2] // 2
    for i in range(2):
        in_total[:, i * width : (i + 1) * width] = in_all[i].astype(F32)
        value_total[:, i * half : (i + 1) * half] = glu_all[i, :, :half].astype(F32)
        gate_total[:, i * half : (i + 1) * half] = glu_all[i, :, half:].astype(F32)

    @pl.when(pl.program_id(0) == 0)
    def _():
        count = small.shape[2]
        top = 4 * modes
        spans = [(i * modes, modes) for i in range(4)] + [(top + i, 1) for i in (0, 8, 9, 10, 11, 12)]
        for ref, (first, rows) in zip(rest, spans):
            for i, which in ((-2, core), (-1, 1 - core)):
                at = pl.ds(pl.multiple_of(which * count, count), count)
                ref[:, at] = small[small.shape[0] + i, first : first + rows, :]


def last_kernel(in_all, out_all, glu_all, small):
    d = in_all.shape[1]
    steps = 8
    modes = (small.shape[1] - 16) // 4
    units, cols, count = in_all.shape[2], glu_all.shape[2], 2 * small.shape[2]
    shape = jax.ShapeDtypeStruct

    def rows(count, width):
        return pl.BlockSpec((count // steps, width), lambda i: (i, 0))

    def pair(width):
        return pl.BlockSpec((2, d // steps, width), lambda i: (0, i, 0))

    def whole(shape):
        return pl.BlockSpec(shape, lambda i: (0,) * len(shape))

    sizes = [(modes, count)] * 4 + [(1, count)] * 6
    return pl.pallas_call(
        functools.partial(last_body, modes=modes),
        grid=(steps,),
        in_specs=[
            pair(units), rows(2 * units, d), pair(cols), whole(small.shape),
        ],
        out_specs=[rows(d, 2 * units), rows(2 * units, d), rows(d, cols), rows(d, cols)]
        + [whole(size) for size in sizes],
        out_shape=[
            shape((d, 2 * units), F32), shape((2 * units, d), F32),
            shape((d, cols), F32), shape((d, cols), F32),
        ]
        + [shape(size, F32) for size in sizes],
        compiler_params=params_of(),
        name="last_kernel",
    )(in_all, out_all, glu_all, small)


SWAP = ((0, 1), (1, 0))


def over_tensor(values):
    return lax.ppermute(values, "tensor", SWAP)


def over_pair(values, flip):
    size = lax.axis_size("pair")
    return lax.ppermute(values, "pair", [(p, p ^ flip) for p in range(size)])


def together(*values):
    return lax.optimization_barrier(values)


def shards(
    inputs, counts, ln1_gain, ln1_bias, log_dt, log_a, freq, c_real, c_imag, skip_gain,
    w_value, w_gate, ln2_gain, ln2_bias, w_in, w_out, cotangent,
):
    _, length, width = inputs.shape
    source = inputs.reshape(length, width)
    gains = jnp.stack([ln1_gain, ln1_bias, ln2_gain, ln2_bias]).astype(F32)
    table = transform_table(length)
    fwd = jnp.asarray(table.astype(ml_dtypes.bfloat16))
    inv = jnp.asarray(np.ascontiguousarray((table.T / length).astype(ml_dtypes.bfloat16)))
    (
        packed, log_dts, skip, grad_low, normed1, mixed, act, spectrum, kernel_spectrum,
        value_proj, gate_sig, residual, normed2, normed2_t,
        value_direct, value_via, gate_direct, gate_via, in_direct, in_via, out_direct, out_via,
    ) = front_kernel(
        source, cotangent.reshape(length, width), counts, gains, log_dt[None], skip_gain[None],
        log_a.T, freq.T, c_real.T, c_imag.T, fwd, inv, w_value, w_gate, w_in, w_out,
    )
    glu_weights = (w_value, value_direct, value_via, w_gate, gate_direct, gate_via)
    units = in_direct.shape[1]
    far_ffn, far_normed2, there_box, there_keep, there_out = ffn_kernel(
        normed2, normed2_t, grad_low, (in_via, in_direct), (out_via, out_direct), units, residual
    )
    normed2, there_out, there_box = together(normed2, there_out, there_box)
    out_come, there_come = over_tensor(there_out), over_pair(there_box, 1)
    own_sums = ffn_kernel(
        normed2, normed2_t, grad_low, (w_in, w_in), (w_out, w_out), units, far_ffn,
        (counts, far_normed2),
    )
    own_sums, out_come, there_come = together(own_sums, out_come, there_come)
    output, grad_normed2, in_box, in_keep, here_out = own_sums
    blocks = lax.axis_size("pair")
    split = (blocks // 2, 2, width // blocks, width)
    here_out, out_come = here_out.reshape(split), out_come.reshape(split)
    (
        grad_residual, grad_act, gain_second_grad, bias_second_grad, there_glu, here_glu,
        in_x, in_y, out_z,
    ) = glu_back_kernel(
        grad_normed2, residual, grad_low, value_proj, gate_sig, act, glu_weights, gains,
        there_keep, there_come, in_box, here_out, out_come,
    )
    halved = (blocks // 2, width // blocks, width)
    by_block = (blocks, width // blocks, -1)
    input_grad, in_all, out_all, glu_all, small = back_kernel(
        grad_act, mixed, normed1, spectrum, kernel_spectrum, fwd, inv, source, grad_residual,
        in_keep.reshape(halved), in_x.reshape(halved), in_y.reshape(halved),
        here_out, out_come, out_z, here_glu.reshape(by_block), there_glu.reshape(by_block),
        skip, gains, gain_second_grad, bias_second_grad, packed, log_dts,
    )
    (
        in_total, out_total, value_total, gate_total,
        log_a_grad, freq_grad, real_grad, imag_grad, *vectors,
    ) = last_kernel(
        in_all.reshape(2, width, -1), out_all.reshape(-1, width), glu_all.reshape(2, width, -1), small
    )
    log_dt_grad, skip_grad, gain1, bias1, gain2, bias2 = (v.reshape(-1) for v in vectors)
    return (
        output.reshape(inputs.shape),
        input_grad.reshape(inputs.shape),
        gain1,
        bias1,
        log_dt_grad,
        log_a_grad.T,
        freq_grad.T,
        real_grad.T,
        imag_grad.T,
        skip_grad,
        value_total,
        gate_total,
        gain2,
        bias2,
        in_total,
        out_total,
    )


def solution(mesh):
    devices = mesh.devices
    cores = jax.sharding.Mesh(
        devices.reshape(devices.shape[0] // 2, 2, devices.shape[1]), ("pair", "core", "tensor")
    )
    batch, every = ("pair", "core"), ("pair", "core", "tensor")
    in_specs = (
        P(every, None, None), P(batch), P(), P(), P("tensor"), P("tensor", None), P("tensor", None),
        P("tensor", None), P("tensor", None), P("tensor"), P(None, "tensor"), P(None, "tensor"),
        P(), P(), P(None, "tensor"), P("tensor", None), P(every, None, None),
    )
    out_specs = (
        P(every, None, None), P(every, None, None), P("tensor"), P("tensor"), P("tensor"),
        P("tensor", None), P("tensor", None), P("tensor", None), P("tensor", None), P("tensor"),
        P(None, "tensor"), P(None, "tensor"), P("tensor"), P("tensor"), P(None, "tensor"),
        P("tensor", None),
    )
    return jax.shard_map(shards, mesh=cores, in_specs=in_specs, out_specs=out_specs, check_vma=False)
```

```python
import functools

import ml_dtypes
import numpy as np

import jax
import jax.numpy as jnp
from jax import lax
from jax.experimental import pallas as pl
from jax.experimental.pallas import tpu as pltpu
from jax.sharding import PartitionSpec as P

VMEM_LIMIT = 60 * 1024 * 1024
F32, BF16 = jnp.float32, jnp.bfloat16
LANES = 128
MESH = pl.DeviceIdType.MESH
KERNEL_INNER = 64
MOMENT_INNER = 32
CB = 256
DFT_ROWS = 512
TOKEN_ROWS = 256
FFN_TILE = 512
GELU_A = 0.7978845608028654
GELU_B = 0.044715
norm_eps = 1e-05


def params_of(**extra):
    return pltpu.CompilerParams(vmem_limit_bytes=VMEM_LIMIT, **extra)


class CoreExchange:
    def __init__(self, pairs, send, recv):
        self.pairs, self.send, self.recv = pairs, send, recv
        self.other = {"core": 1 - lax.axis_index("core")}

    def copies(self, slot):
        return [
            pltpu.make_async_remote_copy(
                src_ref=mine.at[slot], dst_ref=theirs.at[slot],
                send_sem=self.send.at[i, slot], recv_sem=self.recv.at[i, slot],
                device_id=self.other, device_id_type=MESH,
            )
            for i, (mine, theirs) in enumerate(self.pairs)
        ]

    def start(self, slot):
        for copy in self.copies(slot):
            copy.start()

    def arrived(self, slot):
        for copy in self.copies(slot):
            copy.wait_recv()

    def sent(self, slots):
        for slot in range(slots):
            for copy in self.copies(slot):
                copy.wait_send()


class Posts:
    def __init__(self, bits, send, recv):
        self.bits, self.send, self.recv, self.used = bits, send, recv, 0
        self.place = lax.axis_index("pair")
        self.started = []

    def bit(self, b):
        return lax.rem(lax.div(self.place, 1 << b), 2)

    def device(self, link):
        if isinstance(link, str):
            return {link: 1 - lax.axis_index(link)}
        return {"pair": self.place + (1 - 2 * self.bit(link)) * (1 << link)}

    def block(self, flipped):
        at = 0
        for b in range(self.bits):
            here = 1 - self.bit(b) if flipped >> b & 1 else self.bit(b)
            at = at + here * (1 << (self.bits - 1 if b == 0 else b - 1))
        return at

    def slot(self):
        self.used += 1
        return self.used - 1

    def copy(self, src, dst, slot, link):
        return pltpu.make_async_remote_copy(
            src_ref=src, dst_ref=dst, send_sem=self.send.at[slot], recv_sem=self.recv.at[slot],
            device_id=self.device(link), device_id_type=MESH,
        )

    def post(self, src, dst, slot, link):
        copy = self.copy(src, dst, slot, link)
        copy.start()
        self.started.append(copy)

    def await_(self, dst, slot, link):
        self.copy(dst, dst, slot, link).wait_recv()

    def greet(self, links):
        for link in links:
            pl.semaphore_signal(
                pltpu.get_barrier_semaphore(), inc=1, device_id=self.device(link),
                device_id_type=MESH,
            )

    def meet(self, count):
        pl.semaphore_wait(pltpu.get_barrier_semaphore(), count)

    def finish(self):
        for copy in self.started:
            copy.wait_send()


def exchange_sems(pairs, slots):
    return [pltpu.SemaphoreType.DMA((pairs, slots))] * 2


def transform_table(length):
    f = np.arange(length, dtype=np.int64)[:, None]
    t = np.arange(length, dtype=np.int64)[None, :]
    turn = ((4 * f + 1) * t) % (4 * length)
    angle = turn * (2.0 * np.pi / (4 * length))
    return np.concatenate([np.cos(angle), -np.sin(angle)], axis=0)


def cmul(a, b):
    return a[0] * b[0] - a[1] * b[1], a[0] * b[1] + a[1] * b[0]


def log2_of(count):
    bits = count.bit_length() - 1
    assert 1 << bits == count
    return bits


def fill_powers(base, count, out_r, out_i, tmp, scale=None):
    bits = log2_of(count)
    p = base
    for i in range(bits):
        tmp[2 * i] = p[0]
        tmp[2 * i + 1] = p[1]
        p = cmul(p, p)
    if scale is not None:
        tmp[2 * bits] = scale[0]
        tmp[2 * bits + 1] = scale[1]
    row = lax.broadcasted_iota(jnp.int32, (8, LANES), 0)

    def mode(n, carry):
        def at(i):
            return tuple(
                jnp.broadcast_to(tmp[2 * i + j, pl.ds(n, 1), :], (8, LANES)) for j in range(2)
            )

        if scale is None:
            p = (jnp.ones((8, LANES), F32), jnp.zeros((8, LANES), F32))
        else:
            p = at(bits)
        for bit in range(3):
            q = cmul(p, at(bit))
            on = (row & (1 << bit)) != 0
            p = (jnp.where(on, q[0], p[0]), jnp.where(on, q[1], p[1]))
        parts = [p]
        for bit in range(3, bits):
            w = at(bit)
            parts += [cmul(x, w) for x in parts]
        for j, part in enumerate(parts):
            out_r[n, 8 * j : 8 * j + 8, :] = part[0]
            out_i[n, 8 * j : 8 * j + 8, :] = part[1]
        return carry

    lax.fori_loop(0, base[0].shape[0], mode, 0)
    return p


def split_params(packed_ref, log_dt_ref):
    rows = packed_ref[...]
    modes = rows.shape[0] // 4
    log_a, freq, c_real, c_imag = (rows[i * modes : (i + 1) * modes] for i in range(4))
    step = jnp.exp(log_dt_ref[...])
    rate = jnp.exp(log_a)
    decay = jnp.exp(-(step * rate))
    turn = step * freq
    return step, rate, freq, c_real, c_imag, (decay * jnp.cos(turn), decay * jnp.sin(turn))


def kernel_block(packed_ref, log_dt_ref, k_ref, zr, zi, wr, wi, tmp):
    step, _, _, c_real, c_imag, z = split_params(packed_ref, log_dt_ref)
    inner = KERNEL_INNER
    outer = k_ref.shape[0] // inner
    modes = c_real.shape[0]
    z_inner = fill_powers(z, inner, zr, zi, tmp)
    fill_powers(z_inner, outer, wr, wi, tmp, (2.0 * step * c_real, 2.0 * step * c_imag))
    group = 2

    def rows(i, carry):
        d = i * group
        acc = [jnp.zeros((inner, LANES), F32) for _ in range(group)]
        for n in range(modes):
            a, b = zr[n], zi[n]
            for u in range(group):
                acc[u] = acc[u] + (
                    wr[n, pl.ds(d + u, 1), :] * a - wi[n, pl.ds(d + u, 1), :] * b
                )
        for u in range(group):
            at = pl.ds(pl.multiple_of((d + u) * inner, inner), inner)
            k_ref[at, :] = acc[u].astype(BF16)
        return carry

    lax.fori_loop(0, outer // group, rows, 0)


def power_scratch(modes, inner, outer):
    return (
        [pltpu.VMEM((modes, inner, LANES), F32)] * 2
        + [pltpu.VMEM((modes, outer, LANES), F32)] * 2
        + [pltpu.VMEM((20, modes, LANES), F32)]
    )


def moments_block(packed_ref, log_dt_ref, g_ref, out_ref, zr, zi, wr, wi, tmp, sums):
    step, rate, freq, c_real, c_imag, z = split_params(packed_ref, log_dt_ref)
    inner, outer = zr.shape[1], wr.shape[1]
    z_inner = fill_powers(z, inner, zr, zi, tmp)
    fill_powers(z_inner, outer, wr, wi, tmp)
    modes = c_real.shape[0]
    pos = lax.broadcasted_iota(jnp.int32, (inner, LANES), 0).astype(F32)

    def mode(n, carry):
        zero = jnp.zeros((inner, LANES), F32)
        sr, si, tr, ti = zero, zero, zero, zero
        for d in reversed(range(outer)):
            v = g_ref[d * inner : (d + 1) * inner, :]
            sr = sr + v * wr[n, d : d + 1, :]
            si = si + v * wi[n, d : d + 1, :]
            if d > 0:
                tr = tr + sr
                ti = ti + si
        zn = (zr[n], zi[n])
        first = cmul(zn, (sr, si))
        second = cmul(zn, (pos * sr + float(inner) * tr, pos * si + float(inner) * ti))
        for j, v in enumerate(first + second):
            sums[j, pl.ds(n, 1), :] = jnp.sum(v, axis=0, keepdims=True)
        return carry

    lax.fori_loop(0, modes, mode, 0)
    scale = 2.0 * step
    real_grad, imag_grad = scale * sums[0], -scale * sums[1]
    slope_r = scale * (c_real * sums[2] - c_imag * sums[3])
    slope_i = scale * (c_real * sums[3] + c_imag * sums[2])
    log_a_grad = -step * rate * slope_r
    freq_grad = -step * slope_i
    log_dt_grad = jnp.sum(
        c_real * real_grad + c_imag * imag_grad + log_a_grad + freq * freq_grad,
        axis=0, keepdims=True,
    )
    for i, part in enumerate((log_a_grad, freq_grad, real_grad, imag_grad)):
        out_ref[i * modes : (i + 1) * modes, :] = part
    top = 4 * modes
    row = lax.broadcasted_iota(jnp.int32, (8, LANES), 0)
    out_ref[top : top + 8, :] = jnp.where(row == 0, log_dt_grad, 0.0)


def gelu_both(v):
    sq = v * v
    th = jnp.tanh(v * (GELU_A + (GELU_A * GELU_B) * sq))
    rise = 0.5 + 0.5 * th
    act = v * rise
    slope = rise + act * (1.0 - rise) * (2.0 * GELU_A + (6.0 * GELU_A * GELU_B) * sq)
    return act, slope


def gelu(v):
    return gelu_both(v)[0]


def gelu_slope(v):
    return gelu_both(v)[1]


def dot(a, b):
    return jnp.dot(a, b, preferred_element_type=F32)


def conv_block(x, k, skip, fwd_ref, inv_ref, mixed_ref, act_ref, xs_ref, ks_ref, ys):
    n = x.shape[0]
    for i in range(n // DFT_ROWS):
        re = pl.ds(i * DFT_ROWS, DFT_ROWS)
        im = pl.ds(n + i * DFT_ROWS, DFT_ROWS)
        xr, xi = dot(fwd_ref[re, :], x), dot(fwd_ref[im, :], x)
        kr, ki = dot(fwd_ref[re, :], k), dot(fwd_ref[im, :], k)
        xs_ref[re, :] = xr.astype(BF16)
        xs_ref[im, :] = xi.astype(BF16)
        ks_ref[re, :] = kr.astype(BF16)
        ks_ref[im, :] = ki.astype(BF16)
        ys[re, :] = (xr * kr - xi * ki).astype(BF16)
        ys[im, :] = (xr * ki + xi * kr).astype(BF16)
    y = ys[...]
    for i in range(n // TOKEN_ROWS):
        at = pl.ds(i * TOKEN_ROWS, TOKEN_ROWS)
        mixed = dot(inv_ref[at, :], y) + skip * x[i * TOKEN_ROWS : (i + 1) * TOKEN_ROWS].astype(F32)
        mixed_ref[at, :] = mixed
        act_ref[at, :] = gelu(mixed).astype(BF16)


def front_body(
    inputs, cot, counts, gains, log_dt, skip, log_a, freq, c_real, c_imag, fwd_hbm, inv_hbm,
    w_value, w_gate, w_in, w_out,
    packed_ref, vec_ref, skip_ref, grad_ref, x_out, mixed_out, act_out, xs_out, ks_out,
    value_out, sig_out, residual_out, n2_out, n2t_out,
    value_direct, value_via, gate_direct, gate_via, in_direct, in_via, out_direct, out_via,
    zr, zi, wr, wi, tmp, fwd, inv, packed, vec, got_vec, nx, k, mixed, act, xs, ks, ys,
    owns, fars, values, gates, value_s, sig_s, residual_s, n2_s, n2t_s,
    local, send, recv, *, bits
):
    posts = Posts(bits, send, recv)
    core, side = lax.axis_index("core"), lax.axis_index("tensor")
    half = packed.shape[2]
    modes = log_a.shape[0]
    posts.greet([0, 1, "core", "tensor"])
    tables = [
        pltpu.make_async_copy(src, dst, local.at[i])
        for i, (src, dst) in enumerate(
            ((fwd_hbm, fwd), (inv_hbm, inv), (w_value, owns.at[0]), (w_gate, owns.at[1]))
        )
    ]
    for copy in tables:
        copy.start()
    mine = pl.ds(pl.multiple_of(core * half, half), half)
    for i, ref in enumerate((log_a, freq, c_real, c_imag)):
        packed[1, i * modes : (i + 1) * modes, :] = ref[:, mine]
    vec[0:1, :] = log_dt[...]
    vec[1:2, :] = skip[...]
    posts.meet(4)

    def exchange(src, dst, link):
        slot = posts.slot()
        posts.post(src, dst, slot, link)
        return lambda: posts.await_(dst, slot, link)

    params_come = [
        exchange(packed.at[1], packed.at[0], "tensor"), exchange(vec, got_vec, "tensor")
    ]
    rows = value_direct.shape[0] // 4
    place = 2 * posts.bit(1) + posts.bit(0)

    def quarter(at, part=None):
        first, count = (0, rows) if part is None else (part * (rows // 2), rows // 2)
        return pl.ds(pl.multiple_of(at * rows + first, rows // 2), count)

    def cols(count):
        return pl.ds(pl.multiple_of(core * count, count), count)

    near, up, across = (place + 1 - 2 * posts.bit(0)), (place + 2 - 4 * posts.bit(1)), 3 - place
    out_row = pl.multiple_of(core * (4 * rows) + place * rows, rows)
    sources = [
        [(w_value.at[quarter(place), cols(half)], value_direct, value_via),
         (w_gate.at[quarter(place), cols(half)], gate_direct, gate_via)],
        [(w_in.at[quarter(place), cols(in_direct.shape[1])], in_direct, in_via)],
        [(w_out.at[pl.ds(out_row, rows), :], out_direct, out_via)],
    ]

    def fetch_steps(items):
        slots = []
        for src, direct, via in items:
            took = [posts.slot() for _ in range(9)]
            slots.append(took)
            posts.post(src, direct.at[quarter(place)], took[0], "tensor")
        yield
        for (src, direct, via), took in zip(items, slots):
            own = direct.at[quarter(place)]
            posts.await_(own, took[0], "tensor")
            posts.post(own, own, took[1], 0)
            posts.post(own, own, took[2], 1)
            posts.post(own, via.at[quarter(place)], took[5], "core")
        yield
        for (src, direct, via), took in zip(items, slots):
            for link, at, slot, on, over, piece in (
                (0, near, 1, 3, 1, 0), (1, up, 2, 4, 0, 1)
            ):
                come = direct.at[quarter(at)]
                posts.await_(come, took[slot], link)
                passed = direct.at[quarter(at, piece)]
                posts.post(passed, passed, took[on], over)
                posts.post(come, via.at[quarter(at)], took[5 + slot], "core")
        yield
        for (src, direct, via), took in zip(items, slots):
            for slot, link, piece in ((3, 1, 0), (4, 0, 1)):
                posts.await_(direct.at[quarter(across, piece)], took[slot], link)
            come = direct.at[quarter(across)]
            posts.post(come, via.at[quarter(across)], took[8], "core")
        yield
        for (src, direct, via), took in zip(items, slots):
            for at, slot in ((place, 5), (near, 6), (up, 7), (across, 8)):
                posts.await_(via.at[quarter(at)], took[slot], "core")

    flows = [fetch_steps(items) for items in sources]
    for flow in flows:
        next(flow)

    def kernel_of(j, log_dt, between=lambda: None):
        for i in range(half // LANES):
            if i:
                between()
            at = pl.ds(i * LANES, LANES)
            kernel_block(packed.at[1 - j, :, at], log_dt.at[:, at], k.at[2 * j, :, at], zr, zi, wr, wi, tmp)

    vec_ref[1] = vec[0:1, mine]
    kernel_of(0, vec_ref.at[1])
    kernels_come = [exchange(k.at[0], k.at[1], "core")]
    for come in params_come:
        come()
    vec_ref[0] = got_vec[0:1, mine]
    kernel_of(1, vec_ref.at[0], lambda: next(flows[0]))
    kernels_come.append(exchange(k.at[2], k.at[3], "core"))
    for i in range(nx.shape[0] // TOKEN_ROWS):
        at = pl.ds(i * TOKEN_ROWS, TOKEN_ROWS)
        source = inputs[at, :].astype(F32)
        nx[at, :] = norm_forward(source, gains[0:1, :], gains[1:2, :])[0].astype(BF16)
    used = (side < counts[0]).astype(F32)
    grad_ref[...] = (used * cot[...].astype(F32)).astype(BF16)
    width = vec.shape[1]
    for ref, at in ((vec, side), (got_vec, 1 - side)):
        skip_ref[:, pl.ds(pl.multiple_of(at * width, width), width)] = ref[1:2, :]
    stores = [
        pltpu.make_async_copy(nx, x_out, local.at[4]),
        pltpu.make_async_copy(packed, packed_ref, local.at[5]),
    ]
    for copy in stores:
        copy.start()
    for copy in tables:
        copy.wait()
    next(flows[0])
    next(flows[1])
    plan = ((0, None), (2, flows[2]), (1, flows[1]), (3, flows[0]))
    for n, (j, flow) in enumerate(plan):
        there = lax.rem(side + j // 2, 2)
        which = lax.rem(core + j % 2, 2)
        at = pl.ds(pl.multiple_of((2 * there + which) * half, half), half)
        if j % 2:
            kernels_come[j // 2]()
        params = vec if j < 2 else got_vec
        skip = params[1:2, pl.ds(pl.multiple_of(which * half, half), half)]
        conv_block(
            nx[:, at], k[j], skip, fwd, inv, mixed.at[j], act.at[:, at], xs.at[j], ks.at[j], ys
        )
        for i, (src, dst) in enumerate(
            ((mixed.at[j], mixed_out.at[j]), (xs.at[j], xs_out.at[j]), (ks.at[j], ks_out.at[j]))
        ):
            copy = pltpu.make_async_copy(src, dst, local.at[6 + 3 * j + i])
            copy.start()
            stores.append(copy)
        if flow is not None:
            next(flow)
    next(flows[0], None)
    loads = [
        pltpu.make_async_copy(src, fars.at[i], local.at[18 + i])
        for i, src in enumerate((value_direct, value_via, gate_direct, gate_via))
    ]
    for copy in loads:
        copy.start()
    stores.append(pltpu.make_async_copy(act, act_out, local.at[22]))
    stores[-1].start()
    for copy in loads:
        copy.wait()
    services = {0: [flows[2]], 1: [flows[1]], 2: [], 3: []}
    for r in range(nx.shape[0] // TOKEN_ROWS):
        at = pl.ds(r * TOKEN_ROWS, TOKEN_ROWS)
        left = act[at, :]
        project_all(left, owns.at[0], fars.at[0], fars.at[1], values)
        project_all(left, owns.at[1], fars.at[2], fars.at[3], gates)
        value = values[...]
        sig = 1.0 / (1.0 + jnp.exp(-gates[...]))
        value_s[r] = value.astype(BF16)
        sig_s[r] = sig.astype(BF16)
        residual = inputs[at, :].astype(F32) + (value * sig).astype(BF16).astype(F32)
        residual_s[r] = residual
        n2 = norm_forward(residual, gains[2:3, :], gains[3:4, :])[0].astype(BF16)
        n2_s[r] = n2
        n2t_s[r] = n2.T
        for i, (src, dst) in enumerate((
            (value_s, value_out.at[at]), (sig_s, sig_out.at[at]), (residual_s, residual_out.at[at]),
            (n2_s, n2_out.at[at]), (n2t_s, n2t_out.at[:, at]),
        )):
            copy = pltpu.make_async_copy(src.at[r], dst, local.at[23 + 5 * r + i])
            copy.start()
            stores.append(copy)
        for flow in services[r]:
            next(flow)
    for flow in (flows[1], flows[2], flows[2]):
        next(flow, None)
    for copy in stores:
        copy.wait()
    posts.finish()


def front_kernel(
    inputs, cot, counts, gains, log_dt, skip, log_a, freq, c_real, c_imag, fwd, inv,
    w_value, w_gate, w_in, w_out,
):
    bits = log2_of(lax.axis_size("pair"))
    n, d = inputs.shape
    modes = log_a.shape[0]
    half = d // 4
    units = w_in.shape[1] // 2
    chunks = n // TOKEN_ROWS
    vmem = pl.BlockSpec(memory_space=pltpu.VMEM)
    hbm = pl.BlockSpec(memory_space=pl.ANY)
    shape = jax.ShapeDtypeStruct
    return pl.pallas_call(
        functools.partial(front_body, bits=bits),
        in_specs=[vmem] * 2 + [pl.BlockSpec(memory_space=pltpu.SMEM)] + [vmem] * 7 + [hbm] * 6,
        out_specs=[hbm, vmem, vmem, vmem] + [hbm] * 18,
        out_shape=[
            shape((2, 4 * modes, half), F32), shape((2, 1, half), F32), shape((1, d), F32),
            shape((n, d), BF16), shape((n, d), BF16), shape((4, n, half), F32), shape((n, d), BF16),
            shape((4, 2 * n, half), BF16), shape((4, 2 * n, half), BF16),
            shape((n, d), BF16), shape((n, d), BF16), shape((n, d), F32), shape((n, d), BF16),
            shape((d, n), BF16),
        ]
        + [shape((d, half), BF16)] * 4
        + [shape((d, units), BF16)] * 2
        + [shape((units, d), BF16)] * 2,
        scratch_shapes=power_scratch(modes, KERNEL_INNER, n // KERNEL_INNER)
        + [
            pltpu.VMEM(fwd.shape, BF16), pltpu.VMEM(inv.shape, BF16),
            pltpu.VMEM((2, 4 * modes, half), F32),
            pltpu.VMEM((2, d // 2), F32), pltpu.VMEM((2, d // 2), F32),
            pltpu.VMEM((n, d), BF16), pltpu.VMEM((4, n, half), BF16),
            pltpu.VMEM((4, n, half), F32), pltpu.VMEM((n, d), BF16),
            pltpu.VMEM((4, 2 * n, half), BF16), pltpu.VMEM((4, 2 * n, half), BF16),
            pltpu.VMEM((2 * n, half), BF16),
            pltpu.VMEM((2, d, 2 * half), BF16), pltpu.VMEM((4, d, half), BF16),
            pltpu.VMEM((TOKEN_ROWS, d), F32), pltpu.VMEM((TOKEN_ROWS, d), F32),
            pltpu.VMEM((chunks, TOKEN_ROWS, d), BF16), pltpu.VMEM((chunks, TOKEN_ROWS, d), BF16),
            pltpu.VMEM((chunks, TOKEN_ROWS, d), F32), pltpu.VMEM((chunks, TOKEN_ROWS, d), BF16),
            pltpu.VMEM((chunks, d, TOKEN_ROWS), BF16),
            pltpu.SemaphoreType.DMA((24 + 5 * chunks,)),
            pltpu.SemaphoreType.DMA((40,)), pltpu.SemaphoreType.DMA((40,)),
        ],
        compiler_params=params_of(collective_id=5, has_side_effects=True),
        name="front_kernel",
    )(
        inputs, cot, counts, gains, log_dt, skip, log_a, freq, c_real, c_imag, fwd, inv,
        w_value, w_gate, w_in, w_out,
    )


def conv_back_block(ga, mixed, x, xs, ks, skip, fwd, inv, gm, gy, ax, ak, put_gn, put_gk):
    n = x.shape[0]
    total = jnp.zeros((1, x.shape[1]), F32)
    for i in range(n // TOKEN_ROWS):
        at = pl.ds(i * TOKEN_ROWS, TOKEN_ROWS)
        v = ga[at, :] * gelu_slope(mixed[at, :])
        gm[at, :] = v
        gy[at, :] = v.astype(BF16)
        total += jnp.sum(v * x[at, :].astype(F32), axis=0, keepdims=True)
    g = gy[...]
    for i in range(n // DFT_ROWS):
        re = pl.ds(i * DFT_ROWS, DFT_ROWS)
        im = pl.ds(n + i * DFT_ROWS, DFT_ROWS)
        gr, gi = dot(fwd[re, :], g), dot(fwd[im, :], g)
        for src, dst in ((ks, ax), (xs, ak)):
            a, b = src[re, :].astype(F32), src[im, :].astype(F32)
            dst[re, :] = (a * gr + b * gi).astype(BF16)
            dst[im, :] = (a * gi - b * gr).astype(BF16)
    yx = ax[...]
    yk = ak[...]
    for i in range(n // TOKEN_ROWS):
        at = pl.ds(i * TOKEN_ROWS, TOKEN_ROWS)
        put_gk(at, dot(inv[at, :], yk))
        put_gn(at, dot(inv[at, :], yx) + skip * gm[at, :])
    return total


def project_all(left, own, direct, via, out):
    core, side = lax.axis_index("core"), lax.axis_index("tensor")
    width = direct.shape[1]
    far = (1 - side) * 2 * width
    for ref, first, count in (
        (own, side * 2 * width, 2 * width), (direct, far + core * width, width),
        (via, far + (1 - core) * width, width),
    ):
        out[:, pl.ds(pl.multiple_of(first, width), count)] = dot(left, ref[...])


def glu_back_body(
    g_sum, residual, cot, value, sig, act, value_own, value_direct, value_via,
    gate_own, gate_direct, gate_via, gains,
    there_keep, there_come, in_box, here_out, out_come,
    resid_ref, ga_ref, gain_ref, bias_ref, there_ref, here_ref, in_x, in_y, out_z,
    gv, gt, mine, theirs, in_a, in_b, out_a, out_b, out_box, local, send, recv, *, bits
):
    step = pl.program_id(0)
    posts = Posts(bits, send, recv)
    links = [0, 1, "core", "tensor"]
    slots = {name: posts.slot() for name in ("x", "y", "z")}
    swap = [posts.slot(), posts.slot()]

    def transfers():
        return [
            posts.copy(in_box, in_x, slots["x"], 0),
            posts.copy(in_a, in_y, slots["y"], "tensor"),
            posts.copy(out_box, out_z, slots["z"], 1),
        ]

    @pl.when(step == 0)
    def _():
        posts.greet(links)
        other = 1 - posts.bit(1)
        loads = [
            pltpu.make_async_copy(src, dst, local.at[i])
            for i, (src, dst) in enumerate((
                (there_keep, in_a), (there_come, in_b),
                (here_out.at[:, other], out_a), (out_come.at[:, other], out_b),
            ))
        ]
        for copy in loads:
            copy.start()
        posts.meet(len(links))
        sends = transfers()
        sends[0].start()
        for copy in loads[:2]:
            copy.wait()
        in_a[...] = (in_a[...].astype(F32) + in_b[...].astype(F32)).astype(BF16)
        sends[1].start()
        for copy in loads[2:]:
            copy.wait()
        out_box[...] = (out_a[...] + out_b[...].astype(F32)).astype(BF16)
        sends[2].start()

    chunks = act.shape[0] // TOKEN_ROWS
    width = gv.shape[2]

    @pl.when(step < chunks)
    def _():
        standard, inv_std = norm_forward(residual[...], 1.0, 0.0)[1:]
        part, gain_grad, bias_grad = norm_backward(
            g_sum[...], standard, inv_std, gains[2:3, :]
        )
        new = step == 0
        gain_ref[...] = jnp.where(new, 0.0, gain_ref[...]) + gain_grad[None]
        bias_ref[...] = jnp.where(new, 0.0, bias_ref[...]) + bias_grad[None]
        resid = cot[...].astype(F32) + part
        resid_ref[...] = resid
        grad = resid.astype(BF16).astype(F32)
        gate = sig[...].astype(F32)
        grad_value = (grad * gate).astype(BF16)
        grad_gate = (grad * value[...].astype(F32) * gate * (1.0 - gate)).astype(BF16)
        at = pl.ds(pl.multiple_of(step * TOKEN_ROWS, TOKEN_ROWS), TOKEN_ROWS)
        for i in range(gv.shape[0]):
            gv[i, at, :] = grad_value[:, i * width : (i + 1) * width]
            gt[i, at, :] = grad_gate[:, i * width : (i + 1) * width]
        core, side = lax.axis_index("core"), lax.axis_index("tensor")
        far = 2 * (1 - side)
        total = 0.0
        for grads, own, direct, via in (
            (gv, value_own, value_direct, value_via), (gt, gate_own, gate_direct, gate_via)
        ):
            ours = jnp.concatenate([grads[2 * side, at, :], grads[2 * side + 1, at, :]], axis=1)
            total += contract_cols(ours, own[...])
            total += contract_cols(grads[far + core, at, :], direct[...])
            total += contract_cols(grads[far + 1 - core, at, :], via[...])
        ga_ref[...] = total

    @pl.when(step >= chunks)
    def _():
        j = step - chunks
        side = lax.rem(lax.axis_index("tensor") + 1 + j, 2)
        half = lax.rem(lax.axis_index("core") + 1 + j // 2, 2)
        block = 2 * side + half
        grads = [contract_rows(act[...], gv[block]), contract_rows(act[...], gt[block])]
        for slot in range(2):
            @pl.when(j == slot)
            def _():
                for i, g in enumerate(grads):
                    mine[slot, :, i * width : (i + 1) * width] = g.astype(BF16)
                posts.copy(mine.at[slot], theirs.at[slot], swap[slot], "core").start()

        @pl.when(j == 2)
        def _():
            posts.await_(theirs.at[0], swap[0], "core")
            for i, g in enumerate(grads):
                at = pl.ds(i * width, width)
                there_ref[:, at] = (g + theirs[0, :, at].astype(F32)).astype(BF16)

        @pl.when(j == 3)
        def _():
            posts.await_(theirs.at[1], swap[1], "core")
            for i, g in enumerate(grads):
                at = pl.ds(i * width, width)
                here_ref[:, at] = g + theirs[1, :, at].astype(F32)
            for slot in range(2):
                posts.copy(mine.at[slot], theirs.at[slot], swap[slot], "core").wait_send()
            for copy in transfers():
                copy.wait()


def glu_back_kernel(
    g_sum, residual, cot, value, sig, act, weights, gains,
    there_keep, there_come, in_box, here_out, out_come,
):
    bits = log2_of(lax.axis_size("pair"))
    n, d = act.shape
    chunks = n // TOKEN_ROWS
    width = d // 4
    hbm = pl.BlockSpec(memory_space=pl.ANY)
    extra = (there_keep, there_come, in_box, here_out, out_come)
    split = (here_out.shape[0],) + here_out.shape[2:]

    def whole(a):
        return pl.BlockSpec(a.shape, lambda i: (0, 0), pipeline_mode=pl.Buffered(1))

    rows = pl.BlockSpec((TOKEN_ROWS, d), lambda i: (jnp.minimum(i, chunks - 1), 0))
    vector = pl.BlockSpec((1, d), lambda i: (0, 0))
    weight = pl.BlockSpec((d, 2 * width), lambda i: (0, 0))
    return pl.pallas_call(
        functools.partial(glu_back_body, bits=bits),
        grid=(chunks + 4,),
        in_specs=[rows] * 5 + [whole(act)] + [whole(w) for w in weights] + [whole(gains)] + [hbm] * 5,
        out_specs=[rows, rows, vector, vector, weight, weight] + [hbm] * 3,
        scratch_shapes=[pltpu.VMEM((4, n, width), BF16)] * 2
        + [pltpu.VMEM((2, d, 2 * width), BF16)] * 2
        + [pltpu.VMEM(there_keep.shape, BF16)] * 2
        + [pltpu.VMEM(split, F32), pltpu.VMEM(split, BF16), pltpu.VMEM(split, BF16)]
        + [pltpu.SemaphoreType.DMA((4,))]
        + [pltpu.SemaphoreType.DMA((5,))] * 2,
        out_shape=[
            jax.ShapeDtypeStruct((n, d), F32), jax.ShapeDtypeStruct((n, d), F32),
            jax.ShapeDtypeStruct((1, d), F32), jax.ShapeDtypeStruct((1, d), F32),
            jax.ShapeDtypeStruct((d, 2 * width), BF16), jax.ShapeDtypeStruct((d, 2 * width), F32),
            jax.ShapeDtypeStruct(in_box.shape, BF16), jax.ShapeDtypeStruct(in_box.shape, BF16),
            jax.ShapeDtypeStruct(split, BF16),
        ],
        compiler_params=params_of(collective_id=2, has_side_effects=True),
        name="glu_back_kernel",
    )(g_sum, residual, cot, value, sig, act, *weights, gains, *extra)


def ffn_body(*refs, own):
    n2, n2t, gl, ia, ib, oa, ob, before, *refs = refs
    if own:
        counts, gn2_before, *refs = refs
    first_out, gn2, box_ref, keep_ref, out_ref, *refs = refs
    if own:
        ffn, *refs = refs
    else:
        ffn = first_out
    wi, wo, h, gp, total, in_mine, out_mine, in_theirs, out_theirs, local, send, recv = refs
    step, half = pl.program_id(0), in_mine.shape[0]
    first = step < half
    cores = CoreExchange([(in_mine, in_theirs), (out_mine, out_theirs)], send, recv)
    barrier = pltpu.get_barrier_semaphore()

    def before_loads():
        pairs = [(before, ffn)] + ([(gn2_before, gn2)] if own else [])
        return [pltpu.make_async_copy(src, dst, local.at[i]) for i, (src, dst) in enumerate(pairs)]

    @pl.when(step == 0)
    def _():
        pl.semaphore_signal(barrier, inc=1, device_id=cores.other, device_id_type=MESH)
        for copy in before_loads():
            copy.start()
        if not own:
            gn2[...] = jnp.zeros_like(gn2)

    @pl.when(first)
    def _():
        wi[...] = ia[...]
        wo[...] = oa[...]

    @pl.when(jnp.logical_not(first))
    def _():
        wi[...] = ib[...]
        wo[...] = ob[...]

    w1, w2 = wi[...], wo[...]
    for r in range(n2.shape[0] // TOKEN_ROWS):
        at = pl.ds(r * TOKEN_ROWS, TOKEN_ROWS)
        act, slope = gelu_both(dot(n2[at, :], w1))
        h[at, :] = act.astype(BF16)
        gp[at, :] = (contract_cols(gl[at, :], w2) * slope).astype(BF16)

    @pl.when(step == 0)
    def _():
        for copy in before_loads():
            copy.wait()

    for r in range(n2.shape[0] // TOKEN_ROWS):
        at = pl.ds(r * TOKEN_ROWS, TOKEN_ROWS)
        ffn[at, :] += dot(h[at, :], w2)
        gn2[at, :] += contract_cols(gp[at, :], w1)
    out_grad = contract_rows(h[...], gl[...])
    in_grad = dot(n2t[...], gp[...])

    @pl.when(step == 0)
    def _():
        pl.semaphore_wait(barrier, 1)

    @pl.when(first)
    def _():
        in_mine[step] = in_grad.astype(BF16)
        out_mine[step] = out_grad.astype(BF16)
        cores.start(step)

    @pl.when(jnp.logical_not(first))
    def _():
        cores.arrived(step - half)
        total[...] = in_grad + in_theirs[step - half].astype(F32)
        near, rows = lax.rem(lax.axis_index("pair"), 2), keep_ref.shape[0]
        for ref, at in ((keep_ref, near), (box_ref, 1 - near)):
            part = pl.ds(pl.multiple_of(at * rows, rows), rows)
            ref[...] = total[part, :].astype(ref.dtype)
        out_ref[...] = (out_grad + out_theirs[step - half].astype(F32)).astype(out_ref.dtype)

    @pl.when(step == 2 * half - 1)
    def _():
        if own:
            used = (lax.axis_index("tensor") < counts[0]).astype(F32)
            first_out[...] = (used * ffn[...]).astype(BF16)
        cores.sent(half)


def ffn_kernel(n2, n2t, gl, ins, outs, units, before, own=()):
    n, d = n2.shape
    half = units // FFN_TILE
    owned = bool(own)
    hbm = pl.BlockSpec(memory_space=pl.ANY)

    def whole(a):
        return pl.BlockSpec(a.shape, lambda s: (0, 0), pipeline_mode=pl.Buffered(1))

    def fst(s):
        at = jnp.minimum(s, half - 1)
        return at + (1 - lax.axis_index("core")) * half if owned else at

    def snd(s):
        at = jnp.maximum(s - half, 0)
        return at + lax.axis_index("core") * half if owned else at

    def late(s):
        return jnp.maximum(s - half, 0)

    total = pl.BlockSpec((n, d), lambda s: (0, 0))
    dtype = F32 if owned else BF16
    shape = jax.ShapeDtypeStruct
    return pl.pallas_call(
        functools.partial(ffn_body, own=owned),
        grid=(2 * half,),
        in_specs=[
            whole(n2), whole(n2t), whole(gl),
            pl.BlockSpec((d, FFN_TILE), lambda s: (0, fst(s))),
            pl.BlockSpec((d, FFN_TILE), lambda s: (0, snd(s))),
            pl.BlockSpec((FFN_TILE, d), lambda s: (fst(s), 0)),
            pl.BlockSpec((FFN_TILE, d), lambda s: (snd(s), 0)),
            hbm,
        ]
        + ([pl.BlockSpec(memory_space=pltpu.SMEM), hbm] if owned else []),
        out_specs=[
            total, total,
            pl.BlockSpec((d // 2, FFN_TILE), lambda s: (0, late(s))),
            pl.BlockSpec((d // 2, FFN_TILE), lambda s: (0, late(s))),
            pl.BlockSpec((FFN_TILE, d), lambda s: (late(s), 0)),
        ],
        scratch_shapes=([pltpu.VMEM((n, d), F32)] if owned else [])
        + [
            pltpu.VMEM((d, FFN_TILE), BF16), pltpu.VMEM((FFN_TILE, d), BF16),
            pltpu.VMEM((n, FFN_TILE), BF16), pltpu.VMEM((n, FFN_TILE), BF16),
            pltpu.VMEM((d, FFN_TILE), F32),
        ]
        + [pltpu.VMEM((half, d, FFN_TILE), BF16), pltpu.VMEM((half, FFN_TILE, d), BF16)] * 2
        + [pltpu.SemaphoreType.DMA((2,))]
        + exchange_sems(2, half),
        out_shape=[
            shape((n, d), BF16 if owned else F32), shape((n, d), F32),
            shape((d // 2, units), BF16), shape((d // 2, units), dtype), shape((units, d), dtype),
        ],
        compiler_params=params_of(collective_id=int(owned), has_side_effects=True),
        name="ffn_kernel",
    )(n2, n2t, gl, *ins, *outs, before, *own)


def norm_forward(values, norm_gain, norm_bias):
    center = values - jnp.mean(values, axis=-1, keepdims=True)
    inv_std = lax.rsqrt(jnp.mean(center * center, axis=-1, keepdims=True) + norm_eps)
    standard = center * inv_std
    return (standard * norm_gain + norm_bias, standard, inv_std)


def norm_backward(incoming, standard, inv_std, norm_gain):
    scaled = incoming * norm_gain
    value_grad = inv_std * (
        scaled
        - jnp.mean(scaled, axis=-1, keepdims=True)
        - standard * jnp.mean(scaled * standard, axis=-1, keepdims=True)
    )
    return (value_grad, jnp.sum(incoming * standard, axis=0), jnp.sum(incoming, axis=0))


def contract_rows(left, right):
    return lax.dot_general(left, right, (((0,), (0,)), ((), ())), preferred_element_type=F32)


def contract_cols(left, right):
    return lax.dot_general(left, right, (((1,), (1,)), ((), ())), preferred_element_type=F32)


def scatter_steps(posts, acc, bits, order, boxes, come):
    def at(known, flipped):
        place = 0
        for i, b in enumerate(bits):
            here = posts.bit(b)
            if b in known:
                bit = 1 - here if known[b] else here
            else:
                bit = flipped >> i & 1
            place = place + bit * (1 << i)
        return place

    done = {}
    used = 0
    for n, b in enumerate(order):
        rest = [bits.index(i) for i in order[n + 1 :]]
        combos = [sum((c >> k & 1) << i for k, i in enumerate(rest)) for c in range(1 << len(rest))]
        slots = []
        for c, combo in enumerate(combos):
            slot = posts.slot()
            boxes[used + c] = acc[at({**done, b: True}, combo)].astype(BF16)
            posts.post(boxes.at[used + c], come.at[used + c], slot, b)
            slots.append(slot)
        yield
        done[b] = False
        for c, combo in enumerate(combos):
            posts.await_(come.at[used + c], slots[c], b)
            keep = at(done, combo)
            acc[keep] = acc[keep] + come[used + c].astype(F32)
        used += len(combos)
    posts.result = at(done, 0)


def gather_steps(posts, own, whole, local, order):
    core = lax.axis_index("core")
    count = 1 << posts.bits
    slots = {(rel, link): posts.slot() for rel in range(count) for link in ("bit", "core")}
    first = pltpu.make_async_copy(own, whole.at[core, posts.block(0)], local)
    first.start()

    def pass_on(src, rel, bits):
        dst = whole.at[core, posts.block(rel)]
        for b in bits:
            posts.post(src, dst, slots[rel ^ (1 << b), "bit"], b)
        posts.post(src, dst, slots[rel, "core"], "core")

    pass_on(own, 0, order)
    for n, b in enumerate(order):
        for c in range(1 << n):
            yield
            rel = sum((c >> k & 1) << order[k] for k in range(n)) | 1 << b
            block = whole.at[core, posts.block(rel)]
            posts.await_(block, slots[rel, "bit"], b)
            pass_on(block, rel, order[n + 1 :])
    yield
    first.wait()
    for rel in range(count):
        posts.await_(whole.at[1 - core, posts.block(rel)], slots[rel, "core"], "core")


def back_body(
    ga_hbm, mixed_hbm, x_hbm, xs_hbm, ks_hbm, fwd_hbm, inv_hbm, source_hbm, resid_hbm,
    in_keep, in_x, in_y, out_keep, out_come, out_z, glu_keep, glu_box,
    skip, gains, gain2, bias2, packed, log_dt,
    input_ref, in_all, out_all, glu_all, small_all,
    ga, fwd, inv, mixed, x, xs, ks, gm, gy, ax, ak, gk, gk_mine, gk_theirs, source, resid, staged,
    zr, zi, wr, wi, tmp, sums, moments, rows, rows_mine, rows_other, rows_come,
    in_acc, in_a, in_b, out_acc, out_a, out_b, glu_acc, glu_come, in_own, out_own, glu_own,
    in_boxes, in_got, out_boxes, out_got, glu_boxes, glu_got, small, small_far, small_got,
    local, send, recv, *, bits
):
    posts = Posts(bits, send, recv)
    links = list(range(bits)) + ["core", "tensor"]
    posts.greet(links)
    core, side = lax.axis_index("core"), lax.axis_index("tensor")
    n, width = mixed.shape[1:]
    used = [3]

    def load(src, dst):
        copy = pltpu.make_async_copy(src, dst, local.at[used[0]])
        used[0] += 1
        copy.start()
        return copy

    def columns(i):
        there = lax.rem(side + 1 + i, 2)
        which = lax.rem(core + 1 + i // 2, 2)
        return pl.ds(pl.multiple_of((2 * there + which) * width, width), width)

    def load_block(i):
        j, slot = 2 * ((i + 1) % 2) + 1 - i // 2, i % 2
        return [
            load(mixed_hbm.at[j], mixed.at[slot]), load(x_hbm.at[:, columns(i)], x.at[slot]),
            load(xs_hbm.at[j], xs.at[slot]), load(ks_hbm.at[j], ks.at[slot]),
        ]

    mine = posts.bit(1)
    in_loads = [load(in_keep, in_acc), load(in_x, in_a), load(in_y, in_b)]
    out_loads = [
        load(out_keep.at[:, mine], out_acc), load(out_come.at[:, mine], out_a), load(out_z, out_b)
    ]
    ga_load = load(ga_hbm, ga)
    block_loads = load_block(0)
    tables = [load(fwd_hbm, fwd), load(inv_hbm, inv)]
    glu_load = load(glu_keep, glu_acc)
    posts.meet(len(links))
    near, far = list(range(1, bits)), list(range(2, bits))

    def in_steps():
        for copy in in_loads:
            copy.wait()
        in_acc[...] = in_acc[...] + in_a[...].astype(F32) + in_b[...].astype(F32)
        yield from scatter_steps(posts, in_acc, near, near, in_boxes, in_got)
        in_own[...] = in_acc[posts.result].astype(BF16)
        yield from gather_steps(posts, in_own, in_all, local.at[0], list(reversed(range(bits))))

    def out_steps():
        for copy in out_loads:
            copy.wait()
        out_acc[...] = out_acc[...] + out_a[...].astype(F32) + out_b[...].astype(F32)
        yield from scatter_steps(posts, out_acc, far + [0], [0] + far, out_boxes, out_got)
        out_own[...] = out_acc[posts.result].astype(BF16)
        yield from gather_steps(posts, out_own, out_all, local.at[1], list(reversed(range(bits))))

    def glu_steps():
        slot = posts.slot()
        posts.post(glu_box, glu_come, slot, "tensor")
        yield
        posts.await_(glu_come, slot, "tensor")
        glu_load.wait()
        glu_acc[...] = glu_acc[...] + glu_come[...].astype(F32)
        yield from scatter_steps(posts, glu_acc, near + [0], [0] + near, glu_boxes, glu_got)
        glu_own[...] = glu_acc[posts.result].astype(BF16)
        yield from gather_steps(posts, glu_own, glu_all, local.at[2], GLU_ORDER(bits))

    def small_steps():
        for j in range(2):
            for half, ref in ((core, rows_mine), (1 - core, rows_other)):
                there = lax.rem(side + 1 + j, 2)
                at = pl.multiple_of((2 * there + half) * width, width)
                ref[j] = rows[:, pl.ds(at, width)]
        slot = posts.slot()
        posts.post(rows_other, rows_come, slot, "core")
        yield
        posts.await_(rows_come, slot, "core")
        top = moments.shape[1]
        for j, ref in ((0, small_far), (1, small)):
            ref[:top, :] = moments[j]
            ref[top:, :] = rows_mine[j] + rows_come[j]
        slot = posts.slot()
        posts.post(small_far, small_got.at[0], slot, "tensor")
        yield
        posts.await_(small_got.at[0], slot, "tensor")
        small[...] = small[...] + small_got[0]
        for b in range(bits):
            slot = posts.slot()
            small_all[b] = small[...]
            posts.post(small_all.at[b], small_got.at[1 + b], slot, b)
            yield
            posts.await_(small_got.at[1 + b], slot, b)
            small[...] = small[...] + small_got[1 + b]
        slot = posts.slot()
        small_all[bits] = small[...]
        posts.post(small_all.at[bits], small_got.at[1 + bits], slot, "core")
        yield
        posts.await_(small_got.at[1 + bits], slot, "core")
        small_all[bits + 1] = small_got[1 + bits]

    flows = {"in": in_steps(), "out": out_steps(), "glu": glu_steps()}
    done = object()

    def advance(*names):
        for name in names:
            if name in flows and next(flows[name], done) is done:
                del flows[name]

    advance("glu", "in", "out")
    rows[...] = jnp.zeros_like(rows)
    rows[3:4, :] = gain2[...]
    rows[4:5, :] = bias2[...]
    ga_load.wait()
    slots = [posts.slot(), posts.slot()]
    for i in range(4):
        slot = i % 2
        for copy in block_loads:
            copy.wait()
        if i < 3:
            block_loads = load_block(i + 1)
        if i == 0:
            for copy in tables:
                copy.wait()
        at = columns(i)

        def put_gn(tokens, value, at=at):
            ga[tokens, at] = value

        def put_gk(tokens, value, i=i):
            if i < 2:
                gk_mine[i, tokens, :] = value.astype(BF16)
            else:
                gk[i - 2, tokens, :] = value

        rows[0:1, at] = conv_back_block(
            ga.at[:, at], mixed.at[slot], x.at[slot], xs.at[slot], ks.at[slot], skip[:, at],
            fwd, inv, gm, gy, ax, ak, put_gn, put_gk,
        )
        if i < 2:
            posts.post(gk_mine.at[i], gk_theirs.at[i], slots[i], "core")
        else:
            posts.await_(gk_theirs.at[i - 2], slots[i - 2], "core")
            gk[i - 2] = gk[i - 2] + gk_theirs[i - 2].astype(F32)
        if i in BACK_ROUNDS:
            advance(*BACK_ROUNDS[i])

    chunks = n // TOKEN_ROWS

    def load_rows(r):
        at = pl.ds(r * TOKEN_ROWS, TOKEN_ROWS)
        return [load(source_hbm.at[at], source.at[r % 2]), load(resid_hbm.at[at], resid.at[r % 2])]

    row_loads = load_rows(0)
    stores = []
    for r in range(chunks):
        for copy in row_loads:
            copy.wait()
        if r + 1 < chunks:
            row_loads = load_rows(r + 1)
        at = pl.ds(r * TOKEN_ROWS, TOKEN_ROWS)
        standard, inv_std = norm_forward(source[r % 2].astype(F32), 1.0, 0.0)[1:]
        part, gain_grad, bias_grad = norm_backward(ga[at, :], standard, inv_std, gains[0:1, :])
        rows[1:2, :] = rows[1:2, :] + gain_grad[None]
        rows[2:3, :] = rows[2:3, :] + bias_grad[None]
        staged[r] = (resid[r % 2] + part).astype(BF16)
        stores.append(load(staged.at[r], input_ref.at[at]))
    advance(*BACK_ROUNDS["norm"])

    def block(j, i):
        at = pl.ds(i * LANES, LANES)
        moments_block(
            packed.at[j, :, at], log_dt.at[j, :, at], gk.at[j, :, at], moments.at[j, :, at],
            zr, zi, wr, wi, tmp, sums,
        )

    for j in range(2):
        for i in range(width // LANES):
            block(j, i)
            advance("in", "out", "glu")
    flows["small"] = small_steps()
    while flows:
        advance("small", "in", "out", "glu")
    for copy in stores:
        copy.wait()
    posts.finish()


def back_kernel(
    ga, mixed, x, xs, ks, fwd, inv, source, resid, in_keep, in_x, in_y, out_keep, out_come, out_z,
    glu_keep, glu_box, skip, gains, gain2, bias2, packed, log_dt,
):
    bits = log2_of(lax.axis_size("pair"))
    blocks = 1 << bits
    width, modes = packed.shape[2], packed.shape[1] // 4
    n, d = ga.shape
    block_rows, cols = glu_keep.shape[1:]
    kept = in_keep.shape[0]
    small_rows = 4 * modes + 8 + 8
    vmem = pl.BlockSpec(memory_space=pltpu.VMEM)
    hbm = pl.BlockSpec(memory_space=pl.ANY)
    big = pltpu.VMEM((block_rows, d), BF16)
    small = pltpu.VMEM((small_rows, width), F32)
    rows = pltpu.VMEM((2, 8, width), F32)
    copies = 3 * 2 * blocks + 2 * kept + blocks + bits + 12
    shape = jax.ShapeDtypeStruct
    return pl.pallas_call(
        functools.partial(back_body, bits=bits),
        in_specs=[hbm] * 17 + [vmem] * 6,
        out_specs=[hbm] * 4 + [vmem],
        out_shape=[
            shape((n, d), BF16), shape((2, blocks, block_rows, d), BF16),
            shape((2, blocks, block_rows, d), BF16), shape((2, blocks, block_rows, cols), BF16),
            shape((bits + 2, small_rows, width), F32),
        ],
        scratch_shapes=[
            pltpu.VMEM((n, d), F32), pltpu.VMEM(fwd.shape, BF16), pltpu.VMEM(inv.shape, BF16),
            pltpu.VMEM((2, n, width), F32), pltpu.VMEM((2, n, width), BF16),
            pltpu.VMEM((2, 2 * n, width), BF16), pltpu.VMEM((2, 2 * n, width), BF16),
            pltpu.VMEM((n, width), F32), pltpu.VMEM((n, width), BF16),
            pltpu.VMEM((2 * n, width), BF16), pltpu.VMEM((2 * n, width), BF16),
            pltpu.VMEM((2, n, width), F32), pltpu.VMEM((2, n, width), BF16),
            pltpu.VMEM((2, n, width), BF16),
            pltpu.VMEM((2, TOKEN_ROWS, d), BF16), pltpu.VMEM((2, TOKEN_ROWS, d), F32),
            pltpu.VMEM((n // TOKEN_ROWS, TOKEN_ROWS, d), BF16),
        ]
        + power_scratch(modes, MOMENT_INNER, n // MOMENT_INNER)
        + [
            pltpu.VMEM((4, modes, LANES), F32), pltpu.VMEM((2, 4 * modes + 8, width), F32),
            pltpu.VMEM((8, d), F32), rows, rows, rows,
            pltpu.VMEM(in_keep.shape, F32), pltpu.VMEM(in_keep.shape, BF16),
            pltpu.VMEM(in_keep.shape, BF16),
            pltpu.VMEM(in_keep.shape, F32), pltpu.VMEM(in_keep.shape, BF16),
            pltpu.VMEM(in_keep.shape, BF16),
            pltpu.VMEM(glu_keep.shape, F32), pltpu.VMEM(glu_keep.shape, BF16),
            big, big, pltpu.VMEM((block_rows, cols), BF16),
        ]
        + [pltpu.VMEM((kept - 1, block_rows, d), BF16)] * 4
        + [pltpu.VMEM((blocks - 1, block_rows, cols), BF16)] * 2
        + [small, small, pltpu.VMEM((bits + 2, small_rows, width), F32)]
        + [pltpu.SemaphoreType.DMA((48,))]
        + [pltpu.SemaphoreType.DMA((copies,))] * 2,
        compiler_params=params_of(collective_id=4, has_side_effects=True),
        name="back_kernel",
    )(
        ga, mixed, x, xs, ks, fwd, inv, source, resid, in_keep, in_x, in_y, out_keep, out_come, out_z,
        glu_keep, glu_box, skip, gains, gain2, bias2, packed, log_dt,
    )


def GLU_ORDER(bits):
    return list(reversed(range(bits)))


BACK_ROUNDS = {1: ("in", "out"), 3: ("glu", "in"), "norm": ("out", "in", "glu")}


def last_body(
    in_all, out_all, glu_all, small, in_total, out_total, value_total, gate_total, *rest, modes
):
    core = lax.axis_index("core")
    out_total[...] = out_all[...].astype(F32)
    width = in_all.shape[2]
    half = glu_all.shape[2] // 2
    for i in range(2):
        in_total[:, i * width : (i + 1) * width] = in_all[i].astype(F32)
        value_total[:, i * half : (i + 1) * half] = glu_all[i, :, :half].astype(F32)
        gate_total[:, i * half : (i + 1) * half] = glu_all[i, :, half:].astype(F32)

    @pl.when(pl.program_id(0) == 0)
    def _():
        count = small.shape[2]
        top = 4 * modes
        spans = [(i * modes, modes) for i in range(4)] + [(top + i, 1) for i in (0, 8, 9, 10, 11, 12)]
        for ref, (first, rows) in zip(rest, spans):
            for i, which in ((-2, core), (-1, 1 - core)):
                at = pl.ds(pl.multiple_of(which * count, count), count)
                ref[:, at] = small[small.shape[0] + i, first : first + rows, :]


def last_kernel(in_all, out_all, glu_all, small):
    d = in_all.shape[1]
    steps = 8
    modes = (small.shape[1] - 16) // 4
    units, cols, count = in_all.shape[2], glu_all.shape[2], 2 * small.shape[2]
    shape = jax.ShapeDtypeStruct

    def rows(count, width):
        return pl.BlockSpec((count // steps, width), lambda i: (i, 0))

    def pair(width):
        return pl.BlockSpec((2, d // steps, width), lambda i: (0, i, 0))

    def whole(shape):
        return pl.BlockSpec(shape, lambda i: (0,) * len(shape))

    sizes = [(modes, count)] * 4 + [(1, count)] * 6
    return pl.pallas_call(
        functools.partial(last_body, modes=modes),
        grid=(steps,),
        in_specs=[
            pair(units), rows(2 * units, d), pair(cols), whole(small.shape),
        ],
        out_specs=[rows(d, 2 * units), rows(2 * units, d), rows(d, cols), rows(d, cols)]
        + [whole(size) for size in sizes],
        out_shape=[
            shape((d, 2 * units), F32), shape((2 * units, d), F32),
            shape((d, cols), F32), shape((d, cols), F32),
        ]
        + [shape(size, F32) for size in sizes],
        compiler_params=params_of(),
        name="last_kernel",
    )(in_all, out_all, glu_all, small)


SWAP = ((0, 1), (1, 0))


def over_tensor(values):
    return lax.ppermute(values, "tensor", SWAP)


def over_pair(values, flip):
    size = lax.axis_size("pair")
    return lax.ppermute(values, "pair", [(p, p ^ flip) for p in range(size)])


def together(*values):
    return lax.optimization_barrier(values)


def shards(
    inputs, counts, ln1_gain, ln1_bias, log_dt, log_a, freq, c_real, c_imag, skip_gain,
    w_value, w_gate, ln2_gain, ln2_bias, w_in, w_out, cotangent,
):
    _, length, width = inputs.shape
    source = inputs.reshape(length, width)
    gains = jnp.stack([ln1_gain, ln1_bias, ln2_gain, ln2_bias]).astype(F32)
    table = transform_table(length)
    fwd = jnp.asarray(table.astype(ml_dtypes.bfloat16))
    inv = jnp.asarray(np.ascontiguousarray((table.T / length).astype(ml_dtypes.bfloat16)))
    (
        packed, log_dts, skip, grad_low, normed1, mixed, act, spectrum, kernel_spectrum,
        value_proj, gate_sig, residual, normed2, normed2_t,
        value_direct, value_via, gate_direct, gate_via, in_direct, in_via, out_direct, out_via,
    ) = front_kernel(
        source, cotangent.reshape(length, width), counts, gains, log_dt[None], skip_gain[None],
        log_a.T, freq.T, c_real.T, c_imag.T, fwd, inv, w_value, w_gate, w_in, w_out,
    )
    glu_weights = (w_value, value_direct, value_via, w_gate, gate_direct, gate_via)
    units = in_direct.shape[1]
    far_ffn, far_normed2, there_box, there_keep, there_out = ffn_kernel(
        normed2, normed2_t, grad_low, (in_via, in_direct), (out_via, out_direct), units, residual
    )
    normed2, there_out, there_box = together(normed2, there_out, there_box)
    out_come, there_come = over_tensor(there_out), over_pair(there_box, 1)
    own_sums = ffn_kernel(
        normed2, normed2_t, grad_low, (w_in, w_in), (w_out, w_out), units, far_ffn,
        (counts, far_normed2),
    )
    own_sums, out_come, there_come = together(own_sums, out_come, there_come)
    output, grad_normed2, in_box, in_keep, here_out = own_sums
    blocks = lax.axis_size("pair")
    split = (blocks // 2, 2, width // blocks, width)
    here_out, out_come = here_out.reshape(split), out_come.reshape(split)
    (
        grad_residual, grad_act, gain_second_grad, bias_second_grad, there_glu, here_glu,
        in_x, in_y, out_z,
    ) = glu_back_kernel(
        grad_normed2, residual, grad_low, value_proj, gate_sig, act, glu_weights, gains,
        there_keep, there_come, in_box, here_out, out_come,
    )
    halved = (blocks // 2, width // blocks, width)
    by_block = (blocks, width // blocks, -1)
    input_grad, in_all, out_all, glu_all, small = back_kernel(
        grad_act, mixed, normed1, spectrum, kernel_spectrum, fwd, inv, source, grad_residual,
        in_keep.reshape(halved), in_x.reshape(halved), in_y.reshape(halved),
        here_out, out_come, out_z, here_glu.reshape(by_block), there_glu.reshape(by_block),
        skip, gains, gain_second_grad, bias_second_grad, packed, log_dts,
    )
    (
        in_total, out_total, value_total, gate_total,
        log_a_grad, freq_grad, real_grad, imag_grad, *vectors,
    ) = last_kernel(
        in_all.reshape(2, width, -1), out_all.reshape(-1, width), glu_all.reshape(2, width, -1), small
    )
    log_dt_grad, skip_grad, gain1, bias1, gain2, bias2 = (v.reshape(-1) for v in vectors)
    return (
        output.reshape(inputs.shape),
        input_grad.reshape(inputs.shape),
        gain1,
        bias1,
        log_dt_grad,
        log_a_grad.T,
        freq_grad.T,
        real_grad.T,
        imag_grad.T,
        skip_grad,
        value_total,
        gate_total,
        gain2,
        bias2,
        in_total,
        out_total,
    )


def solution(mesh):
    devices = mesh.devices
    cores = jax.sharding.Mesh(
        devices.reshape(devices.shape[0] // 2, 2, devices.shape[1]), ("pair", "core", "tensor")
    )
    batch, every = ("pair", "core"), ("pair", "core", "tensor")
    in_specs = (
        P(every, None, None), P(batch), P(), P(), P("tensor"), P("tensor", None), P("tensor", None),
        P("tensor", None), P("tensor", None), P("tensor"), P(None, "tensor"), P(None, "tensor"),
        P(), P(), P(None, "tensor"), P("tensor", None), P(every, None, None),
    )
    out_specs = (
        P(every, None, None), P(every, None, None), P("tensor"), P("tensor"), P("tensor"),
        P("tensor", None), P("tensor", None), P("tensor", None), P("tensor", None), P("tensor"),
        P(None, "tensor"), P(None, "tensor"), P("tensor"), P("tensor"), P(None, "tensor"),
        P("tensor", None),
    )
    return jax.shard_map(shards, mesh=cores, in_specs=in_specs, out_specs=out_specs, check_vma=False)
```
